32 devices in a mesh: slab: 8 (over y, x, core), pencil: 4 (over z).
Axes of the slice: x: 2, y: 2, z: 4, core: 2. Of those that a mesh axis runs over, the one named last changes fastest.
Arguments:
- surface_eta: float32 [2048, 4096], P('pencil', 'slab'), may hold values from -1.2 to 1.2
- surface_potential: float32 [2048, 4096], P('pencil', 'slab'), may hold values from -1.8 to 1.8
- velocity: float32 [3, 128, 64, 128], P(None, 'slab', 'pencil'), may hold values from -3 to 3
- send_point: int32 [8, 4, 8, 256], P('slab', 'pencil'), may hold values from 0 to 262143
- send_count: int32 [8, 4, 8], P('slab', 'pencil'), may hold values from 1 to 256, as said below
- stencil: int32 [4, 128, 64], P(None, 'slab', 'pencil'), may hold values from 0 to 2047, as said below
- interp_weight: float32 [4, 128, 64], P(None, 'slab', 'pencil'), may hold values from 0.2 to 1
Outputs:
- surface_vertical: float32 [2048, 4096], P('pencil', 'slab')
- velocity_next: float32 [3, 128, 64, 128], P(None, 'slab', 'pencil')
The draws below stay inside these ranges and needn't reach their ends.
Inputs may be any that keep to these rules, and one draw needn't show every extreme that they name: `send_count`: equals 256 toward the first and the last 1 slabs d, at most 64 toward the others. stencil[q, x, y] = r * 256 + j with j < send_count[r, y // 16, x // 16].
All inputs are finite; a program needn't handle non-finite values.
Results may differ from the reference program's by a relative error of at most 0.00015.
Values sent between devices are 32-bit elements; how exact they have to be, the bound alone decides.
A program may use at most 256 MiB of HBM per device.

```python
import math
import jax
import jax.numpy as jnp
from jax import lax

NXW = 4096
NYW = 2048
CX = 16
CY = 16
CZ = 128
STEPS = 2
CAP = 256
Q = 4
NX = 128
NY = 64
TX = 512
TY = 512
ZONE = 1
N_SLAB = 8
N_PENCIL = 4


def count_table(key):
    count_key = jax.random.fold_in(key, 11)
    small_count = jax.random.randint(count_key, (N_SLAB, N_PENCIL, N_SLAB), 1, CAP // 4 + 1)
    target_slab = jnp.arange(N_SLAB, dtype=jnp.int32)
    in_zone = (target_slab < ZONE) | (target_slab >= N_SLAB - ZONE)
    return jnp.where(in_zone[None, None, :], CAP, small_count).astype(jnp.int32)


def draw_send_count(key, part):
    return count_table(key)


def draw_stencil(key, part):
    counts = count_table(key)
    source = jax.random.randint(jax.random.fold_in(key, 21), (Q, NX, NY), 0, N_SLAB)
    slab_of = (jnp.arange(NX, dtype=jnp.int32) // CX)[None, :, None]
    pencil_of = (jnp.arange(NY, dtype=jnp.int32) // CY)[None, None, :]
    slot_limit = counts[source, pencil_of, slab_of]
    slot_index = jax.random.randint(jax.random.fold_in(key, 22), (Q, NX, NY), 0, slot_limit)
    flat_index = source * CAP + slot_index
    flat_index = flat_index.at[0, 0, 0].set(N_SLAB * CAP - 1).at[1, 0, 0].set(0)
    return flat_index.astype(jnp.int32)


def plant(result, own_key, low, high):
    longest = result.shape.index(max(result.shape))
    spots = []
    for shift in (0, 1):
        where = [jax.random.randint(jax.random.fold_in(own_key, axis), (), 0, length) for axis, length in enumerate(result.shape)]
        where[longest] = (where[longest] + shift) % result.shape[longest]
        spots.append(tuple(where))
    return result.at[spots[0]].set(low).at[spots[1]].set(high)


def level_of(own_key, extent, cuts, smallest, largest):
    def one(position, shards_of):
        heights = jax.random.uniform(jax.random.fold_in(jax.random.fold_in(own_key, 6), position), (shards_of,), jnp.float32, smallest / len(cuts), largest / len(cuts))
        return jnp.repeat(jnp.exp(heights), extent[position] // shards_of).reshape((-1,) + (1,) * (len(extent) - position - 1))

    factor_of = one(*cuts[0])
    for cut in cuts[1:]:
        factor_of = factor_of * one(*cut)
    return factor_of


def gaussian(own_key, extent, spread, most, cuts=(), kind=jnp.bfloat16):
    array = spread * jax.random.normal(own_key, extent, jnp.float32)
    if cuts:
        array = array * level_of(own_key, extent, cuts, -0.22, 0.18)
    return jnp.clip(array, -most, most).astype(kind)


def setup_inputs(seed: int = 0) -> dict:
    key_list = jax.random.split(jax.random.key(seed), 8)
    return {
        "surface_eta": gaussian(key_list[0], (NYW, NXW), 0.2, 1.2, ((0, 4), (1, 8)), jnp.float32),
        "surface_potential": gaussian(key_list[1], (NYW, NXW), 0.3, 1.8, ((0, 4), (1, 8)), jnp.float32),
        "velocity": gaussian(key_list[2], (3, NX, NY, CZ), 0.5, 3.0, ((1, 8), (2, 4)), jnp.float32),
        "send_point": plant(jax.random.randint(key_list[3], (N_SLAB, N_PENCIL, N_SLAB, CAP), 0, TX * TY), jax.random.fold_in(key_list[3], 1), 0, (TX * TY) - 1).astype(jnp.int32),
        "send_count": draw_send_count(jax.random.fold_in(key_list[7], 71), 0),
        "stencil": draw_stencil(jax.random.fold_in(key_list[7], 71), 0),
        "interp_weight": jnp.clip(0.2 + 0.8 * jax.random.uniform(key_list[6], (Q, NX, NY), jnp.float32) ** level_of(key_list[6], (Q, NX, NY), ((1, 8), (2, 4)), -0.2, 0.2), 0.2, 1.0),
    }


TIME_STEP = 0.2
VISCOSITY = 0.6
DEPTH_RATE = 3.0

def hartley(values, axis):
    spectrum = jnp.fft.fft(values, axis=axis)
    return (spectrum.real - spectrum.imag).astype(jnp.float32)

def transform(values):
    return hartley(hartley(values, 1), 0)

def wavenumber(index, length):
    folded = jnp.minimum(index, length - index)
    return 2.0 * math.pi / length * folded.astype(jnp.float32)

def ramp_weight(distance, reach_len):
    ratio = jnp.clip(1.0 - distance / reach_len, 0.0, 1.0)
    return ratio * ratio

def blend_weight(pos_x, pos_y, total_x, total_y, reach_x, reach_y):
    along_x = jnp.maximum(ramp_weight(pos_x, reach_x), ramp_weight(total_x - 1.0 - pos_x, reach_x))
    across = jnp.maximum(ramp_weight(pos_y, reach_y), ramp_weight(total_y - 1.0 - pos_y, reach_y))
    return jnp.maximum(along_x[:, None], across[None, :])[:, :, None]

def advance(velocity, padded, relax_weight, target):
    shifted = jnp.pad(padded, ((0, 0), (0, 0), (0, 0), (1, 1)))
    components = []
    for component in range(3):
        current = shifted[component]
        plus_x = current[2:, 1:-1, 1:-1]
        minus_x = current[:-2, 1:-1, 1:-1]
        plus_y = current[1:-1, 2:, 1:-1]
        minus_y = current[1:-1, :-2, 1:-1]
        plus_z = current[1:-1, 1:-1, 2:]
        minus_z = current[1:-1, 1:-1, :-2]
        laplace = plus_x + minus_x + (plus_y + minus_y) + (plus_z + minus_z) - 6.0 * velocity[component]
        advect = velocity[0] * (plus_x - minus_x) + velocity[1] * (plus_y - minus_y) + velocity[2] * (plus_z - minus_z)
        predicted = velocity[component] + TIME_STEP * (VISCOSITY * laplace - 0.5 * advect)
        components.append((1.0 - relax_weight) * predicted + relax_weight * target[component])
    return jnp.stack(components)

def tile_view(field):
    return field.reshape(N_PENCIL, TY, N_SLAB, TX).transpose(2, 0, 1, 3).reshape(N_SLAB, N_PENCIL, TY * TX)

def reference(surface_eta, surface_potential, velocity, send_point, send_count, stencil, interp_weight):
    wave_y = wavenumber(jnp.arange(NYW, dtype=jnp.int32), NYW)[:, None]
    wave_x = wavenumber(jnp.arange(NXW, dtype=jnp.int32), NXW)[None, :]
    magnitude = jnp.sqrt(wave_x * wave_x + wave_y * wave_y)
    norm_scale = 1.0 / (NXW * NYW)
    first_mult = magnitude * norm_scale
    second_mult = magnitude * magnitude * norm_scale
    third_mult = magnitude * magnitude * magnitude * norm_scale
    height = surface_eta
    spectrum = transform(surface_potential)
    slope_one = transform(spectrum * first_mult)
    curve_one = transform(spectrum * second_mult)
    cubic_one = transform(spectrum * third_mult)
    potential_two = -height * slope_one
    spectrum = transform(potential_two)
    slope_two = transform(spectrum * first_mult)
    curve_two = transform(spectrum * second_mult)
    potential_three = -height * slope_two - 0.5 * height * height * curve_one
    spectrum = transform(potential_three)
    slope_three = transform(spectrum * first_mult)
    vertical = slope_one + slope_two + height * curve_one + slope_three + height * curve_two + 0.5 * height * height * cubic_one
    both_tiles = jnp.stack([tile_view(surface_eta), tile_view(vertical)])
    point_lists = send_point.reshape(N_SLAB, N_PENCIL, N_SLAB * CAP)
    sent = jnp.take_along_axis(both_tiles, point_lists[None], axis=3).reshape(2, N_SLAB, N_PENCIL, N_SLAB, CAP)
    live_mask = jnp.arange(CAP, dtype=jnp.int32)[None, None, None, :] < send_count[..., None]
    sent = jnp.where(live_mask[None], sent, 0.0)
    arrived = sent.transpose(0, 3, 2, 1, 4).reshape(2, N_SLAB * N_PENCIL * N_SLAB * CAP)
    slab_of = jnp.arange(NX, dtype=jnp.int32) // CX
    pencil_of = jnp.arange(NY, dtype=jnp.int32) // CY
    base_index = (slab_of[:, None] * N_PENCIL + pencil_of[None, :]) * (N_SLAB * CAP)
    sampled = arrived[:, base_index[None] + stencil]
    shares = interp_weight / lax.optimization_barrier(jnp.sum(interp_weight, axis=0))
    surface_at = lax.optimization_barrier(jnp.sum(sampled * shares[None], axis=1))
    pos_x = jnp.arange(NX, dtype=jnp.float32)
    pos_y = jnp.arange(NY, dtype=jnp.float32)
    relax_weight = blend_weight(pos_x, pos_y, float(NX), float(NY), float(ZONE * CX), float(CY))
    levels = jnp.arange(CZ, dtype=jnp.float32)
    depth_decay = jnp.exp(-DEPTH_RATE * (CZ - 1.0 - levels) / CZ)
    target = jnp.stack([surface_at[0][:, :, None] * depth_decay, jnp.zeros((NX, NY, CZ), jnp.float32), surface_at[1][:, :, None] * depth_decay])
    for substep in range(STEPS):
        padded = jnp.pad(velocity, ((0, 0), (1, 1), (1, 1), (0, 0)))
        velocity = advance(velocity, padded, relax_weight, target)
    return (vertical, velocity)
```

```python
import math

import jax
import jax.numpy as jnp
import numpy as np
from jax import lax
from jax.sharding import PartitionSpec as P

NXW = 4096
NYW = 2048
STEPS = 2
INNER = 256


TIME_STEP = 0.2
VISCOSITY = 0.6
DEPTH_RATE = 3.0

HIGH = lax.Precision.HIGH
BOTH = ("pencil", "slab")


def real_dft(parts):
    size = len(parts)
    if size == 2:
        return [(parts[0] + parts[1], None), (parts[0] - parts[1], None)]
    even = real_dft(parts[0::2])
    odd = real_dft(parts[1::2])
    half = size // 2
    result = [None] * (half + 1)
    for k in range(size // 4 + 1):
        (even_re, even_im), (odd_re, odd_im) = even[k], odd[k]
        if k == 0:
            result[0] = (even_re + odd_re, None)
            result[half] = (even_re - odd_re, None)
        elif 4 * k == size:
            result[k] = (even_re, -odd_re)
        else:
            c, s = math.cos(2.0 * math.pi * k / size), math.sin(2.0 * math.pi * k / size)
            turned_re = c * odd_re + s * odd_im
            turned_im = c * odd_im - s * odd_re
            result[k] = (even_re + turned_re, even_im + turned_im)
            result[half - k] = (even_re - turned_re, turned_im - even_im)
    return result


def outer_dft(parts):
    bins = real_dft(list(parts))
    out = [bins[0][0], bins[-1][0]]
    for re, im in bins[1:-1]:
        out += [re, im]
    return tuple(out)


def outer_dft_transposed(pieces):
    shapes = tuple(jax.ShapeDtypeStruct(piece.shape, piece.dtype) for piece in pieces)
    return jax.linear_transpose(lambda *parts: outer_dft(parts), *shapes)(tuple(pieces))


def tables(length):
    outer = length // INNER
    within = np.arange(INNER)
    blocks = np.zeros((outer // 2, 2 * INNER, 2 * INNER), np.float64)
    order = np.zeros((outer // 2, 2 * INNER), np.int32)
    for b in range(outer // 2):
        for side in range(2):
            if b == 0:
                first = 0 if side == 0 else outer // 2
            else:
                first = b if side == 0 else outer - b
            freq = first + outer * within
            angle = 2.0 * math.pi / length * ((within[:, None] * freq[None, :]) % length)
            cos, sin = np.cos(angle), np.sin(angle)
            columns = slice(side * INNER, (side + 1) * INNER)
            order[b, columns] = freq
            if b == 0:
                blocks[b, columns, columns] = cos + sin
            else:
                sign = 1.0 if side == 0 else -1.0
                blocks[b, :INNER, columns] = cos + sin
                blocks[b, INNER:, columns] = sign * (sin - cos)
    return blocks.astype(np.float32), np.minimum(order, length - order)


def rows_forward(values, blocks, device_count):
    rows, length = values.shape
    pieces = outer_dft([values[:, i : i + INNER] for i in range(0, length, INNER)])
    stacked = jnp.stack(
        [jnp.concatenate(pieces[2 * b : 2 * b + 2], axis=1) for b in range(len(pieces) // 2)]
    )
    spectrum = jnp.einsum("brk,bkn->brn", stacked, blocks, precision=HIGH)
    columns = length // device_count
    spectrum = spectrum.reshape(spectrum.shape[0], rows, 2 * INNER // columns, columns)
    return spectrum.transpose(0, 2, 1, 3).reshape(device_count, rows, columns)


def rows_inverse(values, blocks):
    device_count, rows, columns = values.shape
    grouped = values.reshape(blocks.shape[0], 2 * INNER // columns, rows, columns)
    grouped = grouped.transpose(0, 2, 1, 3).reshape(blocks.shape[0], rows, 2 * INNER)
    stacked = jnp.einsum("brn,bkn->brk", grouped, blocks, precision=HIGH)
    pieces = []
    for b in range(blocks.shape[0]):
        pieces += [stacked[b, :, :INNER], stacked[b, :, INNER:]]
    return jnp.concatenate(outer_dft_transposed(pieces), axis=1)


def columns_forward(values, blocks):
    pieces = outer_dft([values[i : i + INNER] for i in range(0, values.shape[0], INNER)])
    stacked = jnp.concatenate(pieces, axis=0).reshape(
        blocks.shape[0], 2 * INNER, values.shape[1]
    )
    return jnp.einsum("bkn,bkc->bnc", blocks, stacked, precision=HIGH)


def columns_inverse(values, blocks):
    stacked = jnp.einsum("bkn,bnc->bkc", blocks, values, precision=HIGH)
    pieces = []
    for b in range(blocks.shape[0]):
        pieces += [stacked[b, :INNER], stacked[b, INNER:]]
    return jnp.concatenate(outer_dft_transposed(pieces), axis=0)


def exchange(values):
    return lax.all_to_all(values, BOTH, split_axis=0, concat_axis=0, tiled=True)


def ramp_weight(distance, reach_len):
    ratio = jnp.clip(1.0 - distance / reach_len, 0.0, 1.0)
    return ratio * ratio


def blend_weight(pos_x, pos_y, total_x, total_y, reach_x, reach_y):
    along_x = jnp.maximum(ramp_weight(pos_x, reach_x), ramp_weight(total_x - 1.0 - pos_x, reach_x))
    across = jnp.maximum(ramp_weight(pos_y, reach_y), ramp_weight(total_y - 1.0 - pos_y, reach_y))
    return jnp.maximum(along_x[:, None], across[None, :])[:, :, None]


def neighbours(shard, axis, dim):
    size, length = lax.axis_size(axis), shard.shape[dim]
    up = [(i, i + 1) for i in range(size - 1)]
    down = [(i + 1, i) for i in range(size - 1)]
    before = lax.ppermute(lax.slice_in_dim(shard, length - 1, length, axis=dim), axis, up)
    after = lax.ppermute(lax.slice_in_dim(shard, 0, 1, axis=dim), axis, down)
    minus = jnp.concatenate([before, lax.slice_in_dim(shard, 0, length - 1, axis=dim)], axis=dim)
    plus = jnp.concatenate([lax.slice_in_dim(shard, 1, length, axis=dim), after], axis=dim)
    return minus, plus


def predict(velocity):
    minus_x, plus_x = neighbours(velocity, "slab", 1)
    minus_y, plus_y = neighbours(velocity, "pencil", 2)
    padded = jnp.pad(velocity, ((0, 0), (0, 0), (0, 0), (1, 1)))
    minus_z, plus_z = padded[..., :-2], padded[..., 2:]
    laplace = plus_x + minus_x + (plus_y + minus_y) + (plus_z + minus_z) - 6.0 * velocity
    advect = (
        velocity[0] * (plus_x - minus_x)
        + velocity[1] * (plus_y - minus_y)
        + velocity[2] * (plus_z - minus_z)
    )
    return velocity + TIME_STEP * (VISCOSITY * laplace - 0.5 * advect)


def on_device(
    surface_eta, surface_potential, velocity, send_point, send_count, stencil, interp_weight
):
    slab_count = lax.axis_size("slab")
    pencil_count = lax.axis_size("pencil")
    device_count = slab_count * pencil_count
    slab_index = lax.axis_index("slab")
    pencil_index = lax.axis_index("pencil")
    tile_rows, tile_cols = surface_eta.shape
    rows = NYW // device_count
    columns = NXW // device_count
    row_table, row_order = tables(NXW)
    column_table, column_order = tables(NYW)
    row_blocks, column_blocks = jnp.asarray(row_table), jnp.asarray(column_table)

    both = jnp.stack([surface_potential, surface_eta]).reshape(2, slab_count, rows, tile_cols)
    both = lax.all_to_all(both, "slab", split_axis=1, concat_axis=1, tiled=True)
    both = both.transpose(0, 2, 1, 3).reshape(2, rows, NXW)
    potential, eta = both[0], both[1]

    own = pencil_index * slab_count + slab_index
    wave_x = 2.0 * math.pi / NXW * jnp.asarray(row_order.reshape(-1)).astype(jnp.float32)
    wave_x = lax.dynamic_slice(wave_x, (own * columns,), (columns,))
    wave_y = 2.0 * math.pi / NYW * jnp.asarray(column_order).astype(jnp.float32)[:, :, None]
    magnitude = jnp.sqrt(wave_x * wave_x + wave_y * wave_y)
    first_mult = magnitude * (1.0 / (NXW * NYW))
    second_mult = magnitude * first_mult
    third_mult = magnitude * second_mult

    def forward(field):
        arrived = exchange(rows_forward(field, row_blocks, device_count))
        return columns_forward(arrived.reshape(NYW, columns), column_blocks)

    def inverse(spectrum):
        field = columns_inverse(spectrum, column_blocks)
        return rows_inverse(exchange(field.reshape(device_count, rows, columns)), row_blocks)

    spectrum = forward(potential)
    slope_one = inverse(spectrum * first_mult)
    curve_one = inverse(spectrum * second_mult)
    cubic_one = inverse(spectrum * third_mult)
    spectrum = forward(-eta * slope_one)
    slope_two = inverse(spectrum * first_mult)
    curve_two = inverse(spectrum * second_mult)
    spectrum = forward(-eta * slope_two - 0.5 * eta * eta * curve_one)
    slope_three = inverse(spectrum * first_mult)
    vertical = (
        slope_one
        + slope_two
        + eta * curve_one
        + slope_three
        + eta * curve_two
        + 0.5 * eta * eta * cubic_one
    )
    vertical = vertical.reshape(rows, slab_count, tile_cols).transpose(1, 0, 2)
    vertical = lax.all_to_all(vertical, "slab", split_axis=0, concat_axis=0, tiled=True)
    vertical = vertical.reshape(tile_rows, tile_cols)

    points = send_point[0, 0]
    capacity = points.shape[1]
    counts = send_count[0, 0]
    flat_points = points.reshape(-1)
    live = (jnp.arange(capacity, dtype=jnp.int32)[None, :] < counts[:, None]).reshape(-1)
    row_pick = (
        (flat_points // tile_cols)[:, None] == jnp.arange(tile_rows, dtype=jnp.int32)[None, :]
    ).astype(jnp.float32)
    column_pick = (flat_points % tile_cols)[:, None] == jnp.arange(tile_cols, dtype=jnp.int32)[
        None, :
    ]
    column_pick = column_pick & live[:, None]

    def pick(tile):
        picked_rows = jnp.dot(row_pick, tile, precision=HIGH)
        return jnp.sum(jnp.where(column_pick, picked_rows, 0.0), axis=1)

    picked = jnp.stack([pick(surface_eta), pick(vertical)]).reshape(2, slab_count, capacity)
    arrived = lax.all_to_all(picked, "slab", split_axis=1, concat_axis=1, tiled=True).reshape(
        2, slab_count * capacity
    )
    block_x, block_y, depth_cells = velocity.shape[1:]
    shares = interp_weight / jnp.sum(interp_weight, axis=0)
    slots = jnp.arange(slab_count * capacity, dtype=jnp.int32)[:, None]
    mixing = 0.0
    for q in range(stencil.shape[0]):
        mixing = mixing + jnp.where(
            slots == stencil[q].reshape(1, -1), shares[q].reshape(1, -1), 0.0
        )
    surface_at = jnp.dot(arrived, mixing, precision=lax.Precision.HIGHEST)
    surface_at = surface_at.reshape(2, block_x, block_y)

    zone_slabs = max(1, slab_count // 16)
    pos_x = (slab_index * block_x + jnp.arange(block_x, dtype=jnp.int32)).astype(jnp.float32)
    pos_y = (pencil_index * block_y + jnp.arange(block_y, dtype=jnp.int32)).astype(jnp.float32)
    relax_weight = blend_weight(
        pos_x,
        pos_y,
        float(block_x * slab_count),
        float(block_y * pencil_count),
        float(zone_slabs * block_x),
        float(block_y),
    )
    levels = jnp.arange(depth_cells, dtype=jnp.float32)
    depth_decay = jnp.exp(-DEPTH_RATE * (depth_cells - 1.0 - levels) / depth_cells)
    target = jnp.stack(
        [
            surface_at[0][:, :, None] * depth_decay,
            jnp.zeros((block_x, block_y, depth_cells), jnp.float32),
            surface_at[1][:, :, None] * depth_decay,
        ]
    )
    for substep in range(STEPS):
        velocity = (1.0 - relax_weight) * predict(velocity) + relax_weight * target
    return (vertical, velocity)


def solution(mesh):
    in_specs = (
        P("pencil", "slab"),
        P("pencil", "slab"),
        P(None, "slab", "pencil", None),
        P("slab", "pencil", None, None),
        P("slab", "pencil", None),
        P(None, "slab", "pencil"),
        P(None, "slab", "pencil"),
    )
    out_specs = (P("pencil", "slab"), P(None, "slab", "pencil", None))
    return jax.shard_map(
        on_device, mesh=mesh, in_specs=in_specs, out_specs=out_specs, check_vma=False
    )
```

```python
import math

import jax
import jax.numpy as jnp
import numpy as np
from jax import lax
from jax.experimental import pallas as pl
from jax.experimental.pallas import tpu as pltpu
from jax.sharding import PartitionSpec as P

NXW = 4096
NYW = 2048
STEPS = 2
INNER = 256


TIME_STEP = 0.2
VISCOSITY = 0.6
DEPTH_RATE = 3.0

HIGH = lax.Precision.HIGH
BOTH = ("pencil", "slab")


def real_dft(parts):
    size = len(parts)
    if size == 2:
        return [(parts[0] + parts[1], None), (parts[0] - parts[1], None)]
    even = real_dft(parts[0::2])
    odd = real_dft(parts[1::2])
    half = size // 2
    result = [None] * (half + 1)
    for k in range(size // 4 + 1):
        (even_re, even_im), (odd_re, odd_im) = even[k], odd[k]
        if k == 0:
            result[0] = (even_re + odd_re, None)
            result[half] = (even_re - odd_re, None)
        elif 4 * k == size:
            result[k] = (even_re, -odd_re)
        else:
            c, s = math.cos(2.0 * math.pi * k / size), math.sin(2.0 * math.pi * k / size)
            turned_re = c * odd_re + s * odd_im
            turned_im = c * odd_im - s * odd_re
            result[k] = (even_re + turned_re, even_im + turned_im)
            result[half - k] = (even_re - turned_re, turned_im - even_im)
    return result


def outer_dft(parts):
    bins = real_dft(list(parts))
    out = [bins[0][0], bins[-1][0]]
    for re, im in bins[1:-1]:
        out += [re, im]
    return tuple(out)


def real_dft_transposed(bins):
    half = len(bins) - 1
    size = 2 * half
    if size == 2:
        return [bins[0][0] + bins[1][0], bins[0][0] - bins[1][0]]
    even, odd = [None] * (half // 2 + 1), [None] * (half // 2 + 1)
    for k in range(size // 4 + 1):
        re, im = bins[k]
        if k == 0:
            even[0] = (re + bins[half][0], None)
            odd[0] = (re - bins[half][0], None)
        elif 4 * k == size:
            even[k] = (re, None)
            odd[k] = (-im, None)
        else:
            other_re, other_im = bins[half - k]
            c, s = math.cos(2.0 * math.pi * k / size), math.sin(2.0 * math.pi * k / size)
            turned_re, turned_im = re - other_re, im + other_im
            even[k] = (re + other_re, im - other_im)
            odd[k] = (c * turned_re - s * turned_im, s * turned_re + c * turned_im)
    result = [None] * size
    result[0::2] = real_dft_transposed(even)
    result[1::2] = real_dft_transposed(odd)
    return result


def outer_dft_transposed(pieces):
    half = len(pieces) // 2
    bins = [(pieces[0], None)]
    bins += [(pieces[2 * k], pieces[2 * k + 1]) for k in range(1, half)]
    return real_dft_transposed(bins + [(pieces[1], None)])


def tables(length):
    outer = length // INNER
    within = np.arange(INNER)
    blocks = np.zeros((outer // 2, 2 * INNER, 2 * INNER), np.float64)
    order = np.zeros((outer // 2, 2 * INNER), np.int32)
    for b in range(outer // 2):
        for side in range(2):
            if b == 0:
                first = 0 if side == 0 else outer // 2
            else:
                first = b if side == 0 else outer - b
            freq = first + outer * within
            angle = 2.0 * math.pi / length * ((within[:, None] * freq[None, :]) % length)
            cos, sin = np.cos(angle), np.sin(angle)
            columns = slice(side * INNER, (side + 1) * INNER)
            order[b, columns] = freq
            if b == 0:
                blocks[b, columns, columns] = cos + sin
            else:
                sign = 1.0 if side == 0 else -1.0
                blocks[b, :INNER, columns] = cos + sin
                blocks[b, INNER:, columns] = sign * (sin - cos)
    return blocks.astype(np.float32), np.minimum(order, length - order)


def rows_forward(values, blocks, device_count):
    rows, length = values.shape
    pieces = outer_dft([values[:, i : i + INNER] for i in range(0, length, INNER)])
    stacked = jnp.stack(
        [jnp.concatenate(pieces[2 * b : 2 * b + 2], axis=1) for b in range(len(pieces) // 2)]
    )
    spectrum = jnp.einsum("brk,bkn->brn", stacked, blocks, precision=HIGH)
    columns = length // device_count
    spectrum = spectrum.reshape(spectrum.shape[0], rows, 2 * INNER // columns, columns)
    return spectrum.transpose(0, 2, 1, 3).reshape(device_count, rows, columns)


def rows_inverse(values, blocks):
    device_count, rows, columns = values.shape
    grouped = values.reshape(blocks.shape[0], 2 * INNER // columns, rows, columns)
    grouped = grouped.transpose(0, 2, 1, 3).reshape(blocks.shape[0], rows, 2 * INNER)
    stacked = jnp.einsum("brn,bkn->brk", grouped, blocks, precision=HIGH)
    pieces = []
    for b in range(blocks.shape[0]):
        pieces += [stacked[b, :, :INNER], stacked[b, :, INNER:]]
    return jnp.concatenate(outer_dft_transposed(pieces), axis=1)


def columns_forward(values, blocks):
    pieces = outer_dft([values[i : i + INNER] for i in range(0, values.shape[0], INNER)])
    stacked = jnp.concatenate(pieces, axis=0).reshape(
        blocks.shape[0], 2 * INNER, values.shape[1]
    )
    return jnp.einsum("bkn,bkc->bnc", blocks, stacked, precision=HIGH)


def columns_inverse(values, blocks):
    stacked = jnp.einsum("bkn,bnc->bkc", blocks, values, precision=HIGH)
    pieces = []
    for b in range(blocks.shape[0]):
        pieces += [stacked[b, :INNER], stacked[b, INNER:]]
    return jnp.concatenate(outer_dft_transposed(pieces), axis=0)


def exchange(values):
    return lax.all_to_all(values, BOTH, split_axis=0, concat_axis=0, tiled=True)


def split(values):
    high = values.astype(jnp.bfloat16)
    return high, (values - high.astype(jnp.float32)).astype(jnp.bfloat16)


def row_product(values, high_ref, low_ref, block, contract):
    rows = values.shape[0]
    high, low = split(values)
    dims = (((1,), (contract,)), ((), ()))
    main = lax.dot_general(
        jnp.concatenate([high, low], axis=0),
        high_ref[block],
        dims,
        preferred_element_type=jnp.float32,
    )
    rest = lax.dot_general(high, low_ref[block], dims, preferred_element_type=jnp.float32)
    return main[:rows] + (main[rows:] + rest)


def column_product(values, high_ref, low_ref, block):
    columns = values.shape[1]
    high, low = split(values)
    main = jnp.dot(
        high_ref[block],
        jnp.concatenate([high, low], axis=1),
        preferred_element_type=jnp.float32,
    )
    rest = jnp.dot(low_ref[block], high, preferred_element_type=jnp.float32)
    return main[:, :columns] + (main[:, columns:] + rest)


def surface_kernel(
    slab_count,
    pencil_count,
    potential_ref,
    eta_ref,
    magnitude_ref,
    row_high_in,
    row_low_in,
    col_high_in,
    col_low_in,
    colt_high_in,
    colt_low_in,
    out_ref,
    row_high,
    row_low,
    col_high,
    col_low,
    colt_high,
    colt_low,
    potential,
    eta,
    back,
    total,
    curve,
    stage_rows,
    stage_cols,
    spectrum,
    sent,
    held,
    table_sem,
    send_sem,
    recv_sem,
):
    slab = lax.axis_index("slab")
    pencil = lax.axis_index("pencil")
    device_count = slab_count * pencil_count
    own = pencil * slab_count + slab
    rows = sent.shape[2]
    columns = sent.shape[3]
    per_block = 2 * INNER // columns
    row_blocks = row_high.shape[0]
    col_blocks = col_high.shape[0]
    chunk = potential.shape[2]
    per_part = INNER // rows
    row_parts = 2 * row_blocks
    col_parts = 2 * col_blocks
    step = 8

    pairs = (
        (row_high_in, row_high),
        (row_low_in, row_low),
        (colt_high_in, colt_high),
        (colt_low_in, colt_low),
        (col_high_in, col_high),
        (col_low_in, col_low),
    )
    tables_in = [
        pltpu.make_async_copy(source, target, table_sem.at[i])
        for i, (source, target) in enumerate(pairs)
    ]
    for copy in tables_in:
        copy.start()

    def partner(i):
        return lax.rem(pencil + lax.rem(i, pencil_count), pencil_count), lax.rem(
            slab + i // pencil_count, slab_count
        )

    barrier = pltpu.get_barrier_semaphore()

    @pl.loop(1, device_count)
    def _(i):
        to_pencil, to_slab = partner(i)
        pl.semaphore_signal(
            barrier,
            inc=1,
            device_id={"slab": to_slab, "pencil": to_pencil},
            device_id_type=pl.DeviceIdType.MESH,
        )

    pl.semaphore_wait(barrier, device_count - 1)

    def remote(source, target, index, to_slab, to_pencil):
        return pltpu.make_async_remote_copy(
            src_ref=source,
            dst_ref=target,
            send_sem=send_sem.at[index],
            recv_sem=recv_sem.at[index],
            device_id={"slab": to_slab, "pencil": to_pencil},
            device_id_type=pl.DeviceIdType.MESH,
        )

    def send(n):
        @pl.loop(1, device_count)
        def _(i):
            to_pencil, to_slab = partner(i)
            to = to_pencil * slab_count + to_slab
            remote(sent.at[n, to], held.at[n, own], n, to_slab, to_pencil).start()

        held[n, own] = sent[n, own]

    def all_of(n):
        others = pl.ds(0, device_count - 1)
        return remote(sent.at[n, others], held.at[n, others], n, slab, pencil)

    def send_slab(source_of, target, n):
        for i in range(1, slab_count):
            to = lax.rem(slab + i, slab_count)
            remote(source_of(to), target.at[slab], n, to, pencil).start()

    def all_of_slab(target, n):
        others = target.at[pl.ds(0, slab_count - 1)]
        return remote(others, others, n, slab, pencil)

    fields = sent.shape[0]

    def tile_rows(ref):
        return lambda to: ref.at[pl.ds(pl.multiple_of(to * rows, rows), rows)]

    own_rows = pl.ds(pl.multiple_of(slab * rows, rows), rows)
    send_slab(tile_rows(potential_ref), potential, fields)
    send_slab(tile_rows(eta_ref), eta, fields + 1)
    potential[slab] = potential_ref[own_rows]
    eta[slab] = eta_ref[own_rows]

    def part_of(ref, part, at):
        start = part * INNER % chunk
        return ref.at[part * INNER // chunk, at, pl.ds(start, INNER)]

    def piece_of(piece, at):
        return stage_rows.at[piece // 2, at, pl.ds(piece % 2 * INNER, INNER)]

    def over_rows(body):
        @pl.loop(0, rows // step)
        def _(i):
            body(pl.ds(pl.multiple_of(i * step, step), step))

    def begin_rows(parts, at):
        for piece, value in enumerate(outer_dft(parts)):
            piece_of(piece, at)[...] = value

    def finish_rows(n):
        @pl.loop(0, row_blocks)
        def _(b):
            result = row_product(stage_rows[b], row_high, row_low, b, 0)
            for i in range(per_block):
                sent[n, b * per_block + i] = result[:, i * columns : (i + 1) * columns]

        send(n)

    def inverse_rows(n, use):
        all_of(n).wait_recv()

        @pl.loop(0, row_blocks)
        def _(b):
            values = jnp.concatenate(
                [held[n, b * per_block + i] for i in range(per_block)], axis=1
            )
            stage_rows[b] = row_product(values, row_high, row_low, b, 1)

        def body(at):
            use(at, outer_dft_transposed([piece_of(p, at)[...] for p in range(row_parts)]))

        over_rows(body)

    def over_columns(body):
        @pl.loop(0, 2 * per_part)
        def _(i):
            body(i // 2, pl.multiple_of(lax.rem(i, 2) * (rows // 2), rows // 2))

    def forward_columns(n):
        all_of(n).wait_recv()

        def body(q, start):
            parts = [held[n, p * per_part + q, pl.ds(start, rows // 2)] for p in range(col_parts)]
            for piece, value in enumerate(outer_dft(parts)):
                at = pl.multiple_of(piece % 2 * INNER + q * rows + start, rows // 2)
                stage_cols[piece // 2, pl.ds(at, rows // 2)] = value

        over_columns(body)

        @pl.loop(0, col_blocks)
        def _(b):
            spectrum[b] = column_product(stage_cols[b], colt_high, colt_low, b)

    def inverse_columns(n):
        @pl.loop(0, col_blocks)
        def _(b):
            values = spectrum[b] * magnitude_ref[b]
            spectrum[b] = values
            stage_cols[b] = column_product(values, col_high, col_low, b)

        def body(q, start):
            pieces = []
            for piece in range(col_parts):
                at = pl.multiple_of(piece % 2 * INNER + q * rows + start, rows // 2)
                pieces.append(stage_cols[piece // 2, pl.ds(at, rows // 2)])
            for p, value in enumerate(outer_dft_transposed(pieces)):
                sent[n, p * per_part + q, pl.ds(start, rows // 2)] = value * (1.0 / (NXW * NYW))

        over_columns(body)
        send(n)

    all_of_slab(potential, fields).wait_recv()
    over_rows(
        lambda at: begin_rows([part_of(potential, p, at)[...] for p in range(row_parts)], at)
    )
    tables_in[0].wait()
    tables_in[1].wait()
    finish_rows(0)
    for copy in tables_in[2:]:
        copy.wait()

    forward_columns(0)
    inverse_columns(1)
    inverse_columns(2)
    all_of_slab(eta, fields + 1).wait_recv()

    def use_slope_one(at, parts):
        for p, value in enumerate(parts):
            part_of(total, p, at)[...] = value
        begin_rows([-part_of(eta, p, at)[...] * value for p, value in enumerate(parts)], at)

    def use_curve_one(at, parts):
        for p, value in enumerate(parts):
            height = part_of(eta, p, at)[...]
            term = height * value
            part_of(total, p, at)[...] += term
            part_of(curve, p, at)[...] = 0.5 * height * term

    def use_cubic_one(at, parts):
        for p, value in enumerate(parts):
            height = part_of(eta, p, at)[...]
            part_of(total, p, at)[...] += 0.5 * height * height * value

    def use_slope_two(at, parts):
        following = []
        for p, value in enumerate(parts):
            part_of(total, p, at)[...] += value
            following.append(-part_of(eta, p, at)[...] * value - part_of(curve, p, at)[...])
        begin_rows(following, at)

    def use_curve_two(at, parts):
        for p, value in enumerate(parts):
            part_of(total, p, at)[...] += part_of(eta, p, at)[...] * value

    def use_slope_three(at, parts):
        for p, value in enumerate(parts):
            part_of(total, p, at)[...] += value

    inverse_columns(3)
    inverse_rows(1, use_slope_one)
    finish_rows(4)
    inverse_rows(2, use_curve_one)
    inverse_rows(3, use_cubic_one)
    forward_columns(4)
    inverse_columns(5)
    inverse_columns(6)
    inverse_rows(5, use_slope_two)
    finish_rows(7)
    inverse_rows(6, use_curve_two)
    forward_columns(7)
    inverse_columns(8)
    inverse_rows(8, use_slope_three)

    send_slab(lambda to: total.at[to], back, fields + 2)
    out_ref[own_rows] = total[slab]
    all_of_slab(back, fields + 2).wait_recv()
    for i in range(1, slab_count):
        source = lax.rem(slab + i, slab_count)
        out_ref[pl.ds(pl.multiple_of(source * rows, rows), rows)] = back[source]
    for n in range(fields):
        all_of(n).wait_send()
    all_of_slab(potential, fields).wait_send()
    all_of_slab(eta, fields + 1).wait_send()
    all_of_slab(back, fields + 2).wait_send()


def two_terms(table):
    high = table.astype(jnp.bfloat16)
    low = (table - high.astype(np.float32)).astype(jnp.bfloat16)
    return jnp.asarray(high), jnp.asarray(low)


def surface_chain(potential, eta, magnitude, slab_count, pencil_count):
    tile_rows, tile_cols = eta.shape
    device_count = slab_count * pencil_count
    rows, columns = NYW // device_count, NXW // device_count
    row_table, _ = tables(NXW)
    col_table, _ = tables(NYW)
    constants = [
        *two_terms(row_table),
        *two_terms(col_table),
        *two_terms(np.ascontiguousarray(col_table.transpose(0, 2, 1))),
    ]
    fields = 9
    strip = pltpu.VMEM((slab_count, rows, tile_cols), jnp.float32)
    vmem = pl.BlockSpec(memory_space=pltpu.VMEM)
    return pl.pallas_call(
        lambda *refs: surface_kernel(slab_count, pencil_count, *refs),
        out_shape=jax.ShapeDtypeStruct((tile_rows, tile_cols), jnp.float32),
        in_specs=[vmem] * 3 + [pl.BlockSpec(memory_space=pl.ANY)] * 6,
        out_specs=vmem,
        scratch_shapes=[
            *(pltpu.VMEM(table.shape, jnp.bfloat16) for table in constants),
            *([strip] * 5),
            pltpu.VMEM(row_table.shape[:1] + (rows, 2 * INNER), jnp.float32),
            pltpu.VMEM(magnitude.shape, jnp.float32),
            pltpu.VMEM(magnitude.shape, jnp.float32),
            pltpu.VMEM((fields, device_count, rows, columns), jnp.float32),
            pltpu.VMEM((fields, device_count, rows, columns), jnp.float32),
            pltpu.SemaphoreType.DMA((6,)),
            pltpu.SemaphoreType.DMA((fields + 3,)),
            pltpu.SemaphoreType.DMA((fields + 3,)),
        ],
        compiler_params=pltpu.CompilerParams(
            collective_id=0, has_side_effects=True, vmem_limit_bytes=56 * 1024 * 1024
        ),
    )(potential, eta, magnitude, *constants)


def surface_plain(potential, eta, magnitude, row_table, column_table, slab_count):
    tile_rows, tile_cols = eta.shape
    columns = magnitude.shape[-1]
    device_count = NXW // columns
    rows = NYW // device_count
    row_blocks, column_blocks = jnp.asarray(row_table), jnp.asarray(column_table)
    both = jnp.stack([potential, eta]).reshape(2, slab_count, rows, tile_cols)
    both = lax.all_to_all(both, "slab", split_axis=1, concat_axis=1, tiled=True)
    both = both.transpose(0, 2, 1, 3).reshape(2, rows, NXW)
    potential, eta = both[0], both[1]
    first_mult = magnitude * (1.0 / (NXW * NYW))
    second_mult = magnitude * first_mult
    third_mult = magnitude * second_mult

    def forward(field):
        arrived = exchange(rows_forward(field, row_blocks, device_count))
        return columns_forward(arrived.reshape(NYW, columns), column_blocks)

    def inverse(spectrum):
        field = columns_inverse(spectrum, column_blocks)
        return rows_inverse(exchange(field.reshape(device_count, rows, columns)), row_blocks)

    spectrum = forward(potential)
    slope_one = inverse(spectrum * first_mult)
    curve_one = inverse(spectrum * second_mult)
    cubic_one = inverse(spectrum * third_mult)
    spectrum = forward(-eta * slope_one)
    slope_two = inverse(spectrum * first_mult)
    curve_two = inverse(spectrum * second_mult)
    spectrum = forward(-eta * slope_two - 0.5 * eta * eta * curve_one)
    slope_three = inverse(spectrum * first_mult)
    vertical = (
        slope_one
        + slope_two
        + eta * curve_one
        + slope_three
        + eta * curve_two
        + 0.5 * eta * eta * cubic_one
    )
    vertical = vertical.reshape(rows, slab_count, tile_cols).transpose(1, 0, 2)
    vertical = lax.all_to_all(vertical, "slab", split_axis=0, concat_axis=0, tiled=True)
    vertical = vertical.reshape(tile_rows, tile_cols)

    return vertical


def ramp_weight(distance, reach_len):
    ratio = jnp.clip(1.0 - distance / reach_len, 0.0, 1.0)
    return ratio * ratio


def blend_weight(pos_x, pos_y, total_x, total_y, reach_x, reach_y):
    along_x = jnp.maximum(ramp_weight(pos_x, reach_x), ramp_weight(total_x - 1.0 - pos_x, reach_x))
    across = jnp.maximum(ramp_weight(pos_y, reach_y), ramp_weight(total_y - 1.0 - pos_y, reach_y))
    return jnp.maximum(along_x[:, None], across[None, :])[:, :, None]


def neighbours(shard, axis, dim):
    size, length = lax.axis_size(axis), shard.shape[dim]
    up = [(i, i + 1) for i in range(size - 1)]
    down = [(i + 1, i) for i in range(size - 1)]
    before = lax.ppermute(lax.slice_in_dim(shard, length - 1, length, axis=dim), axis, up)
    after = lax.ppermute(lax.slice_in_dim(shard, 0, 1, axis=dim), axis, down)
    minus = jnp.concatenate([before, lax.slice_in_dim(shard, 0, length - 1, axis=dim)], axis=dim)
    plus = jnp.concatenate([lax.slice_in_dim(shard, 1, length, axis=dim), after], axis=dim)
    return minus, plus


def predict(velocity):
    minus_x, plus_x = neighbours(velocity, "slab", 1)
    minus_y, plus_y = neighbours(velocity, "pencil", 2)
    padded = jnp.pad(velocity, ((0, 0), (0, 0), (0, 0), (1, 1)))
    minus_z, plus_z = padded[..., :-2], padded[..., 2:]
    laplace = plus_x + minus_x + (plus_y + minus_y) + (plus_z + minus_z) - 6.0 * velocity
    advect = (
        velocity[0] * (plus_x - minus_x)
        + velocity[1] * (plus_y - minus_y)
        + velocity[2] * (plus_z - minus_z)
    )
    return velocity + TIME_STEP * (VISCOSITY * laplace - 0.5 * advect)


def on_device(
    surface_eta, surface_potential, velocity, send_point, send_count, stencil, interp_weight
):
    slab_count = lax.axis_size("slab")
    pencil_count = lax.axis_size("pencil")
    device_count = slab_count * pencil_count
    slab_index = lax.axis_index("slab")
    pencil_index = lax.axis_index("pencil")
    tile_rows, tile_cols = surface_eta.shape
    rows = NYW // device_count
    columns = NXW // device_count
    own = pencil_index * slab_count + slab_index
    row_table, row_order = tables(NXW)
    column_table, column_order = tables(NYW)
    wave_x = 2.0 * math.pi / NXW * jnp.asarray(row_order.reshape(-1)).astype(jnp.float32)
    wave_x = lax.dynamic_slice(wave_x, (own * columns,), (columns,))
    wave_y = 2.0 * math.pi / NYW * jnp.asarray(column_order).astype(jnp.float32)[:, :, None]
    magnitude = jnp.sqrt(wave_x * wave_x + wave_y * wave_y)
    if columns % 128 == 0 and rows % 16 == 0 and INNER % rows == 0:
        vertical = surface_chain(
            surface_potential, surface_eta, magnitude, slab_count, pencil_count
        )
    else:
        vertical = surface_plain(
            surface_potential, surface_eta, magnitude, row_table, column_table, slab_count
        )

    points = send_point[0, 0]
    capacity = points.shape[1]
    counts = send_count[0, 0]
    flat_points = points.reshape(-1)
    live = (jnp.arange(capacity, dtype=jnp.int32)[None, :] < counts[:, None]).reshape(-1)
    row_pick = (
        (flat_points // tile_cols)[:, None] == jnp.arange(tile_rows, dtype=jnp.int32)[None, :]
    ).astype(jnp.float32)
    column_pick = (flat_points % tile_cols)[:, None] == jnp.arange(tile_cols, dtype=jnp.int32)[
        None, :
    ]
    column_pick = column_pick & live[:, None]

    def pick(tile):
        picked_rows = jnp.dot(row_pick, tile, precision=HIGH)
        return jnp.sum(jnp.where(column_pick, picked_rows, 0.0), axis=1)

    picked = jnp.stack([pick(surface_eta), pick(vertical)]).reshape(2, slab_count, capacity)
    arrived = lax.all_to_all(picked, "slab", split_axis=1, concat_axis=1, tiled=True).reshape(
        2, slab_count * capacity
    )
    block_x, block_y, depth_cells = velocity.shape[1:]
    shares = interp_weight / jnp.sum(interp_weight, axis=0)
    slots = jnp.arange(slab_count * capacity, dtype=jnp.int32)[:, None]
    mixing = 0.0
    for q in range(stencil.shape[0]):
        mixing = mixing + jnp.where(
            slots == stencil[q].reshape(1, -1), shares[q].reshape(1, -1), 0.0
        )
    surface_at = jnp.dot(arrived, mixing, precision=lax.Precision.HIGHEST)
    surface_at = surface_at.reshape(2, block_x, block_y)

    zone_slabs = max(1, slab_count // 16)
    pos_x = (slab_index * block_x + jnp.arange(block_x, dtype=jnp.int32)).astype(jnp.float32)
    pos_y = (pencil_index * block_y + jnp.arange(block_y, dtype=jnp.int32)).astype(jnp.float32)
    relax_weight = blend_weight(
        pos_x,
        pos_y,
        float(block_x * slab_count),
        float(block_y * pencil_count),
        float(zone_slabs * block_x),
        float(block_y),
    )
    levels = jnp.arange(depth_cells, dtype=jnp.float32)
    depth_decay = jnp.exp(-DEPTH_RATE * (depth_cells - 1.0 - levels) / depth_cells)
    target = jnp.stack(
        [
            surface_at[0][:, :, None] * depth_decay,
            jnp.zeros((block_x, block_y, depth_cells), jnp.float32),
            surface_at[1][:, :, None] * depth_decay,
        ]
    )
    for substep in range(STEPS):
        velocity = (1.0 - relax_weight) * predict(velocity) + relax_weight * target
    return (vertical, velocity)


def solution(mesh):
    in_specs = (
        P("pencil", "slab"),
        P("pencil", "slab"),
        P(None, "slab", "pencil", None),
        P("slab", "pencil", None, None),
        P("slab", "pencil", None),
        P(None, "slab", "pencil"),
        P(None, "slab", "pencil"),
    )
    out_specs = (P("pencil", "slab"), P(None, "slab", "pencil", None))
    return jax.shard_map(
        on_device, mesh=mesh, in_specs=in_specs, out_specs=out_specs, check_vma=False
    )
```

```python
import math

import jax
import jax.numpy as jnp
import numpy as np
from jax import lax
from jax.experimental import pallas as pl
from jax.experimental.pallas import tpu as pltpu
from jax.sharding import PartitionSpec as P

NXW = 4096
NYW = 2048
STEPS = 2
INNER = 256


TIME_STEP = 0.2
VISCOSITY = 0.6
DEPTH_RATE = 3.0

HIGH = lax.Precision.HIGH
BOTH = ("pencil", "slab")


def real_dft(parts):
    size = len(parts)
    if size == 2:
        return [(parts[0] + parts[1], None), (parts[0] - parts[1], None)]
    even = real_dft(parts[0::2])
    odd = real_dft(parts[1::2])
    half = size // 2
    result = [None] * (half + 1)
    for k in range(size // 4 + 1):
        (even_re, even_im), (odd_re, odd_im) = even[k], odd[k]
        if k == 0:
            result[0] = (even_re + odd_re, None)
            result[half] = (even_re - odd_re, None)
        elif 4 * k == size:
            result[k] = (even_re, -odd_re)
        else:
            c, s = math.cos(2.0 * math.pi * k / size), math.sin(2.0 * math.pi * k / size)
            turned_re = c * odd_re + s * odd_im
            turned_im = c * odd_im - s * odd_re
            result[k] = (even_re + turned_re, even_im + turned_im)
            result[half - k] = (even_re - turned_re, turned_im - even_im)
    return result


def outer_dft(parts):
    bins = real_dft(list(parts))
    out = [bins[0][0], bins[-1][0]]
    for re, im in bins[1:-1]:
        out += [re, im]
    return tuple(out)


def real_dft_transposed(bins):
    half = len(bins) - 1
    size = 2 * half
    if size == 2:
        return [bins[0][0] + bins[1][0], bins[0][0] - bins[1][0]]
    even, odd = [None] * (half // 2 + 1), [None] * (half // 2 + 1)
    for k in range(size // 4 + 1):
        re, im = bins[k]
        if k == 0:
            even[0] = (re + bins[half][0], None)
            odd[0] = (re - bins[half][0], None)
        elif 4 * k == size:
            even[k] = (re, None)
            odd[k] = (-im, None)
        else:
            other_re, other_im = bins[half - k]
            c, s = math.cos(2.0 * math.pi * k / size), math.sin(2.0 * math.pi * k / size)
            turned_re, turned_im = re - other_re, im + other_im
            even[k] = (re + other_re, im - other_im)
            odd[k] = (c * turned_re - s * turned_im, s * turned_re + c * turned_im)
    result = [None] * size
    result[0::2] = real_dft_transposed(even)
    result[1::2] = real_dft_transposed(odd)
    return result


def outer_dft_transposed(pieces):
    half = len(pieces) // 2
    bins = [(pieces[0], None)]
    bins += [(pieces[2 * k], pieces[2 * k + 1]) for k in range(1, half)]
    return real_dft_transposed(bins + [(pieces[1], None)])


def tables(length):
    outer = length // INNER
    within = np.arange(INNER)
    blocks = np.zeros((outer // 2, 2 * INNER, 2 * INNER), np.float64)
    order = np.zeros((outer // 2, 2 * INNER), np.int32)
    for b in range(outer // 2):
        for side in range(2):
            if b == 0:
                first = 0 if side == 0 else outer // 2
            else:
                first = b if side == 0 else outer - b
            freq = first + outer * within
            angle = 2.0 * math.pi / length * ((within[:, None] * freq[None, :]) % length)
            cos, sin = np.cos(angle), np.sin(angle)
            columns = slice(side * INNER, (side + 1) * INNER)
            order[b, columns] = freq
            if b == 0:
                blocks[b, columns, columns] = cos + sin
            else:
                sign = 1.0 if side == 0 else -1.0
                blocks[b, :INNER, columns] = cos + sin
                blocks[b, INNER:, columns] = sign * (sin - cos)
    return blocks.astype(np.float32), np.minimum(order, length - order)


def rows_forward(values, blocks, device_count):
    rows, length = values.shape
    pieces = outer_dft([values[:, i : i + INNER] for i in range(0, length, INNER)])
    stacked = jnp.stack(
        [jnp.concatenate(pieces[2 * b : 2 * b + 2], axis=1) for b in range(len(pieces) // 2)]
    )
    spectrum = jnp.einsum("brk,bkn->brn", stacked, blocks, precision=HIGH)
    columns = length // device_count
    spectrum = spectrum.reshape(spectrum.shape[0], rows, 2 * INNER // columns, columns)
    return spectrum.transpose(0, 2, 1, 3).reshape(device_count, rows, columns)


def rows_inverse(values, blocks):
    device_count, rows, columns = values.shape
    grouped = values.reshape(blocks.shape[0], 2 * INNER // columns, rows, columns)
    grouped = grouped.transpose(0, 2, 1, 3).reshape(blocks.shape[0], rows, 2 * INNER)
    stacked = jnp.einsum("brn,bkn->brk", grouped, blocks, precision=HIGH)
    pieces = []
    for b in range(blocks.shape[0]):
        pieces += [stacked[b, :, :INNER], stacked[b, :, INNER:]]
    return jnp.concatenate(outer_dft_transposed(pieces), axis=1)


def columns_forward(values, blocks):
    pieces = outer_dft([values[i : i + INNER] for i in range(0, values.shape[0], INNER)])
    stacked = jnp.concatenate(pieces, axis=0).reshape(
        blocks.shape[0], 2 * INNER, values.shape[1]
    )
    return jnp.einsum("bkn,bkc->bnc", blocks, stacked, precision=HIGH)


def columns_inverse(values, blocks):
    stacked = jnp.einsum("bkn,bnc->bkc", blocks, values, precision=HIGH)
    pieces = []
    for b in range(blocks.shape[0]):
        pieces += [stacked[b, :INNER], stacked[b, INNER:]]
    return jnp.concatenate(outer_dft_transposed(pieces), axis=0)


def exchange(values):
    return lax.all_to_all(values, BOTH, split_axis=0, concat_axis=0, tiled=True)


def split(values):
    high = values.astype(jnp.bfloat16)
    return high, (values - high.astype(jnp.float32)).astype(jnp.bfloat16)


def row_product(values, high_ref, low_ref, block, contract):
    rows = values.shape[0]
    high, low = split(values)
    dims = (((1,), (contract,)), ((), ()))
    main = lax.dot_general(
        jnp.concatenate([high, low], axis=0),
        high_ref[block],
        dims,
        preferred_element_type=jnp.float32,
    )
    rest = lax.dot_general(high, low_ref[block], dims, preferred_element_type=jnp.float32)
    return main[:rows] + (main[rows:] + rest)


def column_product(values, high_ref, low_ref, block):
    columns = values.shape[1]
    high, low = split(values)
    main = jnp.dot(
        high_ref[block],
        jnp.concatenate([high, low], axis=1),
        preferred_element_type=jnp.float32,
    )
    rest = jnp.dot(low_ref[block], high, preferred_element_type=jnp.float32)
    return main[:, :columns] + (main[:, columns:] + rest)


def surface_kernel(
    slab_count,
    pencil_count,
    potential_ref,
    eta_ref,
    velocity_ref,
    row_index_ref,
    col_index_ref,
    stencil_ref,
    share_ref,
    row_high_in,
    row_low_in,
    col_high_in,
    col_low_in,
    colt_high_in,
    colt_low_in,
    out_ref,
    velocity_out,
    row_high,
    row_low,
    col_high,
    col_low,
    colt_high,
    colt_low,
    potential,
    eta,
    back,
    total,
    curve,
    stage_rows,
    stage_cols,
    spectrum,
    magnitude,
    sent,
    held,
    tile_split,
    pick_cols,
    mix_high,
    mix_low,
    picks,
    arrived,
    flow,
    packed,
    halo,
    table_sem,
    send_sem,
    recv_sem,
    halo_send,
    halo_recv,
):
    slab = lax.axis_index("slab")
    pencil = lax.axis_index("pencil")
    device_count = slab_count * pencil_count
    own = pencil * slab_count + slab
    rows = sent.shape[2]
    columns = sent.shape[3]
    per_block = 2 * INNER // columns
    row_blocks = row_high.shape[0]
    col_blocks = col_high.shape[0]
    chunk = potential.shape[2]
    per_part = INNER // rows
    row_parts = 2 * row_blocks
    col_parts = 2 * col_blocks
    step = 8

    pairs = (
        (row_high_in, row_high),
        (row_low_in, row_low),
        (colt_high_in, colt_high),
        (colt_low_in, colt_low),
        (col_high_in, col_high),
        (col_low_in, col_low),
    )
    tables_in = [
        pltpu.make_async_copy(source, target, table_sem.at[i])
        for i, (source, target) in enumerate(pairs)
    ]
    for copy in tables_in:
        copy.start()

    def partner(i):
        return lax.rem(pencil + lax.rem(i, pencil_count), pencil_count), lax.rem(
            slab + i // pencil_count, slab_count
        )

    halo[...] = jnp.zeros(halo.shape, jnp.float32)
    barrier = pltpu.get_barrier_semaphore()

    @pl.loop(1, device_count)
    def _(i):
        to_pencil, to_slab = partner(i)
        pl.semaphore_signal(
            barrier,
            inc=1,
            device_id={"slab": to_slab, "pencil": to_pencil},
            device_id_type=pl.DeviceIdType.MESH,
        )

    pl.semaphore_wait(barrier, device_count - 1)

    def remote(source, target, index, to_slab, to_pencil):
        return pltpu.make_async_remote_copy(
            src_ref=source,
            dst_ref=target,
            send_sem=send_sem.at[index],
            recv_sem=recv_sem.at[index],
            device_id={"slab": to_slab, "pencil": to_pencil},
            device_id_type=pl.DeviceIdType.MESH,
        )

    def start(n, to):
        to_slab, to_pencil = lax.rem(to, slab_count), to // slab_count

        @pl.when(to != own)
        def _():
            remote(sent.at[n, to], held.at[n, own], n, to_slab, to_pencil).start()

    def send(n, first, last):
        @pl.loop(first, last)
        def _(i):
            to_pencil, to_slab = partner(i)
            to = to_pencil * slab_count + to_slab
            remote(sent.at[n, to], held.at[n, own], n, to_slab, to_pencil).start()

    def all_of(n):
        others = pl.ds(0, device_count - 1)
        return remote(sent.at[n, others], held.at[n, others], n, slab, pencil)

    def send_slab(source_of, target, n):
        for i in range(1, slab_count):
            to = lax.rem(slab + i, slab_count)
            remote(source_of(to), target.at[slab], n, to, pencil).start()

    def all_of_slab(target, n):
        others = target.at[pl.ds(0, slab_count - 1)]
        return remote(others, others, n, slab, pencil)

    fields = sent.shape[0]

    def tile_rows(ref):
        return lambda to: ref.at[pl.ds(pl.multiple_of(to * rows, rows), rows)]

    own_rows = pl.ds(pl.multiple_of(slab * rows, rows), rows)
    send_slab(tile_rows(potential_ref), potential, fields)
    send_slab(tile_rows(eta_ref), eta, fields + 1)
    potential[slab] = potential_ref[own_rows]
    eta[slab] = eta_ref[own_rows]

    def part_of(ref, part, at):
        start = part * INNER % chunk
        return ref.at[part * INNER // chunk, at, pl.ds(start, INNER)]

    def piece_of(piece, at):
        return stage_rows.at[piece // 2, at, pl.ds(piece % 2 * INNER, INNER)]

    def over_rows(body):
        @pl.loop(0, rows // step)
        def _(i):
            body(pl.ds(pl.multiple_of(i * step, step), step))

    def begin_rows(parts, at):
        for piece, value in enumerate(outer_dft(parts)):
            piece_of(piece, at)[...] = value

    def finish_rows(n):
        @pl.loop(0, row_blocks)
        def _(i):
            b = lax.rem(i + own // per_block, row_blocks)
            result = row_product(stage_rows[b], row_high, row_low, b, 0)
            for i in range(per_block):
                sent[n, b * per_block + i] = result[:, i * columns : (i + 1) * columns]
                start(n, b * per_block + i)

        held[n, own] = sent[n, own]

    def inverse_rows(n, use):
        if n in (2, 3, 6, 8):
            all_of(n).wait_recv()

        @pl.loop(0, row_blocks)
        def _(b):
            values = jnp.concatenate(
                [held[n, b * per_block + i] for i in range(per_block)], axis=1
            )
            stage_rows[b] = row_product(values, row_high, row_low, b, 1)

        def body(at):
            use(at, outer_dft_transposed([piece_of(p, at)[...] for p in range(row_parts)]))

        over_rows(body)

    def over_columns(body):
        @pl.loop(0, 2 * per_part)
        def _(i):
            body(i // 2, pl.multiple_of(lax.rem(i, 2) * (rows // 2), rows // 2))

    def forward_columns(n):
        if n == 0:
            all_of(n).wait_recv()

        def body(q, start):
            parts = [held[n, p * per_part + q, pl.ds(start, rows // 2)] for p in range(col_parts)]
            for piece, value in enumerate(outer_dft(parts)):
                at = pl.multiple_of(piece % 2 * INNER + q * rows + start, rows // 2)
                stage_cols[piece // 2, pl.ds(at, rows // 2)] = value

        over_columns(body)

        @pl.loop(0, col_blocks)
        def _(b):
            spectrum[b] = column_product(stage_cols[b], colt_high, colt_low, b)

    def inverse_columns(n, now):
        @pl.loop(0, col_blocks)
        def _(b):
            values = spectrum[b] * magnitude[b]
            spectrum[b] = values
            stage_cols[b] = column_product(values, col_high, col_low, b)

        @pl.loop(0, per_part)
        def _(i):
            q = lax.rem(i + own, per_part)
            for half in range(2):
                offset = half * (rows // 2)
                pieces = []
                for piece in range(col_parts):
                    at = pl.multiple_of(piece % 2 * INNER + q * rows + offset, rows // 2)
                    pieces.append(stage_cols[piece // 2, pl.ds(at, rows // 2)])
                for p, value in enumerate(outer_dft_transposed(pieces)):
                    sent[n, p * per_part + q, pl.ds(offset, rows // 2)] = value * (
                        1.0 / (NXW * NYW)
                    )
            if now:
                for p in range(col_parts):
                    start(n, p * per_part + q)

        held[n, own] = sent[n, own]

    capacity = row_index_ref.shape[2]
    block_x, block_y, depth_cells = velocity_ref.shape[1:]
    tile_rows_count, tile_cols = eta_ref.shape
    cells = (block_x, block_y, depth_cells)

    def position(axis):
        return lax.broadcasted_iota(jnp.int32, cells, axis)

    links = (
        (slab < slab_count - 1, slab + 1, pencil, slab > 0),
        (slab > 0, slab - 1, pencil, slab < slab_count - 1),
        (pencil < pencil_count - 1, slab, pencil + 1, pencil > 0),
        (pencil > 0, slab, pencil - 1, pencil < pencil_count - 1),
    )

    def halo_copy(k, side, to_slab, to_pencil):
        return pltpu.make_async_remote_copy(
            src_ref=packed.at[k, side],
            dst_ref=halo.at[k, side],
            send_sem=halo_send.at[4 * k + side],
            recv_sem=halo_recv.at[4 * k + side],
            device_id={"slab": to_slab, "pencil": to_pencil},
            device_id_type=pl.DeviceIdType.MESH,
        )

    def send_halo(k, velocity):
        for c in range(3):
            packed[k, 0, c] = velocity[c][block_x - 1]
            packed[k, 1, c] = velocity[c][0]
            packed[k, 2, c] = velocity[c][:, block_y - 1]
            packed[k, 3, c] = velocity[c][:, 0]
        for side, (sends, to_slab, to_pencil, _) in enumerate(links):

            @pl.when(sends)
            def _(side=side, to_slab=to_slab, to_pencil=to_pencil):
                halo_copy(k, side, to_slab, to_pencil).start()

    def wait_halo(k):
        for side, (_, _, _, receives) in enumerate(links):

            @pl.when(receives)
            def _(side=side):
                halo_copy(k, side, slab, pencil).wait_recv()

    def end_halo(k):
        for side, (sends, _, _, _) in enumerate(links):

            @pl.when(sends)
            def _(side=side):
                halo_copy(k, side, slab, pencil).wait_send()

    def predicted(k, velocity):
        result = []
        for c in range(3):
            here = velocity[c]
            minus_x = jnp.concatenate([halo[k, 0, c][None], here[:-1]], axis=0)
            plus_x = jnp.concatenate([here[1:], halo[k, 1, c][None]], axis=0)
            minus_y = jnp.where(
                position(1) == 0, halo[k, 2, c][:, None], pltpu.roll(here, 1, 1)
            )
            plus_y = jnp.where(
                position(1) == block_y - 1,
                halo[k, 3, c][:, None],
                pltpu.roll(here, block_y - 1, 1),
            )
            minus_z = jnp.where(position(2) == 0, 0.0, pltpu.roll(here, 1, 2))
            plus_z = jnp.where(
                position(2) == depth_cells - 1, 0.0, pltpu.roll(here, depth_cells - 1, 2)
            )
            laplace = (
                plus_x + minus_x + (plus_y + minus_y) + (plus_z + minus_z) - 6.0 * here
            )
            advect = (
                velocity[0] * (plus_x - minus_x)
                + velocity[1] * (plus_y - minus_y)
                + velocity[2] * (plus_z - minus_z)
            )
            result.append(here + TIME_STEP * (VISCOSITY * laplace - 0.5 * advect))
        return result

    def split_tile(ref):
        @pl.loop(0, slab_count)
        def _(i):
            at = pl.multiple_of(i * rows, rows)
            high, low = split(ref[pl.ds(at, rows)])
            tile_split[pl.ds(at, rows)] = high
            tile_split[pl.ds(pl.multiple_of(tile_rows_count + at, rows), rows)] = low

    def pick(d):
        both = jnp.dot(tile_split[...], pick_cols[d], preferred_element_type=jnp.float32)
        row = lax.broadcasted_iota(jnp.int32, (tile_rows_count, capacity), 0)
        found = both[:tile_rows_count] + both[tile_rows_count:]
        return jnp.sum(jnp.where(row == row_index_ref[d], found, 0.0), axis=0, keepdims=True)

    list_row = lax.broadcasted_iota(jnp.int32, (8, capacity), 0)

    def prepare_flow():
        split_tile(eta_ref)

        @pl.loop(0, slab_count)
        def _(d):
            column = lax.broadcasted_iota(jnp.int32, (tile_cols, capacity), 0)
            chosen = jnp.where(column == col_index_ref[d], 1.0, 0.0)
            pick_cols[d] = chosen.astype(jnp.bfloat16)
            slot = lax.broadcasted_iota(jnp.int32, (capacity, block_x * block_y), 0) + d * capacity
            mixing = jnp.zeros(slot.shape, jnp.float32)
            for q in range(stencil_ref.shape[0]):
                mixing = mixing + jnp.where(slot == stencil_ref[q], share_ref[q], 0.0)
            mix_high[d], mix_low[d] = split(mixing)

        @pl.loop(0, slab_count)
        def _(d):
            picks[d] = jnp.where(list_row == 0, pick(d), 0.0)

        wait_halo(0)
        for c, value in enumerate(predicted(0, [velocity_ref[c] for c in range(3)])):
            flow[c] = value

    def finish_flow():
        split_tile(out_ref)

        @pl.loop(1, slab_count + 1)
        def _(i):
            d = lax.rem(slab + i, slab_count)
            picks[d] = jnp.where(list_row == 1, pick(d), picks[d])

            @pl.when(i < slab_count)
            def _():
                remote(picks.at[d], arrived.at[slab], fields + 3, d, pencil).start()

        arrived[slab] = picks[slab]
        all_of_slab(arrived, fields + 3).wait_recv()
        surface = jnp.zeros((8, block_x * block_y), jnp.float32)
        for r in range(slab_count):
            high, low = split(arrived[r])
            surface += jnp.dot(high, mix_high[r], preferred_element_type=jnp.float32) + (
                jnp.dot(low, mix_high[r], preferred_element_type=jnp.float32)
                + jnp.dot(high, mix_low[r], preferred_element_type=jnp.float32)
            )
        turned = surface.T
        level = position(2).astype(jnp.float32)
        decay = jnp.exp(-DEPTH_RATE * (depth_cells - 1.0 - level) / depth_cells)

        def target(c):
            spread = jnp.broadcast_to(turned[:, c : c + 1], (block_x * block_y, depth_cells))
            return spread.reshape(cells) * decay

        targets = [target(0), None, target(1)]
        pos_x = (slab * block_x + position(0)).astype(jnp.float32)
        pos_y = (pencil * block_y + position(1)).astype(jnp.float32)
        reach_x = float(max(1, slab_count // 16) * block_x)
        total_x, total_y = float(block_x * slab_count), float(block_y * pencil_count)
        relax = jnp.maximum(
            jnp.maximum(ramp_weight(pos_x, reach_x), ramp_weight(total_x - 1.0 - pos_x, reach_x)),
            jnp.maximum(
                ramp_weight(pos_y, float(block_y)),
                ramp_weight(total_y - 1.0 - pos_y, float(block_y)),
            ),
        )

        def blend(values):
            blended = [(1.0 - relax) * value for value in values]
            return [
                value if aim is None else value + relax * aim
                for value, aim in zip(blended, targets)
            ]

        velocity = blend([flow[c] for c in range(3)])
        send_halo(1, velocity)
        wait_halo(1)
        for c, value in enumerate(blend(predicted(1, velocity))):
            velocity_out[c] = value
        end_halo(0)
        end_halo(1)
        all_of_slab(arrived, fields + 3).wait_send()

    send_halo(0, [velocity_ref[c] for c in range(3)])

    outer_x, outer_y = row_parts, col_parts
    lane = own * columns + lax.broadcasted_iota(jnp.int32, (2 * INNER, columns), 1)

    def wave(index, block, outer, length):
        first = jnp.where(
            index < INNER,
            jnp.where(block == 0, 0, block),
            jnp.where(block == 0, outer // 2, outer - block),
        )
        freq = first + outer * (index % INNER)
        folded = jnp.minimum(freq, length - freq).astype(jnp.float32)
        return 2.0 * math.pi / length * folded

    wave_x = wave(lane % (2 * INNER), lane // (2 * INNER), outer_x, NXW)
    place = lax.broadcasted_iota(jnp.int32, (2 * INNER, columns), 0)
    for b in range(col_blocks):
        wave_y = wave(place, jnp.full(place.shape, b, jnp.int32), outer_y, NYW)
        magnitude[b] = jnp.sqrt(wave_x * wave_x + wave_y * wave_y)

    all_of_slab(potential, fields).wait_recv()
    over_rows(
        lambda at: begin_rows([part_of(potential, p, at)[...] for p in range(row_parts)], at)
    )
    tables_in[0].wait()
    tables_in[1].wait()
    finish_rows(0)
    for copy in tables_in[2:]:
        copy.wait()

    prepare_flow()
    forward_columns(0)
    inverse_columns(1, True)
    inverse_columns(2, False)
    inverse_columns(3, False)
    all_of_slab(eta, fields + 1).wait_recv()

    def use_slope_one(at, parts):
        for p, value in enumerate(parts):
            part_of(total, p, at)[...] = value
        begin_rows([-part_of(eta, p, at)[...] * value for p, value in enumerate(parts)], at)

    def use_curve_one(at, parts):
        for p, value in enumerate(parts):
            height = part_of(eta, p, at)[...]
            term = height * value
            part_of(total, p, at)[...] += term
            part_of(curve, p, at)[...] = 0.5 * height * term

    def use_cubic_one(at, parts):
        for p, value in enumerate(parts):
            height = part_of(eta, p, at)[...]
            part_of(total, p, at)[...] += 0.5 * height * height * value

    def use_slope_two(at, parts):
        following = []
        for p, value in enumerate(parts):
            part_of(total, p, at)[...] += value
            following.append(-part_of(eta, p, at)[...] * value - part_of(curve, p, at)[...])
        begin_rows(following, at)

    def use_curve_two(at, parts):
        for p, value in enumerate(parts):
            part_of(total, p, at)[...] += part_of(eta, p, at)[...] * value

    def use_slope_three(at, parts):
        for p, value in enumerate(parts):
            part_of(total, p, at)[...] += value

    middle = device_count // 2
    all_of(1).wait_recv()
    send(2, 1, device_count)
    inverse_rows(1, use_slope_one)
    finish_rows(4)
    inverse_rows(2, use_curve_one)
    all_of(4).wait_recv()
    send(3, 1, middle)
    forward_columns(4)
    inverse_columns(5, True)
    inverse_columns(6, False)
    all_of(5).wait_recv()
    send(6, 1, device_count)
    inverse_rows(5, use_slope_two)
    finish_rows(7)
    inverse_rows(6, use_curve_two)
    all_of(7).wait_recv()
    send(3, middle, device_count)
    forward_columns(7)
    inverse_columns(8, True)
    inverse_rows(3, use_cubic_one)
    inverse_rows(8, use_slope_three)

    send_slab(lambda to: total.at[to], back, fields + 2)
    out_ref[own_rows] = total[slab]
    all_of_slab(back, fields + 2).wait_recv()
    for i in range(1, slab_count):
        source = lax.rem(slab + i, slab_count)
        out_ref[pl.ds(pl.multiple_of(source * rows, rows), rows)] = back[source]
    finish_flow()
    for n in range(fields):
        all_of(n).wait_send()
    all_of_slab(potential, fields).wait_send()
    all_of_slab(eta, fields + 1).wait_send()
    all_of_slab(back, fields + 2).wait_send()


def two_terms(table):
    high = table.astype(jnp.bfloat16)
    low = (table - high.astype(np.float32)).astype(jnp.bfloat16)
    return jnp.asarray(high), jnp.asarray(low)


def whole_step(
    potential, eta, velocity, points, counts, stencil, interp_weight, slab_count, pencil_count
):
    tile_rows, tile_cols = eta.shape
    device_count = slab_count * pencil_count
    rows, columns = NYW // device_count, NXW // device_count
    row_table, _ = tables(NXW)
    col_table, _ = tables(NYW)
    constants = [
        *two_terms(row_table),
        *two_terms(col_table),
        *two_terms(np.ascontiguousarray(col_table.transpose(0, 2, 1))),
    ]
    capacity = points.shape[1]
    block_x, block_y, _ = velocity.shape[1:]
    live = jnp.arange(capacity, dtype=jnp.int32)[None, :] < counts[:, None]
    row_index = jnp.where(live, points // tile_cols, -1)[:, None, :]
    col_index = (points % tile_cols)[:, None, :]
    shares = interp_weight / jnp.sum(interp_weight, axis=0)
    flat = (stencil.shape[0], 1, block_x * block_y)
    spectrum = (col_table.shape[0], 2 * INNER, columns)
    list_shape = (slab_count, 8, capacity)
    halo_shape = (STEPS, 4, 3, block_x, velocity.shape[3])
    fields = 9
    strip = pltpu.VMEM((slab_count, rows, tile_cols), jnp.float32)
    vmem = pl.BlockSpec(memory_space=pltpu.VMEM)
    return pl.pallas_call(
        lambda *refs: surface_kernel(slab_count, pencil_count, *refs),
        out_shape=(
            jax.ShapeDtypeStruct((tile_rows, tile_cols), jnp.float32),
            jax.ShapeDtypeStruct(velocity.shape, jnp.float32),
        ),
        in_specs=[vmem] * 7 + [pl.BlockSpec(memory_space=pl.ANY)] * 6,
        out_specs=(vmem, vmem),
        scratch_shapes=[
            *(pltpu.VMEM(table.shape, jnp.bfloat16) for table in constants),
            *([strip] * 5),
            pltpu.VMEM(row_table.shape[:1] + (rows, 2 * INNER), jnp.float32),
            pltpu.VMEM(spectrum, jnp.float32),
            pltpu.VMEM(spectrum, jnp.float32),
            pltpu.VMEM(spectrum, jnp.float32),
            pltpu.VMEM((fields, device_count, rows, columns), jnp.float32),
            pltpu.VMEM((fields, device_count, rows, columns), jnp.float32),
            pltpu.VMEM((2 * tile_rows, tile_cols), jnp.bfloat16),
            pltpu.VMEM((slab_count, tile_cols, capacity), jnp.bfloat16),
            pltpu.VMEM((slab_count, capacity, block_x * block_y), jnp.bfloat16),
            pltpu.VMEM((slab_count, capacity, block_x * block_y), jnp.bfloat16),
            pltpu.VMEM(list_shape, jnp.float32),
            pltpu.VMEM(list_shape, jnp.float32),
            pltpu.VMEM(velocity.shape, jnp.float32),
            pltpu.VMEM(halo_shape, jnp.float32),
            pltpu.VMEM(halo_shape, jnp.float32),
            pltpu.SemaphoreType.DMA((6,)),
            pltpu.SemaphoreType.DMA((fields + 4,)),
            pltpu.SemaphoreType.DMA((fields + 4,)),
            pltpu.SemaphoreType.DMA((4 * STEPS,)),
            pltpu.SemaphoreType.DMA((4 * STEPS,)),
        ],
        compiler_params=pltpu.CompilerParams(
            collective_id=0, has_side_effects=True, vmem_limit_bytes=60 * 1024 * 1024
        ),
    )(
        potential,
        eta,
        velocity,
        row_index,
        col_index,
        stencil.reshape(flat),
        shares.reshape(flat),
        *constants,
    )


def surface_plain(potential, eta, magnitude, row_table, column_table, slab_count):
    tile_rows, tile_cols = eta.shape
    columns = magnitude.shape[-1]
    device_count = NXW // columns
    rows = NYW // device_count
    row_blocks, column_blocks = jnp.asarray(row_table), jnp.asarray(column_table)
    both = jnp.stack([potential, eta]).reshape(2, slab_count, rows, tile_cols)
    both = lax.all_to_all(both, "slab", split_axis=1, concat_axis=1, tiled=True)
    both = both.transpose(0, 2, 1, 3).reshape(2, rows, NXW)
    potential, eta = both[0], both[1]
    first_mult = magnitude * (1.0 / (NXW * NYW))
    second_mult = magnitude * first_mult
    third_mult = magnitude * second_mult

    def forward(field):
        arrived = exchange(rows_forward(field, row_blocks, device_count))
        return columns_forward(arrived.reshape(NYW, columns), column_blocks)

    def inverse(spectrum):
        field = columns_inverse(spectrum, column_blocks)
        return rows_inverse(exchange(field.reshape(device_count, rows, columns)), row_blocks)

    spectrum = forward(potential)
    slope_one = inverse(spectrum * first_mult)
    curve_one = inverse(spectrum * second_mult)
    cubic_one = inverse(spectrum * third_mult)
    spectrum = forward(-eta * slope_one)
    slope_two = inverse(spectrum * first_mult)
    curve_two = inverse(spectrum * second_mult)
    spectrum = forward(-eta * slope_two - 0.5 * eta * eta * curve_one)
    slope_three = inverse(spectrum * first_mult)
    vertical = (
        slope_one
        + slope_two
        + eta * curve_one
        + slope_three
        + eta * curve_two
        + 0.5 * eta * eta * cubic_one
    )
    vertical = vertical.reshape(rows, slab_count, tile_cols).transpose(1, 0, 2)
    vertical = lax.all_to_all(vertical, "slab", split_axis=0, concat_axis=0, tiled=True)
    vertical = vertical.reshape(tile_rows, tile_cols)

    return vertical


def ramp_weight(distance, reach_len):
    ratio = jnp.clip(1.0 - distance / reach_len, 0.0, 1.0)
    return ratio * ratio


def blend_weight(pos_x, pos_y, total_x, total_y, reach_x, reach_y):
    along_x = jnp.maximum(ramp_weight(pos_x, reach_x), ramp_weight(total_x - 1.0 - pos_x, reach_x))
    across = jnp.maximum(ramp_weight(pos_y, reach_y), ramp_weight(total_y - 1.0 - pos_y, reach_y))
    return jnp.maximum(along_x[:, None], across[None, :])[:, :, None]


def neighbours(shard, axis, dim):
    size, length = lax.axis_size(axis), shard.shape[dim]
    up = [(i, i + 1) for i in range(size - 1)]
    down = [(i + 1, i) for i in range(size - 1)]
    before = lax.ppermute(lax.slice_in_dim(shard, length - 1, length, axis=dim), axis, up)
    after = lax.ppermute(lax.slice_in_dim(shard, 0, 1, axis=dim), axis, down)
    minus = jnp.concatenate([before, lax.slice_in_dim(shard, 0, length - 1, axis=dim)], axis=dim)
    plus = jnp.concatenate([lax.slice_in_dim(shard, 1, length, axis=dim), after], axis=dim)
    return minus, plus


def predict(velocity):
    minus_x, plus_x = neighbours(velocity, "slab", 1)
    minus_y, plus_y = neighbours(velocity, "pencil", 2)
    padded = jnp.pad(velocity, ((0, 0), (0, 0), (0, 0), (1, 1)))
    minus_z, plus_z = padded[..., :-2], padded[..., 2:]
    laplace = plus_x + minus_x + (plus_y + minus_y) + (plus_z + minus_z) - 6.0 * velocity
    advect = (
        velocity[0] * (plus_x - minus_x)
        + velocity[1] * (plus_y - minus_y)
        + velocity[2] * (plus_z - minus_z)
    )
    return velocity + TIME_STEP * (VISCOSITY * laplace - 0.5 * advect)


def on_device(
    surface_eta, surface_potential, velocity, send_point, send_count, stencil, interp_weight
):
    slab_count = lax.axis_size("slab")
    pencil_count = lax.axis_size("pencil")
    device_count = slab_count * pencil_count
    slab_index = lax.axis_index("slab")
    pencil_index = lax.axis_index("pencil")
    tile_rows, tile_cols = surface_eta.shape
    rows = NYW // device_count
    columns = NXW // device_count
    if (
        columns % 128 == 0
        and rows % 16 == 0
        and INNER % rows == 0
        and velocity.shape[1] == velocity.shape[2]
        and STEPS == 2
    ):
        return whole_step(
            surface_potential,
            surface_eta,
            velocity,
            send_point[0, 0],
            send_count[0, 0],
            stencil,
            interp_weight,
            slab_count,
            pencil_count,
        )
    own = pencil_index * slab_count + slab_index
    row_table, row_order = tables(NXW)
    column_table, column_order = tables(NYW)
    wave_x = 2.0 * math.pi / NXW * jnp.asarray(row_order.reshape(-1)).astype(jnp.float32)
    wave_x = lax.dynamic_slice(wave_x, (own * columns,), (columns,))
    wave_y = 2.0 * math.pi / NYW * jnp.asarray(column_order).astype(jnp.float32)[:, :, None]
    magnitude = jnp.sqrt(wave_x * wave_x + wave_y * wave_y)
    vertical = surface_plain(
        surface_potential, surface_eta, magnitude, row_table, column_table, slab_count
    )

    points = send_point[0, 0]
    capacity = points.shape[1]
    counts = send_count[0, 0]
    flat_points = points.reshape(-1)
    live = (jnp.arange(capacity, dtype=jnp.int32)[None, :] < counts[:, None]).reshape(-1)
    row_pick = (
        (flat_points // tile_cols)[:, None] == jnp.arange(tile_rows, dtype=jnp.int32)[None, :]
    ).astype(jnp.float32)
    column_pick = (flat_points % tile_cols)[:, None] == jnp.arange(tile_cols, dtype=jnp.int32)[
        None, :
    ]
    column_pick = column_pick & live[:, None]

    def pick(tile):
        picked_rows = jnp.dot(row_pick, tile, precision=HIGH)
        return jnp.sum(jnp.where(column_pick, picked_rows, 0.0), axis=1)

    picked = jnp.stack([pick(surface_eta), pick(vertical)]).reshape(2, slab_count, capacity)
    arrived = lax.all_to_all(picked, "slab", split_axis=1, concat_axis=1, tiled=True).reshape(
        2, slab_count * capacity
    )
    block_x, block_y, depth_cells = velocity.shape[1:]
    shares = interp_weight / jnp.sum(interp_weight, axis=0)
    slots = jnp.arange(slab_count * capacity, dtype=jnp.int32)[:, None]
    mixing = 0.0
    for q in range(stencil.shape[0]):
        mixing = mixing + jnp.where(
            slots == stencil[q].reshape(1, -1), shares[q].reshape(1, -1), 0.0
        )
    surface_at = jnp.dot(arrived, mixing, precision=lax.Precision.HIGHEST)
    surface_at = surface_at.reshape(2, block_x, block_y)

    zone_slabs = max(1, slab_count // 16)
    pos_x = (slab_index * block_x + jnp.arange(block_x, dtype=jnp.int32)).astype(jnp.float32)
    pos_y = (pencil_index * block_y + jnp.arange(block_y, dtype=jnp.int32)).astype(jnp.float32)
    relax_weight = blend_weight(
        pos_x,
        pos_y,
        float(block_x * slab_count),
        float(block_y * pencil_count),
        float(zone_slabs * block_x),
        float(block_y),
    )
    levels = jnp.arange(depth_cells, dtype=jnp.float32)
    depth_decay = jnp.exp(-DEPTH_RATE * (depth_cells - 1.0 - levels) / depth_cells)
    target = jnp.stack(
        [
            surface_at[0][:, :, None] * depth_decay,
            jnp.zeros((block_x, block_y, depth_cells), jnp.float32),
            surface_at[1][:, :, None] * depth_decay,
        ]
    )
    for substep in range(STEPS):
        velocity = (1.0 - relax_weight) * predict(velocity) + relax_weight * target
    return (vertical, velocity)


def solution(mesh):
    in_specs = (
        P("pencil", "slab"),
        P("pencil", "slab"),
        P(None, "slab", "pencil", None),
        P("slab", "pencil", None, None),
        P("slab", "pencil", None),
        P(None, "slab", "pencil"),
        P(None, "slab", "pencil"),
    )
    out_specs = (P("pencil", "slab"), P(None, "slab", "pencil", None))
    return jax.shard_map(
        on_device, mesh=mesh, in_specs=in_specs, out_specs=out_specs, check_vma=False
    )
```

```python
import math

import jax
import jax.numpy as jnp
import numpy as np
from jax import lax
from jax.experimental import pallas as pl
from jax.experimental.pallas import tpu as pltpu
from jax.sharding import PartitionSpec as P

NXW = 4096
NYW = 2048
STEPS = 2
INNER = 256


TIME_STEP = 0.2
VISCOSITY = 0.6
DEPTH_RATE = 3.0

HIGH = lax.Precision.HIGH
BOTH = ("pencil", "slab")


def real_dft(parts):
    size = len(parts)
    if size == 2:
        return [(parts[0] + parts[1], None), (parts[0] - parts[1], None)]
    even = real_dft(parts[0::2])
    odd = real_dft(parts[1::2])
    half = size // 2
    result = [None] * (half + 1)
    for k in range(size // 4 + 1):
        (even_re, even_im), (odd_re, odd_im) = even[k], odd[k]
        if k == 0:
            result[0] = (even_re + odd_re, None)
            result[half] = (even_re - odd_re, None)
        elif 4 * k == size:
            result[k] = (even_re, -odd_re)
        else:
            c, s = math.cos(2.0 * math.pi * k / size), math.sin(2.0 * math.pi * k / size)
            turned_re = c * odd_re + s * odd_im
            turned_im = c * odd_im - s * odd_re
            result[k] = (even_re + turned_re, even_im + turned_im)
            result[half - k] = (even_re - turned_re, turned_im - even_im)
    return result


def outer_dft(parts):
    bins = real_dft(list(parts))
    out = [bins[0][0], bins[-1][0]]
    for re, im in bins[1:-1]:
        out += [re, im]
    return tuple(out)


def real_dft_transposed(bins):
    half = len(bins) - 1
    size = 2 * half
    if size == 2:
        return [bins[0][0] + bins[1][0], bins[0][0] - bins[1][0]]
    even, odd = [None] * (half // 2 + 1), [None] * (half // 2 + 1)
    for k in range(size // 4 + 1):
        re, im = bins[k]
        if k == 0:
            even[0] = (re + bins[half][0], None)
            odd[0] = (re - bins[half][0], None)
        elif 4 * k == size:
            even[k] = (re, None)
            odd[k] = (-im, None)
        else:
            other_re, other_im = bins[half - k]
            c, s = math.cos(2.0 * math.pi * k / size), math.sin(2.0 * math.pi * k / size)
            turned_re, turned_im = re - other_re, im + other_im
            even[k] = (re + other_re, im - other_im)
            odd[k] = (c * turned_re - s * turned_im, s * turned_re + c * turned_im)
    result = [None] * size
    result[0::2] = real_dft_transposed(even)
    result[1::2] = real_dft_transposed(odd)
    return result


def outer_dft_transposed(pieces):
    half = len(pieces) // 2
    bins = [(pieces[0], None)]
    bins += [(pieces[2 * k], pieces[2 * k + 1]) for k in range(1, half)]
    return real_dft_transposed(bins + [(pieces[1], None)])


def tables(length):
    outer = length // INNER
    within = np.arange(INNER)
    blocks = np.zeros((outer // 2, 2 * INNER, 2 * INNER), np.float64)
    order = np.zeros((outer // 2, 2 * INNER), np.int32)
    for b in range(outer // 2):
        for side in range(2):
            if b == 0:
                first = 0 if side == 0 else outer // 2
            else:
                first = b if side == 0 else outer - b
            freq = first + outer * within
            angle = 2.0 * math.pi / length * ((within[:, None] * freq[None, :]) % length)
            cos, sin = np.cos(angle), np.sin(angle)
            columns = slice(side * INNER, (side + 1) * INNER)
            order[b, columns] = freq
            if b == 0:
                blocks[b, columns, columns] = cos + sin
            else:
                sign = 1.0 if side == 0 else -1.0
                blocks[b, :INNER, columns] = cos + sin
                blocks[b, INNER:, columns] = sign * (sin - cos)
    return blocks.astype(np.float32), np.minimum(order, length - order)


def rows_forward(values, blocks, device_count):
    rows, length = values.shape
    pieces = outer_dft([values[:, i : i + INNER] for i in range(0, length, INNER)])
    stacked = jnp.stack(
        [jnp.concatenate(pieces[2 * b : 2 * b + 2], axis=1) for b in range(len(pieces) // 2)]
    )
    spectrum = jnp.einsum("brk,bkn->brn", stacked, blocks, precision=HIGH)
    columns = length // device_count
    spectrum = spectrum.reshape(spectrum.shape[0], rows, 2 * INNER // columns, columns)
    return spectrum.transpose(0, 2, 1, 3).reshape(device_count, rows, columns)


def rows_inverse(values, blocks):
    device_count, rows, columns = values.shape
    grouped = values.reshape(blocks.shape[0], 2 * INNER // columns, rows, columns)
    grouped = grouped.transpose(0, 2, 1, 3).reshape(blocks.shape[0], rows, 2 * INNER)
    stacked = jnp.einsum("brn,bkn->brk", grouped, blocks, precision=HIGH)
    pieces = []
    for b in range(blocks.shape[0]):
        pieces += [stacked[b, :, :INNER], stacked[b, :, INNER:]]
    return jnp.concatenate(outer_dft_transposed(pieces), axis=1)


def columns_forward(values, blocks):
    pieces = outer_dft([values[i : i + INNER] for i in range(0, values.shape[0], INNER)])
    stacked = jnp.concatenate(pieces, axis=0).reshape(
        blocks.shape[0], 2 * INNER, values.shape[1]
    )
    return jnp.einsum("bkn,bkc->bnc", blocks, stacked, precision=HIGH)


def columns_inverse(values, blocks):
    stacked = jnp.einsum("bkn,bnc->bkc", blocks, values, precision=HIGH)
    pieces = []
    for b in range(blocks.shape[0]):
        pieces += [stacked[b, :INNER], stacked[b, INNER:]]
    return jnp.concatenate(outer_dft_transposed(pieces), axis=0)


def exchange(values):
    return lax.all_to_all(values, BOTH, split_axis=0, concat_axis=0, tiled=True)


def split(values):
    high = values.astype(jnp.bfloat16)
    return high, (values - high.astype(jnp.float32)).astype(jnp.bfloat16)


def row_product(values, high_ref, low_ref, block, contract):
    rows = values.shape[0]
    high, low = split(values)
    dims = (((1,), (contract,)), ((), ()))
    main = lax.dot_general(
        jnp.concatenate([high, low], axis=0),
        high_ref[block],
        dims,
        preferred_element_type=jnp.float32,
    )
    rest = lax.dot_general(high, low_ref[block], dims, preferred_element_type=jnp.float32)
    return main[:rows] + (main[rows:] + rest)


def column_product(values, high_ref, low_ref, block):
    columns = values.shape[1]
    high, low = split(values)
    main = jnp.dot(
        high_ref[block],
        jnp.concatenate([high, low], axis=1),
        preferred_element_type=jnp.float32,
    )
    rest = jnp.dot(low_ref[block], high, preferred_element_type=jnp.float32)
    return main[:, :columns] + (main[:, columns:] + rest)


def surface_kernel(
    slab_count,
    pencil_count,
    potential_ref,
    eta_ref,
    velocity_ref,
    points_ref,
    counts_ref,
    mixing_ref,
    row_high_in,
    row_low_in,
    col_high_in,
    col_low_in,
    colt_high_in,
    colt_low_in,
    out_ref,
    velocity_out,
    row_high,
    row_low,
    col_high,
    col_low,
    colt_high,
    colt_low,
    potential,
    eta,
    back,
    total,
    curve,
    stage_rows,
    stage_cols,
    spectrum,
    magnitude,
    sent,
    held,
    tile_split,
    pick_cols,
    mix_high,
    mix_low,
    picks,
    arrived,
    flow,
    packed,
    halo,
    table_sem,
    send_sem,
    recv_sem,
    halo_send,
    halo_recv,
):
    slab = lax.axis_index("slab")
    pencil = lax.axis_index("pencil")
    device_count = slab_count * pencil_count
    own = pencil * slab_count + slab
    own_col = slab * pencil_count + pencil
    rows = sent.shape[2]
    columns = sent.shape[3]
    per_block = 2 * INNER // columns
    row_blocks = row_high.shape[0]
    col_blocks = col_high.shape[0]
    chunk = potential.shape[2]
    per_part = INNER // rows
    row_parts = 2 * row_blocks
    col_parts = 2 * col_blocks
    step = 8

    pairs = (
        (row_high_in, row_high),
        (row_low_in, row_low),
        (colt_high_in, colt_high),
        (colt_low_in, colt_low),
        (col_high_in, col_high),
        (col_low_in, col_low),
    )
    tables_in = [
        pltpu.make_async_copy(source, target, table_sem.at[i])
        for i, (source, target) in enumerate(pairs)
    ]
    for copy in tables_in:
        copy.start()

    def partner(i):
        return lax.rem(pencil + lax.rem(i, pencil_count), pencil_count), lax.rem(
            slab + i // pencil_count, slab_count
        )

    halo[...] = jnp.zeros(halo.shape, jnp.float32)
    barrier = pltpu.get_barrier_semaphore()

    @pl.loop(1, device_count)
    def _(i):
        to_pencil, to_slab = partner(i)
        pl.semaphore_signal(
            barrier,
            inc=1,
            device_id={"slab": to_slab, "pencil": to_pencil},
            device_id_type=pl.DeviceIdType.MESH,
        )

    pl.semaphore_wait(barrier, device_count - 1)

    def remote(source, target, index, to_slab, to_pencil):
        return pltpu.make_async_remote_copy(
            src_ref=source,
            dst_ref=target,
            send_sem=send_sem.at[index],
            recv_sem=recv_sem.at[index],
            device_id={"slab": to_slab, "pencil": to_pencil},
            device_id_type=pl.DeviceIdType.MESH,
        )

    def start_to_columns(n, to):
        @pl.when(to != own_col)
        def _():
            remote(
                sent.at[n, to], held.at[n, own], n, to // pencil_count, lax.rem(to, pencil_count)
            ).start()

    def start_to_rows(n, to):
        @pl.when(to != own)
        def _():
            remote(
                sent.at[n, to], held.at[n, own_col], n, lax.rem(to, slab_count), to // slab_count
            ).start()

    def send(n, first, last):
        @pl.loop(first, last)
        def _(i):
            to_pencil, to_slab = partner(i)
            to = to_pencil * slab_count + to_slab
            remote(sent.at[n, to], held.at[n, own_col], n, to_slab, to_pencil).start()

    def all_of(n):
        others = pl.ds(0, device_count - 1)
        return remote(sent.at[n, others], held.at[n, others], n, slab, pencil)

    def send_slab(source_of, target, n):
        for i in range(1, slab_count):
            to = lax.rem(slab + i, slab_count)
            remote(source_of(to), target.at[slab], n, to, pencil).start()

    def all_of_slab(target, n):
        others = target.at[pl.ds(0, slab_count - 1)]
        return remote(others, others, n, slab, pencil)

    fields = sent.shape[0]

    def tile_rows(ref):
        return lambda to: ref.at[pl.ds(pl.multiple_of(to * rows, rows), rows)]

    own_rows = pl.ds(pl.multiple_of(slab * rows, rows), rows)
    send_slab(tile_rows(potential_ref), potential, fields)
    send_slab(tile_rows(eta_ref), eta, fields + 1)
    potential[slab] = potential_ref[own_rows]
    eta[slab] = eta_ref[own_rows]

    def part_of(ref, part, at):
        start = part * INNER % chunk
        return ref.at[part * INNER // chunk, at, pl.ds(start, INNER)]

    def piece_of(piece, at):
        return stage_rows.at[piece // 2, at, pl.ds(piece % 2 * INNER, INNER)]

    def over_rows(body):
        @pl.loop(0, rows // step)
        def _(i):
            body(pl.ds(pl.multiple_of(i * step, step), step))

    def begin_rows(parts, at):
        for piece, value in enumerate(outer_dft(parts)):
            piece_of(piece, at)[...] = value

    def finish_rows(n):
        @pl.loop(0, row_blocks, unroll=2)
        def _(i):
            b = lax.rem(i + own_col // per_block, row_blocks)
            result = row_product(stage_rows[b], row_high, row_low, b, 0)
            for i in range(per_block):
                sent[n, b * per_block + i] = result[:, i * columns : (i + 1) * columns]
                start_to_columns(n, b * per_block + i)

        held[n, own] = sent[n, own_col]

    def inverse_rows(n, use):
        if n in (2, 3, 6, 8):
            all_of(n).wait_recv()

        @pl.loop(0, row_blocks, unroll=2)
        def _(b):
            values = jnp.concatenate(
                [held[n, b * per_block + i] for i in range(per_block)], axis=1
            )
            stage_rows[b] = row_product(values, row_high, row_low, b, 1)

        def body(at):
            use(at, outer_dft_transposed([piece_of(p, at)[...] for p in range(row_parts)]))

        over_rows(body)

    def over_columns(body):
        @pl.loop(0, 2 * per_part)
        def _(i):
            body(i // 2, pl.multiple_of(lax.rem(i, 2) * (rows // 2), rows // 2))

    def forward_columns(n):
        if n == 0:
            all_of(n).wait_recv()

        def body(q, start):
            parts = [held[n, p * per_part + q, pl.ds(start, rows // 2)] for p in range(col_parts)]
            for piece, value in enumerate(outer_dft(parts)):
                at = pl.multiple_of(piece % 2 * INNER + q * rows + start, rows // 2)
                stage_cols[piece // 2, pl.ds(at, rows // 2)] = value

        over_columns(body)

        @pl.loop(0, col_blocks, unroll=2)
        def _(b):
            spectrum[b] = column_product(stage_cols[b], colt_high, colt_low, b)

    def inverse_columns(n, now):
        @pl.loop(0, col_blocks, unroll=2)
        def _(b):
            values = spectrum[b] * magnitude[b]
            spectrum[b] = values
            stage_cols[b] = column_product(values, col_high, col_low, b)

        @pl.loop(0, per_part)
        def _(i):
            q = lax.rem(i + own, per_part)
            for half in range(2):
                offset = half * (rows // 2)
                pieces = []
                for piece in range(col_parts):
                    at = pl.multiple_of(piece % 2 * INNER + q * rows + offset, rows // 2)
                    pieces.append(stage_cols[piece // 2, pl.ds(at, rows // 2)])
                for p, value in enumerate(outer_dft_transposed(pieces)):
                    sent[n, p * per_part + q, pl.ds(offset, rows // 2)] = value * (
                        1.0 / (NXW * NYW)
                    )
            if now:
                for p in range(col_parts):
                    start_to_rows(n, p * per_part + q)

        held[n, own_col] = sent[n, own]

    capacity = points_ref.shape[1]
    block_x, block_y, depth_cells = velocity_ref.shape[1:]
    tile_rows_count, tile_cols = eta_ref.shape
    cells = (block_x, block_y, depth_cells)

    def position(axis):
        return lax.broadcasted_iota(jnp.int32, cells, axis)

    links = (
        (slab < slab_count - 1, slab + 1, pencil, slab > 0),
        (slab > 0, slab - 1, pencil, slab < slab_count - 1),
        (pencil < pencil_count - 1, slab, pencil + 1, pencil > 0),
        (pencil > 0, slab, pencil - 1, pencil < pencil_count - 1),
    )

    def halo_copy(k, side, to_slab, to_pencil):
        return pltpu.make_async_remote_copy(
            src_ref=packed.at[k, side],
            dst_ref=halo.at[k, side],
            send_sem=halo_send.at[4 * k + side],
            recv_sem=halo_recv.at[4 * k + side],
            device_id={"slab": to_slab, "pencil": to_pencil},
            device_id_type=pl.DeviceIdType.MESH,
        )

    def send_halo(k, velocity):
        for c in range(3):
            packed[k, 0, c] = velocity[c][block_x - 1]
            packed[k, 1, c] = velocity[c][0]
            packed[k, 2, c] = velocity[c][:, block_y - 1]
            packed[k, 3, c] = velocity[c][:, 0]
        for side, (sends, to_slab, to_pencil, _) in enumerate(links):

            @pl.when(sends)
            def _(side=side, to_slab=to_slab, to_pencil=to_pencil):
                halo_copy(k, side, to_slab, to_pencil).start()

    def wait_halo(k):
        for side, (_, _, _, receives) in enumerate(links):

            @pl.when(receives)
            def _(side=side):
                halo_copy(k, side, slab, pencil).wait_recv()

    def end_halo(k):
        for side, (sends, _, _, _) in enumerate(links):

            @pl.when(sends)
            def _(side=side):
                halo_copy(k, side, slab, pencil).wait_send()

    def predicted(k, velocity):
        result = []
        for c in range(3):
            here = velocity[c]
            minus_x = jnp.concatenate([halo[k, 0, c][None], here[:-1]], axis=0)
            plus_x = jnp.concatenate([here[1:], halo[k, 1, c][None]], axis=0)
            minus_y = jnp.where(
                position(1) == 0, halo[k, 2, c][:, None], pltpu.roll(here, 1, 1)
            )
            plus_y = jnp.where(
                position(1) == block_y - 1,
                halo[k, 3, c][:, None],
                pltpu.roll(here, block_y - 1, 1),
            )
            minus_z = jnp.where(position(2) == 0, 0.0, pltpu.roll(here, 1, 2))
            plus_z = jnp.where(
                position(2) == depth_cells - 1, 0.0, pltpu.roll(here, depth_cells - 1, 2)
            )
            laplace = (
                plus_x + minus_x + (plus_y + minus_y) + (plus_z + minus_z) - 6.0 * here
            )
            advect = (
                velocity[0] * (plus_x - minus_x)
                + velocity[1] * (plus_y - minus_y)
                + velocity[2] * (plus_z - minus_z)
            )
            result.append(here + TIME_STEP * (VISCOSITY * laplace - 0.5 * advect))
        return result

    def split_tile(ref):
        @pl.loop(0, slab_count)
        def _(i):
            at = pl.multiple_of(i * rows, rows)
            high, low = split(ref[pl.ds(at, rows)])
            tile_split[pl.ds(at, rows)] = high
            tile_split[pl.ds(pl.multiple_of(tile_rows_count + at, rows), rows)] = low

    def pick(d):
        both = jnp.dot(tile_split[...], pick_cols[d], preferred_element_type=jnp.float32)
        row = lax.broadcasted_iota(jnp.int32, (tile_rows_count, capacity), 0)
        slot = lax.broadcasted_iota(jnp.int32, (1, capacity), 1)
        live = slot < counts_ref[pl.ds(d, 1)]
        wanted = jnp.where(live, points_ref[pl.ds(d, 1)] // tile_cols, -1)
        found = both[:tile_rows_count] + both[tile_rows_count:]
        return jnp.sum(jnp.where(row == wanted, found, 0.0), axis=0, keepdims=True)

    list_row = lax.broadcasted_iota(jnp.int32, (8, capacity), 0)

    def prepare_flow():
        split_tile(eta_ref)
        mixing_in = mixing_ref[...]
        points_each = mixing_in.shape[0] // 2
        weights = [mixing_in[points_each + q][None] for q in range(points_each)]
        shares = [weight / sum(weights[1:], weights[0]) for weight in weights]
        slots = [mixing_in[q][None].astype(jnp.int32) for q in range(points_each)]

        @pl.loop(0, slab_count)
        def _(d):
            column = lax.broadcasted_iota(jnp.int32, (tile_cols, capacity), 0)
            chosen = jnp.where(column == points_ref[pl.ds(d, 1)] % tile_cols, 1.0, 0.0)
            pick_cols[d] = chosen.astype(jnp.bfloat16)
            slot = lax.broadcasted_iota(jnp.int32, (capacity, block_x * block_y), 0) + d * capacity
            mixing = jnp.zeros(slot.shape, jnp.float32)
            for q in range(points_each):
                mixing = mixing + jnp.where(slot == slots[q], shares[q], 0.0)
            mix_high[d], mix_low[d] = split(mixing)

        @pl.loop(0, slab_count)
        def _(d):
            picks[d] = jnp.where(list_row == 0, pick(d), 0.0)

        wait_halo(0)
        for c, value in enumerate(predicted(0, [velocity_ref[c] for c in range(3)])):
            flow[c] = value

    def finish_flow():
        split_tile(out_ref)

        @pl.loop(1, slab_count + 1)
        def _(i):
            d = lax.rem(slab + i, slab_count)
            picks[d] = jnp.where(list_row == 1, pick(d), picks[d])

            @pl.when(i < slab_count)
            def _():
                remote(picks.at[d], arrived.at[slab], fields + 3, d, pencil).start()

        arrived[slab] = picks[slab]
        all_of_slab(arrived, fields + 3).wait_recv()
        surface = jnp.zeros((8, block_x * block_y), jnp.float32)
        for r in range(slab_count):
            high, low = split(arrived[r])
            surface += jnp.dot(high, mix_high[r], preferred_element_type=jnp.float32) + (
                jnp.dot(low, mix_high[r], preferred_element_type=jnp.float32)
                + jnp.dot(high, mix_low[r], preferred_element_type=jnp.float32)
            )
        turned = surface.T
        level = position(2).astype(jnp.float32)
        decay = jnp.exp(-DEPTH_RATE * (depth_cells - 1.0 - level) / depth_cells)

        def target(c):
            spread = jnp.broadcast_to(turned[:, c : c + 1], (block_x * block_y, depth_cells))
            return spread.reshape(cells) * decay

        targets = [target(0), None, target(1)]
        pos_x = (slab * block_x + position(0)).astype(jnp.float32)
        pos_y = (pencil * block_y + position(1)).astype(jnp.float32)
        reach_x = float(max(1, slab_count // 16) * block_x)
        total_x, total_y = float(block_x * slab_count), float(block_y * pencil_count)
        relax = jnp.maximum(
            jnp.maximum(ramp_weight(pos_x, reach_x), ramp_weight(total_x - 1.0 - pos_x, reach_x)),
            jnp.maximum(
                ramp_weight(pos_y, float(block_y)),
                ramp_weight(total_y - 1.0 - pos_y, float(block_y)),
            ),
        )

        def blend(values):
            blended = [(1.0 - relax) * value for value in values]
            return [
                value if aim is None else value + relax * aim
                for value, aim in zip(blended, targets)
            ]

        velocity = blend([flow[c] for c in range(3)])
        send_halo(1, velocity)
        wait_halo(1)
        for c, value in enumerate(blend(predicted(1, velocity))):
            velocity_out[c] = value
        end_halo(0)
        end_halo(1)
        all_of_slab(arrived, fields + 3).wait_send()

    send_halo(0, [velocity_ref[c] for c in range(3)])

    outer_x, outer_y = row_parts, col_parts
    lane = own_col * columns + lax.broadcasted_iota(jnp.int32, (2 * INNER, columns), 1)

    def wave(index, block, outer, length):
        first = jnp.where(
            index < INNER,
            jnp.where(block == 0, 0, block),
            jnp.where(block == 0, outer // 2, outer - block),
        )
        freq = first + outer * (index % INNER)
        folded = jnp.minimum(freq, length - freq).astype(jnp.float32)
        return 2.0 * math.pi / length * folded

    wave_x = wave(lane % (2 * INNER), lane // (2 * INNER), outer_x, NXW)
    place = lax.broadcasted_iota(jnp.int32, (2 * INNER, columns), 0)
    for b in range(col_blocks):
        wave_y = wave(place, jnp.full(place.shape, b, jnp.int32), outer_y, NYW)
        magnitude[b] = jnp.sqrt(wave_x * wave_x + wave_y * wave_y)

    all_of_slab(potential, fields).wait_recv()
    over_rows(
        lambda at: begin_rows([part_of(potential, p, at)[...] for p in range(row_parts)], at)
    )
    tables_in[0].wait()
    tables_in[1].wait()
    finish_rows(0)
    for copy in tables_in[2:]:
        copy.wait()

    prepare_flow()
    forward_columns(0)
    inverse_columns(1, True)
    inverse_columns(2, False)
    inverse_columns(3, False)
    all_of_slab(eta, fields + 1).wait_recv()

    def use_slope_one(at, parts):
        for p, value in enumerate(parts):
            part_of(total, p, at)[...] = value
        begin_rows([-part_of(eta, p, at)[...] * value for p, value in enumerate(parts)], at)

    def use_curve_one(at, parts):
        for p, value in enumerate(parts):
            height = part_of(eta, p, at)[...]
            term = height * value
            part_of(total, p, at)[...] += term
            part_of(curve, p, at)[...] = 0.5 * height * term

    def use_cubic_one(at, parts):
        for p, value in enumerate(parts):
            height = part_of(eta, p, at)[...]
            part_of(total, p, at)[...] += 0.5 * height * height * value

    def use_slope_two(at, parts):
        following = []
        for p, value in enumerate(parts):
            part_of(total, p, at)[...] += value
            following.append(-part_of(eta, p, at)[...] * value - part_of(curve, p, at)[...])
        begin_rows(following, at)

    def use_curve_two(at, parts):
        for p, value in enumerate(parts):
            part_of(total, p, at)[...] += part_of(eta, p, at)[...] * value

    def use_slope_three(at, parts):
        for p, value in enumerate(parts):
            part_of(total, p, at)[...] += value

    middle = device_count // 2
    all_of(1).wait_recv()
    send(2, 1, device_count)
    inverse_rows(1, use_slope_one)
    finish_rows(4)
    inverse_rows(2, use_curve_one)
    all_of(4).wait_recv()
    send(3, 1, middle)
    forward_columns(4)
    inverse_columns(5, True)
    inverse_columns(6, False)
    all_of(5).wait_recv()
    send(6, 1, device_count)
    inverse_rows(5, use_slope_two)
    finish_rows(7)
    inverse_rows(6, use_curve_two)
    all_of(7).wait_recv()
    send(3, middle, device_count)
    forward_columns(7)
    inverse_columns(8, True)
    inverse_rows(3, use_cubic_one)
    inverse_rows(8, use_slope_three)

    send_slab(lambda to: total.at[to], back, fields + 2)
    out_ref[own_rows] = total[slab]
    all_of_slab(back, fields + 2).wait_recv()
    for i in range(1, slab_count):
        source = lax.rem(slab + i, slab_count)
        out_ref[pl.ds(pl.multiple_of(source * rows, rows), rows)] = back[source]
    finish_flow()
    for n in range(fields):
        all_of(n).wait_send()
    all_of_slab(potential, fields).wait_send()
    all_of_slab(eta, fields + 1).wait_send()
    all_of_slab(back, fields + 2).wait_send()


def two_terms(table):
    high = table.astype(jnp.bfloat16)
    low = (table - high.astype(np.float32)).astype(jnp.bfloat16)
    return jnp.asarray(high), jnp.asarray(low)


def whole_step(
    potential, eta, velocity, points, counts, stencil, interp_weight, slab_count, pencil_count
):
    tile_rows, tile_cols = eta.shape
    device_count = slab_count * pencil_count
    rows, columns = NYW // device_count, NXW // device_count
    row_table, _ = tables(NXW)
    col_table, _ = tables(NYW)
    constants = [
        *two_terms(row_table),
        *two_terms(col_table),
        *two_terms(np.ascontiguousarray(col_table.transpose(0, 2, 1))),
    ]
    capacity = points.shape[1]
    block_x, block_y, _ = velocity.shape[1:]
    mixing = jnp.concatenate([stencil.astype(jnp.float32), interp_weight])
    mixing = mixing.reshape(-1, block_x * block_y)
    spectrum = (col_table.shape[0], 2 * INNER, columns)
    list_shape = (slab_count, 8, capacity)
    halo_shape = (STEPS, 4, 3, block_x, velocity.shape[3])
    fields = 9
    strip = pltpu.VMEM((slab_count, rows, tile_cols), jnp.float32)
    vmem = pl.BlockSpec(memory_space=pltpu.VMEM)
    return pl.pallas_call(
        lambda *refs: surface_kernel(slab_count, pencil_count, *refs),
        out_shape=(
            jax.ShapeDtypeStruct((tile_rows, tile_cols), jnp.float32),
            jax.ShapeDtypeStruct(velocity.shape, jnp.float32),
        ),
        in_specs=[vmem] * 6 + [pl.BlockSpec(memory_space=pl.ANY)] * 6,
        out_specs=(vmem, vmem),
        scratch_shapes=[
            *(pltpu.VMEM(table.shape, jnp.bfloat16) for table in constants),
            *([strip] * 5),
            pltpu.VMEM(row_table.shape[:1] + (rows, 2 * INNER), jnp.float32),
            pltpu.VMEM(spectrum, jnp.float32),
            pltpu.VMEM(spectrum, jnp.float32),
            pltpu.VMEM(spectrum, jnp.float32),
            pltpu.VMEM((fields, device_count, rows, columns), jnp.float32),
            pltpu.VMEM((fields, device_count, rows, columns), jnp.float32),
            pltpu.VMEM((2 * tile_rows, tile_cols), jnp.bfloat16),
            pltpu.VMEM((slab_count, tile_cols, capacity), jnp.bfloat16),
            pltpu.VMEM((slab_count, capacity, block_x * block_y), jnp.bfloat16),
            pltpu.VMEM((slab_count, capacity, block_x * block_y), jnp.bfloat16),
            pltpu.VMEM(list_shape, jnp.float32),
            pltpu.VMEM(list_shape, jnp.float32),
            pltpu.VMEM(velocity.shape, jnp.float32),
            pltpu.VMEM(halo_shape, jnp.float32),
            pltpu.VMEM(halo_shape, jnp.float32),
            pltpu.SemaphoreType.DMA((6,)),
            pltpu.SemaphoreType.DMA((fields + 4,)),
            pltpu.SemaphoreType.DMA((fields + 4,)),
            pltpu.SemaphoreType.DMA((4 * STEPS,)),
            pltpu.SemaphoreType.DMA((4 * STEPS,)),
        ],
        compiler_params=pltpu.CompilerParams(
            collective_id=0, has_side_effects=True, vmem_limit_bytes=60 * 1024 * 1024
        ),
    )(
        potential,
        eta,
        velocity,
        points,
        counts[:, None],
        mixing,
        *constants,
    )


def surface_plain(potential, eta, magnitude, row_table, column_table, slab_count):
    tile_rows, tile_cols = eta.shape
    columns = magnitude.shape[-1]
    device_count = NXW // columns
    rows = NYW // device_count
    row_blocks, column_blocks = jnp.asarray(row_table), jnp.asarray(column_table)
    both = jnp.stack([potential, eta]).reshape(2, slab_count, rows, tile_cols)
    both = lax.all_to_all(both, "slab", split_axis=1, concat_axis=1, tiled=True)
    both = both.transpose(0, 2, 1, 3).reshape(2, rows, NXW)
    potential, eta = both[0], both[1]
    first_mult = magnitude * (1.0 / (NXW * NYW))
    second_mult = magnitude * first_mult
    third_mult = magnitude * second_mult

    def forward(field):
        arrived = exchange(rows_forward(field, row_blocks, device_count))
        return columns_forward(arrived.reshape(NYW, columns), column_blocks)

    def inverse(spectrum):
        field = columns_inverse(spectrum, column_blocks)
        return rows_inverse(exchange(field.reshape(device_count, rows, columns)), row_blocks)

    spectrum = forward(potential)
    slope_one = inverse(spectrum * first_mult)
    curve_one = inverse(spectrum * second_mult)
    cubic_one = inverse(spectrum * third_mult)
    spectrum = forward(-eta * slope_one)
    slope_two = inverse(spectrum * first_mult)
    curve_two = inverse(spectrum * second_mult)
    spectrum = forward(-eta * slope_two - 0.5 * eta * eta * curve_one)
    slope_three = inverse(spectrum * first_mult)
    vertical = (
        slope_one
        + slope_two
        + eta * curve_one
        + slope_three
        + eta * curve_two
        + 0.5 * eta * eta * cubic_one
    )
    vertical = vertical.reshape(rows, slab_count, tile_cols).transpose(1, 0, 2)
    vertical = lax.all_to_all(vertical, "slab", split_axis=0, concat_axis=0, tiled=True)
    vertical = vertical.reshape(tile_rows, tile_cols)

    return vertical


def ramp_weight(distance, reach_len):
    ratio = jnp.clip(1.0 - distance / reach_len, 0.0, 1.0)
    return ratio * ratio


def blend_weight(pos_x, pos_y, total_x, total_y, reach_x, reach_y):
    along_x = jnp.maximum(ramp_weight(pos_x, reach_x), ramp_weight(total_x - 1.0 - pos_x, reach_x))
    across = jnp.maximum(ramp_weight(pos_y, reach_y), ramp_weight(total_y - 1.0 - pos_y, reach_y))
    return jnp.maximum(along_x[:, None], across[None, :])[:, :, None]


def neighbours(shard, axis, dim):
    size, length = lax.axis_size(axis), shard.shape[dim]
    up = [(i, i + 1) for i in range(size - 1)]
    down = [(i + 1, i) for i in range(size - 1)]
    before = lax.ppermute(lax.slice_in_dim(shard, length - 1, length, axis=dim), axis, up)
    after = lax.ppermute(lax.slice_in_dim(shard, 0, 1, axis=dim), axis, down)
    minus = jnp.concatenate([before, lax.slice_in_dim(shard, 0, length - 1, axis=dim)], axis=dim)
    plus = jnp.concatenate([lax.slice_in_dim(shard, 1, length, axis=dim), after], axis=dim)
    return minus, plus


def predict(velocity):
    minus_x, plus_x = neighbours(velocity, "slab", 1)
    minus_y, plus_y = neighbours(velocity, "pencil", 2)
    padded = jnp.pad(velocity, ((0, 0), (0, 0), (0, 0), (1, 1)))
    minus_z, plus_z = padded[..., :-2], padded[..., 2:]
    laplace = plus_x + minus_x + (plus_y + minus_y) + (plus_z + minus_z) - 6.0 * velocity
    advect = (
        velocity[0] * (plus_x - minus_x)
        + velocity[1] * (plus_y - minus_y)
        + velocity[2] * (plus_z - minus_z)
    )
    return velocity + TIME_STEP * (VISCOSITY * laplace - 0.5 * advect)


def on_device(
    surface_eta, surface_potential, velocity, send_point, send_count, stencil, interp_weight
):
    slab_count = lax.axis_size("slab")
    pencil_count = lax.axis_size("pencil")
    device_count = slab_count * pencil_count
    slab_index = lax.axis_index("slab")
    pencil_index = lax.axis_index("pencil")
    tile_rows, tile_cols = surface_eta.shape
    rows = NYW // device_count
    columns = NXW // device_count
    if (
        columns % 128 == 0
        and rows % 16 == 0
        and INNER % rows == 0
        and velocity.shape[1] == velocity.shape[2]
        and STEPS == 2
    ):
        return whole_step(
            surface_potential,
            surface_eta,
            velocity,
            send_point[0, 0],
            send_count[0, 0],
            stencil,
            interp_weight,
            slab_count,
            pencil_count,
        )
    own = pencil_index * slab_count + slab_index
    row_table, row_order = tables(NXW)
    column_table, column_order = tables(NYW)
    wave_x = 2.0 * math.pi / NXW * jnp.asarray(row_order.reshape(-1)).astype(jnp.float32)
    wave_x = lax.dynamic_slice(wave_x, (own * columns,), (columns,))
    wave_y = 2.0 * math.pi / NYW * jnp.asarray(column_order).astype(jnp.float32)[:, :, None]
    magnitude = jnp.sqrt(wave_x * wave_x + wave_y * wave_y)
    vertical = surface_plain(
        surface_potential, surface_eta, magnitude, row_table, column_table, slab_count
    )

    points = send_point[0, 0]
    capacity = points.shape[1]
    counts = send_count[0, 0]
    flat_points = points.reshape(-1)
    live = (jnp.arange(capacity, dtype=jnp.int32)[None, :] < counts[:, None]).reshape(-1)
    row_pick = (
        (flat_points // tile_cols)[:, None] == jnp.arange(tile_rows, dtype=jnp.int32)[None, :]
    ).astype(jnp.float32)
    column_pick = (flat_points % tile_cols)[:, None] == jnp.arange(tile_cols, dtype=jnp.int32)[
        None, :
    ]
    column_pick = column_pick & live[:, None]

    def pick(tile):
        picked_rows = jnp.dot(row_pick, tile, precision=HIGH)
        return jnp.sum(jnp.where(column_pick, picked_rows, 0.0), axis=1)

    picked = jnp.stack([pick(surface_eta), pick(vertical)]).reshape(2, slab_count, capacity)
    arrived = lax.all_to_all(picked, "slab", split_axis=1, concat_axis=1, tiled=True).reshape(
        2, slab_count * capacity
    )
    block_x, block_y, depth_cells = velocity.shape[1:]
    shares = interp_weight / jnp.sum(interp_weight, axis=0)
    slots = jnp.arange(slab_count * capacity, dtype=jnp.int32)[:, None]
    mixing = 0.0
    for q in range(stencil.shape[0]):
        mixing = mixing + jnp.where(
            slots == stencil[q].reshape(1, -1), shares[q].reshape(1, -1), 0.0
        )
    surface_at = jnp.dot(arrived, mixing, precision=lax.Precision.HIGHEST)
    surface_at = surface_at.reshape(2, block_x, block_y)

    zone_slabs = max(1, slab_count // 16)
    pos_x = (slab_index * block_x + jnp.arange(block_x, dtype=jnp.int32)).astype(jnp.float32)
    pos_y = (pencil_index * block_y + jnp.arange(block_y, dtype=jnp.int32)).astype(jnp.float32)
    relax_weight = blend_weight(
        pos_x,
        pos_y,
        float(block_x * slab_count),
        float(block_y * pencil_count),
        float(zone_slabs * block_x),
        float(block_y),
    )
    levels = jnp.arange(depth_cells, dtype=jnp.float32)
    depth_decay = jnp.exp(-DEPTH_RATE * (depth_cells - 1.0 - levels) / depth_cells)
    target = jnp.stack(
        [
            surface_at[0][:, :, None] * depth_decay,
            jnp.zeros((block_x, block_y, depth_cells), jnp.float32),
            surface_at[1][:, :, None] * depth_decay,
        ]
    )
    for substep in range(STEPS):
        velocity = (1.0 - relax_weight) * predict(velocity) + relax_weight * target
    return (vertical, velocity)


def solution(mesh):
    in_specs = (
        P("pencil", "slab"),
        P("pencil", "slab"),
        P(None, "slab", "pencil", None),
        P("slab", "pencil", None, None),
        P("slab", "pencil", None),
        P(None, "slab", "pencil"),
        P(None, "slab", "pencil"),
    )
    out_specs = (P("pencil", "slab"), P(None, "slab", "pencil", None))
    return jax.shard_map(
        on_device, mesh=mesh, in_specs=in_specs, out_specs=out_specs, check_vma=False
    )
```

```python
import math

import jax
import jax.numpy as jnp
import numpy as np
from jax import lax
from jax.experimental import pallas as pl
from jax.experimental.pallas import tpu as pltpu
from jax.sharding import PartitionSpec as P

NXW = 4096
NYW = 2048
STEPS = 2
INNER = 256


TIME_STEP = 0.2
VISCOSITY = 0.6
DEPTH_RATE = 3.0

HIGH = lax.Precision.HIGH
BOTH = ("pencil", "slab")


def real_dft(parts):
    size = len(parts)
    if size == 2:
        return [(parts[0] + parts[1], None), (parts[0] - parts[1], None)]
    even = real_dft(parts[0::2])
    odd = real_dft(parts[1::2])
    half = size // 2
    result = [None] * (half + 1)
    for k in range(size // 4 + 1):
        (even_re, even_im), (odd_re, odd_im) = even[k], odd[k]
        if k == 0:
            result[0] = (even_re + odd_re, None)
            result[half] = (even_re - odd_re, None)
        elif 4 * k == size:
            result[k] = (even_re, -odd_re)
        else:
            c, s = math.cos(2.0 * math.pi * k / size), math.sin(2.0 * math.pi * k / size)
            turned_re = c * odd_re + s * odd_im
            turned_im = c * odd_im - s * odd_re
            result[k] = (even_re + turned_re, even_im + turned_im)
            result[half - k] = (even_re - turned_re, turned_im - even_im)
    return result


def outer_dft(parts):
    bins = real_dft(list(parts))
    out = [bins[0][0], bins[-1][0]]
    for re, im in bins[1:-1]:
        out += [re, im]
    return tuple(out)


def real_dft_transposed(bins):
    half = len(bins) - 1
    size = 2 * half
    if size == 2:
        return [bins[0][0] + bins[1][0], bins[0][0] - bins[1][0]]
    even, odd = [None] * (half // 2 + 1), [None] * (half // 2 + 1)
    for k in range(size // 4 + 1):
        re, im = bins[k]
        if k == 0:
            even[0] = (re + bins[half][0], None)
            odd[0] = (re - bins[half][0], None)
        elif 4 * k == size:
            even[k] = (re, None)
            odd[k] = (-im, None)
        else:
            other_re, other_im = bins[half - k]
            c, s = math.cos(2.0 * math.pi * k / size), math.sin(2.0 * math.pi * k / size)
            turned_re, turned_im = re - other_re, im + other_im
            even[k] = (re + other_re, im - other_im)
            odd[k] = (c * turned_re - s * turned_im, s * turned_re + c * turned_im)
    result = [None] * size
    result[0::2] = real_dft_transposed(even)
    result[1::2] = real_dft_transposed(odd)
    return result


def outer_dft_transposed(pieces):
    half = len(pieces) // 2
    bins = [(pieces[0], None)]
    bins += [(pieces[2 * k], pieces[2 * k + 1]) for k in range(1, half)]
    return real_dft_transposed(bins + [(pieces[1], None)])


def tables(length):
    outer = length // INNER
    within = np.arange(INNER)
    blocks = np.zeros((outer // 2, 2 * INNER, 2 * INNER), np.float64)
    order = np.zeros((outer // 2, 2 * INNER), np.int32)
    for b in range(outer // 2):
        for side in range(2):
            if b == 0:
                first = 0 if side == 0 else outer // 2
            else:
                first = b if side == 0 else outer - b
            freq = first + outer * within
            angle = 2.0 * math.pi / length * ((within[:, None] * freq[None, :]) % length)
            cos, sin = np.cos(angle), np.sin(angle)
            columns = slice(side * INNER, (side + 1) * INNER)
            order[b, columns] = freq
            if b == 0:
                blocks[b, columns, columns] = cos + sin
            else:
                sign = 1.0 if side == 0 else -1.0
                blocks[b, :INNER, columns] = cos + sin
                blocks[b, INNER:, columns] = sign * (sin - cos)
    return blocks.astype(np.float32), np.minimum(order, length - order)


def rows_forward(values, blocks, device_count):
    rows, length = values.shape
    pieces = outer_dft([values[:, i : i + INNER] for i in range(0, length, INNER)])
    stacked = jnp.stack(
        [jnp.concatenate(pieces[2 * b : 2 * b + 2], axis=1) for b in range(len(pieces) // 2)]
    )
    spectrum = jnp.einsum("brk,bkn->brn", stacked, blocks, precision=HIGH)
    columns = length // device_count
    spectrum = spectrum.reshape(spectrum.shape[0], rows, 2 * INNER // columns, columns)
    return spectrum.transpose(0, 2, 1, 3).reshape(device_count, rows, columns)


def rows_inverse(values, blocks):
    device_count, rows, columns = values.shape
    grouped = values.reshape(blocks.shape[0], 2 * INNER // columns, rows, columns)
    grouped = grouped.transpose(0, 2, 1, 3).reshape(blocks.shape[0], rows, 2 * INNER)
    stacked = jnp.einsum("brn,bkn->brk", grouped, blocks, precision=HIGH)
    pieces = []
    for b in range(blocks.shape[0]):
        pieces += [stacked[b, :, :INNER], stacked[b, :, INNER:]]
    return jnp.concatenate(outer_dft_transposed(pieces), axis=1)


def columns_forward(values, blocks):
    pieces = outer_dft([values[i : i + INNER] for i in range(0, values.shape[0], INNER)])
    stacked = jnp.concatenate(pieces, axis=0).reshape(
        blocks.shape[0], 2 * INNER, values.shape[1]
    )
    return jnp.einsum("bkn,bkc->bnc", blocks, stacked, precision=HIGH)


def columns_inverse(values, blocks):
    stacked = jnp.einsum("bkn,bnc->bkc", blocks, values, precision=HIGH)
    pieces = []
    for b in range(blocks.shape[0]):
        pieces += [stacked[b, :INNER], stacked[b, INNER:]]
    return jnp.concatenate(outer_dft_transposed(pieces), axis=0)


def exchange(values):
    return lax.all_to_all(values, BOTH, split_axis=0, concat_axis=0, tiled=True)


def split(values):
    high = values.astype(jnp.bfloat16)
    return high, (values - high.astype(jnp.float32)).astype(jnp.bfloat16)


def row_product(values, high_ref, low_ref, block, contract):
    rows = values.shape[0]
    high, low = split(values)
    dims = (((1,), (contract,)), ((), ()))
    main = lax.dot_general(
        jnp.concatenate([high, low], axis=0),
        high_ref[block],
        dims,
        preferred_element_type=jnp.float32,
    )
    rest = lax.dot_general(high, low_ref[block], dims, preferred_element_type=jnp.float32)
    return main[:rows] + (main[rows:] + rest)


def column_product(values, high_ref, low_ref, block):
    columns = values.shape[1]
    high, low = split(values)
    main = jnp.dot(
        high_ref[block],
        jnp.concatenate([high, low], axis=1),
        preferred_element_type=jnp.float32,
    )
    rest = jnp.dot(low_ref[block], high, preferred_element_type=jnp.float32)
    return main[:, :columns] + (main[:, columns:] + rest)


def surface_kernel(
    slab_count,
    pencil_count,
    potential_ref,
    eta_ref,
    velocity_ref,
    points_ref,
    counts_ref,
    mixing_ref,
    row_high_in,
    row_low_in,
    col_high_in,
    col_low_in,
    colt_high_in,
    colt_low_in,
    out_ref,
    velocity_out,
    row_high,
    row_low,
    col_high,
    col_low,
    colt_high,
    colt_low,
    potential,
    eta,
    back,
    total,
    curve,
    stage_rows,
    stage_cols,
    spectrum,
    magnitude,
    sent,
    held,
    tile_split,
    pick_cols,
    mix_high,
    mix_low,
    picks,
    arrived,
    flow,
    packed,
    halo,
    table_sem,
    send_sem,
    recv_sem,
    halo_send,
    halo_recv,
):
    slab = lax.axis_index("slab")
    pencil = lax.axis_index("pencil")
    device_count = slab_count * pencil_count
    own = pencil * slab_count + slab
    own_col = slab * pencil_count + pencil
    rows = sent.shape[2]
    columns = sent.shape[3]
    per_block = 2 * INNER // columns
    row_blocks = row_high.shape[0]
    col_blocks = col_high.shape[0]
    chunk = potential.shape[2]
    per_part = INNER // rows
    row_parts = 2 * row_blocks
    col_parts = 2 * col_blocks
    step = 8

    pairs = (
        (row_high_in, row_high),
        (row_low_in, row_low),
        (colt_high_in, colt_high),
        (colt_low_in, colt_low),
        (col_high_in, col_high),
        (col_low_in, col_low),
    )
    tables_in = [
        pltpu.make_async_copy(source, target, table_sem.at[i])
        for i, (source, target) in enumerate(pairs)
    ]
    for copy in tables_in:
        copy.start()

    def partner(i):
        return lax.rem(pencil + lax.rem(i, pencil_count), pencil_count), lax.rem(
            slab + i // pencil_count, slab_count
        )

    halo[...] = jnp.zeros(halo.shape, jnp.float32)
    barrier = pltpu.get_barrier_semaphore()

    @pl.loop(1, device_count)
    def _(i):
        to_pencil, to_slab = partner(i)
        pl.semaphore_signal(
            barrier,
            inc=1,
            device_id={"slab": to_slab, "pencil": to_pencil},
            device_id_type=pl.DeviceIdType.MESH,
        )

    pl.semaphore_wait(barrier, device_count - 1)

    def remote(source, target, index, to_slab, to_pencil):
        return pltpu.make_async_remote_copy(
            src_ref=source,
            dst_ref=target,
            send_sem=send_sem.at[index],
            recv_sem=recv_sem.at[index],
            device_id={"slab": to_slab, "pencil": to_pencil},
            device_id_type=pl.DeviceIdType.MESH,
        )

    def start_to_columns(n, to):
        @pl.when(to != own_col)
        def _():
            remote(
                sent.at[n, to], held.at[n, own], n, to // pencil_count, lax.rem(to, pencil_count)
            ).start()

    def start_to_rows(n, to):
        @pl.when(to != own)
        def _():
            remote(
                sent.at[n, to], held.at[n, own_col], n, lax.rem(to, slab_count), to // slab_count
            ).start()

    def send(n, first, last):
        @pl.loop(first, last)
        def _(i):
            to_pencil, to_slab = partner(i)
            to = to_pencil * slab_count + to_slab
            remote(sent.at[n, to], held.at[n, own_col], n, to_slab, to_pencil).start()

    def all_of(n):
        others = pl.ds(0, device_count - 1)
        return remote(sent.at[n, others], held.at[n, others], n, slab, pencil)

    def send_slab(source_of, target, n):
        for i in range(1, slab_count):
            to = lax.rem(slab + i, slab_count)
            remote(source_of(to), target.at[slab], n, to, pencil).start()

    def all_of_slab(target, n):
        others = target.at[pl.ds(0, slab_count - 1)]
        return remote(others, others, n, slab, pencil)

    fields = sent.shape[0]
    half_rows = rows // 2
    halves = (pl.ds(0, half_rows), pl.ds(half_rows, half_rows))
    potential_sems = (fields, fields + 4)
    first_sems = (0, fields + 5)
    last_sems = (8, fields + 6)
    back_sems = (fields + 2, fields + 7)

    def tile_rows(ref, half=None):
        if half is None:
            return lambda to: ref.at[pl.ds(pl.multiple_of(to * rows, rows), rows)]
        return lambda to: ref.at[
            pl.ds(pl.multiple_of(to * rows + half * half_rows, half_rows), half_rows)
        ]

    def send_slab_half(source_of, target, half, sems):
        for i in range(1, slab_count):
            to = lax.rem(slab + i, slab_count)
            remote(
                source_of(to), target.at[slab, halves[half]], sems[half], to, pencil
            ).start()

    def all_of_slab_half(target, half, sems):
        others = target.at[pl.ds(0, slab_count - 1), halves[half]]
        return remote(others, others, sems[half], slab, pencil)

    def all_of_half(n, half, sems):
        others = pl.ds(0, device_count - 1)
        return remote(
            sent.at[n, others, halves[half]],
            held.at[n, others, halves[half]],
            sems[half],
            slab,
            pencil,
        )

    own_rows = pl.ds(pl.multiple_of(slab * rows, rows), rows)
    send_slab_half(tile_rows(potential_ref, 0), potential, 0, potential_sems)
    potential[slab] = potential_ref[own_rows]
    eta[slab] = eta_ref[own_rows]

    def part_of(ref, part, at):
        start = part * INNER % chunk
        return ref.at[part * INNER // chunk, at, pl.ds(start, INNER)]

    def piece_of(piece, at):
        return stage_rows.at[piece // 2, at, pl.ds(piece % 2 * INNER, INNER)]

    def over_rows(body, half=None):
        start = 0 if half is None else half * half_rows
        stop = rows if half is None else start + half_rows

        @pl.loop(start // step, stop // step)
        def _(i):
            body(pl.ds(pl.multiple_of(i * step, step), step))

    def begin_rows(parts, at):
        for piece, value in enumerate(outer_dft(parts)):
            piece_of(piece, at)[...] = value

    def finish_rows(n):
        @pl.loop(0, row_blocks)
        def _(i):
            b = lax.rem(i + own_col // per_block, row_blocks)
            result = row_product(stage_rows[b], row_high, row_low, b, 0)
            for i in range(per_block):
                sent[n, b * per_block + i] = result[:, i * columns : (i + 1) * columns]
                start_to_columns(n, b * per_block + i)

        held[n, own] = sent[n, own_col]

    def finish_rows_half(n, half, sems):
        part = halves[half]

        @pl.loop(0, row_blocks)
        def _(i):
            b = lax.rem(i + own_col // per_block, row_blocks)
            result = row_product(stage_rows[b, part], row_high, row_low, b, 0)
            for j in range(per_block):
                to = b * per_block + j
                sent[n, to, part] = result[:, j * columns : (j + 1) * columns]

                @pl.when(to != own_col)
                def _(to=to):
                    remote(
                        sent.at[n, to, part],
                        held.at[n, own, part],
                        sems[half],
                        to // pencil_count,
                        lax.rem(to, pencil_count),
                    ).start()

        held[n, own, part] = sent[n, own_col, part]

    def inverse_rows_half(n, use, half, sems):
        part = halves[half]
        all_of_half(n, half, sems).wait_recv()

        @pl.loop(0, row_blocks)
        def _(b):
            values = jnp.concatenate(
                [held[n, b * per_block + i, part] for i in range(per_block)], axis=1
            )
            stage_rows[b, part] = row_product(values, row_high, row_low, b, 1)

        def body(at):
            use(at, outer_dft_transposed([piece_of(p, at)[...] for p in range(row_parts)]))

        over_rows(body, half)

    def send_half_to_rows(n, half, sems):
        part = halves[half]

        @pl.loop(1, device_count)
        def _(i):
            to_pencil, to_slab = partner(i)
            to = to_pencil * slab_count + to_slab
            remote(
                sent.at[n, to, part], held.at[n, own_col, part], sems[half], to_slab, to_pencil
            ).start()

    def inverse_rows(n, use):
        if n in (2, 3, 6, 8):
            all_of(n).wait_recv()

        @pl.loop(0, row_blocks)
        def _(b):
            values = jnp.concatenate(
                [held[n, b * per_block + i] for i in range(per_block)], axis=1
            )
            stage_rows[b] = row_product(values, row_high, row_low, b, 1)

        def body(at):
            use(at, outer_dft_transposed([piece_of(p, at)[...] for p in range(row_parts)]))

        over_rows(body)

    def over_columns(body):
        @pl.loop(0, 2 * per_part)
        def _(i):
            body(i // 2, pl.multiple_of(lax.rem(i, 2) * (rows // 2), rows // 2))

    def forward_columns(n):
        def body(q, start):
            parts = [held[n, p * per_part + q, pl.ds(start, rows // 2)] for p in range(col_parts)]
            for piece, value in enumerate(outer_dft(parts)):
                at = pl.multiple_of(piece % 2 * INNER + q * rows + start, rows // 2)
                stage_cols[piece // 2, pl.ds(at, rows // 2)] = value

        over_columns(body)

        @pl.loop(0, col_blocks)
        def _(b):
            spectrum[b] = column_product(stage_cols[b], colt_high, colt_low, b)

    def inverse_columns(n, now):
        @pl.loop(0, col_blocks)
        def _(b):
            values = spectrum[b] * magnitude[b]
            spectrum[b] = values
            stage_cols[b] = column_product(values, col_high, col_low, b)

        @pl.loop(0, per_part)
        def _(i):
            q = lax.rem(i + own, per_part)
            for half in (0, 1):
                offset = half * (rows // 2)
                pieces = []
                for piece in range(col_parts):
                    at = pl.multiple_of(piece % 2 * INNER + q * rows + offset, rows // 2)
                    pieces.append(stage_cols[piece // 2, pl.ds(at, rows // 2)])
                for p, value in enumerate(outer_dft_transposed(pieces)):
                    sent[n, p * per_part + q, pl.ds(offset, rows // 2)] = value * (
                        1.0 / (NXW * NYW)
                    )
            if now:
                for p in range(col_parts):
                    start_to_rows(n, p * per_part + q)

        held[n, own_col] = sent[n, own]

    capacity = points_ref.shape[1]
    block_x, block_y, depth_cells = velocity_ref.shape[1:]
    tile_rows_count, tile_cols = eta_ref.shape
    cells = (block_x, block_y, depth_cells)

    def position(axis):
        return lax.broadcasted_iota(jnp.int32, cells, axis)

    links = (
        (slab < slab_count - 1, slab + 1, pencil, slab > 0),
        (slab > 0, slab - 1, pencil, slab < slab_count - 1),
        (pencil < pencil_count - 1, slab, pencil + 1, pencil > 0),
        (pencil > 0, slab, pencil - 1, pencil < pencil_count - 1),
    )

    def halo_copy(k, side, to_slab, to_pencil):
        return pltpu.make_async_remote_copy(
            src_ref=packed.at[k, side],
            dst_ref=halo.at[k, side],
            send_sem=halo_send.at[4 * k + side],
            recv_sem=halo_recv.at[4 * k + side],
            device_id={"slab": to_slab, "pencil": to_pencil},
            device_id_type=pl.DeviceIdType.MESH,
        )

    def send_halo(k, velocity):
        for c in range(3):
            packed[k, 0, c] = velocity[c][block_x - 1]
            packed[k, 1, c] = velocity[c][0]
            packed[k, 2, c] = velocity[c][:, block_y - 1]
            packed[k, 3, c] = velocity[c][:, 0]
        for side, (sends, to_slab, to_pencil, _) in enumerate(links):

            @pl.when(sends)
            def _(side=side, to_slab=to_slab, to_pencil=to_pencil):
                halo_copy(k, side, to_slab, to_pencil).start()

    def wait_halo(k):
        for side, (_, _, _, receives) in enumerate(links):

            @pl.when(receives)
            def _(side=side):
                halo_copy(k, side, slab, pencil).wait_recv()

    def end_halo(k):
        for side, (sends, _, _, _) in enumerate(links):

            @pl.when(sends)
            def _(side=side):
                halo_copy(k, side, slab, pencil).wait_send()

    def predicted(k, velocity):
        result = []
        for c in range(3):
            here = velocity[c]
            minus_x = jnp.concatenate([halo[k, 0, c][None], here[:-1]], axis=0)
            plus_x = jnp.concatenate([here[1:], halo[k, 1, c][None]], axis=0)
            minus_y = jnp.where(
                position(1) == 0, halo[k, 2, c][:, None], pltpu.roll(here, 1, 1)
            )
            plus_y = jnp.where(
                position(1) == block_y - 1,
                halo[k, 3, c][:, None],
                pltpu.roll(here, block_y - 1, 1),
            )
            minus_z = jnp.where(position(2) == 0, 0.0, pltpu.roll(here, 1, 2))
            plus_z = jnp.where(
                position(2) == depth_cells - 1, 0.0, pltpu.roll(here, depth_cells - 1, 2)
            )
            laplace = (
                plus_x + minus_x + (plus_y + minus_y) + (plus_z + minus_z) - 6.0 * here
            )
            advect = (
                velocity[0] * (plus_x - minus_x)
                + velocity[1] * (plus_y - minus_y)
                + velocity[2] * (plus_z - minus_z)
            )
            result.append(here + TIME_STEP * (VISCOSITY * laplace - 0.5 * advect))
        return result

    def split_tile(ref):
        @pl.loop(0, slab_count)
        def _(i):
            at = pl.multiple_of(i * rows, rows)
            high, low = split(ref[pl.ds(at, rows)])
            tile_split[pl.ds(at, rows)] = high
            tile_split[pl.ds(pl.multiple_of(tile_rows_count + at, rows), rows)] = low

    def pick(d):
        both = jnp.dot(tile_split[...], pick_cols[d], preferred_element_type=jnp.float32)
        row = lax.broadcasted_iota(jnp.int32, (tile_rows_count, capacity), 0)
        slot = lax.broadcasted_iota(jnp.int32, (1, capacity), 1)
        live = slot < counts_ref[pl.ds(d, 1)]
        wanted = jnp.where(live, points_ref[pl.ds(d, 1)] // tile_cols, -1)
        found = both[:tile_rows_count] + both[tile_rows_count:]
        return jnp.sum(jnp.where(row == wanted, found, 0.0), axis=0, keepdims=True)

    list_row = lax.broadcasted_iota(jnp.int32, (8, capacity), 0)

    def prepare_flow():
        split_tile(eta_ref)
        mixing_in = mixing_ref[...]
        points_each = mixing_in.shape[0] // 2
        weights = [mixing_in[points_each + q][None] for q in range(points_each)]
        shares = [weight / sum(weights[1:], weights[0]) for weight in weights]
        slots = [mixing_in[q][None].astype(jnp.int32) for q in range(points_each)]

        @pl.loop(0, slab_count)
        def _(d):
            column = lax.broadcasted_iota(jnp.int32, (tile_cols, capacity), 0)
            chosen = jnp.where(column == points_ref[pl.ds(d, 1)] % tile_cols, 1.0, 0.0)
            pick_cols[d] = chosen.astype(jnp.bfloat16)
            slot = lax.broadcasted_iota(jnp.int32, (capacity, block_x * block_y), 0) + d * capacity
            mixing = jnp.zeros(slot.shape, jnp.float32)
            for q in range(points_each):
                mixing = mixing + jnp.where(slot == slots[q], shares[q], 0.0)
            mix_high[d], mix_low[d] = split(mixing)

        @pl.loop(0, slab_count)
        def _(d):
            picks[d] = jnp.where(list_row == 0, pick(d), 0.0)

        wait_halo(0)
        for c, value in enumerate(predicted(0, [velocity_ref[c] for c in range(3)])):
            flow[c] = value

    def finish_flow():
        split_tile(out_ref)

        @pl.loop(1, slab_count + 1)
        def _(i):
            d = lax.rem(slab + i, slab_count)
            picks[d] = jnp.where(list_row == 1, pick(d), picks[d])

            @pl.when(i < slab_count)
            def _():
                remote(picks.at[d], arrived.at[slab], fields + 3, d, pencil).start()

        arrived[slab] = picks[slab]
        all_of_slab(arrived, fields + 3).wait_recv()
        surface = jnp.zeros((8, block_x * block_y), jnp.float32)
        for r in range(slab_count):
            high, low = split(arrived[r])
            surface += jnp.dot(high, mix_high[r], preferred_element_type=jnp.float32) + (
                jnp.dot(low, mix_high[r], preferred_element_type=jnp.float32)
                + jnp.dot(high, mix_low[r], preferred_element_type=jnp.float32)
            )
        turned = surface.T
        level = position(2).astype(jnp.float32)
        decay = jnp.exp(-DEPTH_RATE * (depth_cells - 1.0 - level) / depth_cells)

        def target(c):
            spread = jnp.broadcast_to(turned[:, c : c + 1], (block_x * block_y, depth_cells))
            return spread.reshape(cells) * decay

        targets = [target(0), None, target(1)]
        pos_x = (slab * block_x + position(0)).astype(jnp.float32)
        pos_y = (pencil * block_y + position(1)).astype(jnp.float32)
        reach_x = float(max(1, slab_count // 16) * block_x)
        total_x, total_y = float(block_x * slab_count), float(block_y * pencil_count)
        relax = jnp.maximum(
            jnp.maximum(ramp_weight(pos_x, reach_x), ramp_weight(total_x - 1.0 - pos_x, reach_x)),
            jnp.maximum(
                ramp_weight(pos_y, float(block_y)),
                ramp_weight(total_y - 1.0 - pos_y, float(block_y)),
            ),
        )

        def blend(values):
            blended = [(1.0 - relax) * value for value in values]
            return [
                value if aim is None else value + relax * aim
                for value, aim in zip(blended, targets)
            ]

        velocity = blend([flow[c] for c in range(3)])
        send_halo(1, velocity)
        wait_halo(1)
        for c, value in enumerate(blend(predicted(1, velocity))):
            velocity_out[c] = value
        end_halo(0)
        end_halo(1)
        all_of_slab(arrived, fields + 3).wait_send()

    send_halo(0, [velocity_ref[c] for c in range(3)])

    outer_x, outer_y = row_parts, col_parts
    lane = own_col * columns + lax.broadcasted_iota(jnp.int32, (2 * INNER, columns), 1)

    def wave(index, block, outer, length):
        first = jnp.where(
            index < INNER,
            jnp.where(block == 0, 0, block),
            jnp.where(block == 0, outer // 2, outer - block),
        )
        freq = first + outer * (index % INNER)
        folded = jnp.minimum(freq, length - freq).astype(jnp.float32)
        return 2.0 * math.pi / length * folded

    wave_x = wave(lane % (2 * INNER), lane // (2 * INNER), outer_x, NXW)
    place = lax.broadcasted_iota(jnp.int32, (2 * INNER, columns), 0)
    for b in range(col_blocks):
        wave_y = wave(place, jnp.full(place.shape, b, jnp.int32), outer_y, NYW)
        magnitude[b] = jnp.sqrt(wave_x * wave_x + wave_y * wave_y)

    def begin_potential(half):
        over_rows(
            lambda at: begin_rows([part_of(potential, p, at)[...] for p in range(row_parts)], at),
            half,
        )

    all_of_slab_half(potential, 0, potential_sems).wait_recv()
    send_slab_half(tile_rows(potential_ref, 1), potential, 1, potential_sems)
    begin_potential(0)
    tables_in[0].wait()
    tables_in[1].wait()
    finish_rows_half(0, 0, first_sems)
    all_of_slab_half(potential, 1, potential_sems).wait_recv()
    begin_potential(1)
    finish_rows_half(0, 1, first_sems)
    for copy in tables_in[2:]:
        copy.wait()

    prepare_flow()
    all_of_half(0, 0, first_sems).wait_recv()
    all_of_half(0, 1, first_sems).wait_recv()
    send_slab(tile_rows(eta_ref), eta, fields + 1)
    forward_columns(0)
    inverse_columns(1, True)
    inverse_columns(2, False)
    inverse_columns(3, False)
    all_of_slab(eta, fields + 1).wait_recv()

    def use_slope_one(at, parts):
        for p, value in enumerate(parts):
            part_of(total, p, at)[...] = value
        begin_rows([-part_of(eta, p, at)[...] * value for p, value in enumerate(parts)], at)

    def use_curve_one(at, parts):
        for p, value in enumerate(parts):
            height = part_of(eta, p, at)[...]
            term = height * value
            part_of(total, p, at)[...] += term
            part_of(curve, p, at)[...] = 0.5 * height * term

    def use_cubic_one(at, parts):
        for p, value in enumerate(parts):
            height = part_of(eta, p, at)[...]
            part_of(total, p, at)[...] += 0.5 * height * height * value

    def use_slope_two(at, parts):
        following = []
        for p, value in enumerate(parts):
            part_of(total, p, at)[...] += value
            following.append(-part_of(eta, p, at)[...] * value - part_of(curve, p, at)[...])
        begin_rows(following, at)

    def use_curve_two(at, parts):
        for p, value in enumerate(parts):
            part_of(total, p, at)[...] += part_of(eta, p, at)[...] * value

    def use_slope_three(at, parts):
        for p, value in enumerate(parts):
            part_of(total, p, at)[...] += value

    middle = device_count // 2
    all_of(1).wait_recv()
    send(2, 1, device_count)
    inverse_rows(1, use_slope_one)
    finish_rows(4)
    inverse_rows(2, use_curve_one)
    all_of(4).wait_recv()
    send(3, 1, middle)
    forward_columns(4)
    inverse_columns(5, True)
    inverse_columns(6, False)
    all_of(5).wait_recv()
    send(6, 1, device_count)
    inverse_rows(5, use_slope_two)
    finish_rows(7)
    inverse_rows(6, use_curve_two)
    all_of(7).wait_recv()
    send(3, middle, device_count)
    forward_columns(7)
    inverse_columns(8, False)
    send_half_to_rows(8, 0, last_sems)
    all_of_half(8, 0, last_sems).wait_send()
    send_half_to_rows(8, 1, last_sems)
    inverse_rows(3, use_cubic_one)
    for half in (0, 1):
        inverse_rows_half(8, use_slope_three, half, last_sems)
        send_slab_half(lambda to, half=half: total.at[to, halves[half]], back, half, back_sems)
    out_ref[own_rows] = total[slab]
    for half in (0, 1):
        all_of_slab_half(back, half, back_sems).wait_recv()
        for i in range(1, slab_count):
            source = lax.rem(slab + i, slab_count)
            at = pl.multiple_of(source * rows + half * half_rows, half_rows)
            out_ref[pl.ds(at, half_rows)] = back[source, halves[half]]
    finish_flow()
    for n in range(1, fields - 1):
        all_of(n).wait_send()
    all_of_slab(eta, fields + 1).wait_send()
    all_of_half(8, 1, last_sems).wait_send()
    for half in (0, 1):
        all_of_half(0, half, first_sems).wait_send()
        all_of_slab_half(potential, half, potential_sems).wait_send()
        all_of_slab_half(back, half, back_sems).wait_send()


def two_terms(table):
    high = table.astype(jnp.bfloat16)
    low = (table - high.astype(np.float32)).astype(jnp.bfloat16)
    return jnp.asarray(high), jnp.asarray(low)


def whole_step(
    potential, eta, velocity, points, counts, stencil, interp_weight, slab_count, pencil_count
):
    tile_rows, tile_cols = eta.shape
    device_count = slab_count * pencil_count
    rows, columns = NYW // device_count, NXW // device_count
    row_table, _ = tables(NXW)
    col_table, _ = tables(NYW)
    constants = [
        *two_terms(row_table),
        *two_terms(col_table),
        *two_terms(np.ascontiguousarray(col_table.transpose(0, 2, 1))),
    ]
    capacity = points.shape[1]
    block_x, block_y, _ = velocity.shape[1:]
    mixing = jnp.concatenate([stencil.astype(jnp.float32), interp_weight])
    mixing = mixing.reshape(-1, block_x * block_y)
    spectrum = (col_table.shape[0], 2 * INNER, columns)
    list_shape = (slab_count, 8, capacity)
    halo_shape = (STEPS, 4, 3, block_x, velocity.shape[3])
    fields = 9
    strip = pltpu.VMEM((slab_count, rows, tile_cols), jnp.float32)
    vmem = pl.BlockSpec(memory_space=pltpu.VMEM)
    return pl.pallas_call(
        lambda *refs: surface_kernel(slab_count, pencil_count, *refs),
        out_shape=(
            jax.ShapeDtypeStruct((tile_rows, tile_cols), jnp.float32),
            jax.ShapeDtypeStruct(velocity.shape, jnp.float32),
        ),
        in_specs=[vmem] * 6 + [pl.BlockSpec(memory_space=pl.ANY)] * 6,
        out_specs=(vmem, vmem),
        scratch_shapes=[
            *(pltpu.VMEM(table.shape, jnp.bfloat16) for table in constants),
            *([strip] * 5),
            pltpu.VMEM(row_table.shape[:1] + (rows, 2 * INNER), jnp.float32),
            pltpu.VMEM(spectrum, jnp.float32),
            pltpu.VMEM(spectrum, jnp.float32),
            pltpu.VMEM(spectrum, jnp.float32),
            pltpu.VMEM((fields, device_count, rows, columns), jnp.float32),
            pltpu.VMEM((fields, device_count, rows, columns), jnp.float32),
            pltpu.VMEM((2 * tile_rows, tile_cols), jnp.bfloat16),
            pltpu.VMEM((slab_count, tile_cols, capacity), jnp.bfloat16),
            pltpu.VMEM((slab_count, capacity, block_x * block_y), jnp.bfloat16),
            pltpu.VMEM((slab_count, capacity, block_x * block_y), jnp.bfloat16),
            pltpu.VMEM(list_shape, jnp.float32),
            pltpu.VMEM(list_shape, jnp.float32),
            pltpu.VMEM(velocity.shape, jnp.float32),
            pltpu.VMEM(halo_shape, jnp.float32),
            pltpu.VMEM(halo_shape, jnp.float32),
            pltpu.SemaphoreType.DMA((6,)),
            pltpu.SemaphoreType.DMA((fields + 8,)),
            pltpu.SemaphoreType.DMA((fields + 8,)),
            pltpu.SemaphoreType.DMA((4 * STEPS,)),
            pltpu.SemaphoreType.DMA((4 * STEPS,)),
        ],
        compiler_params=pltpu.CompilerParams(
            collective_id=0, has_side_effects=True, vmem_limit_bytes=60 * 1024 * 1024
        ),
    )(
        potential,
        eta,
        velocity,
        points,
        counts[:, None],
        mixing,
        *constants,
    )


def surface_plain(potential, eta, magnitude, row_table, column_table, slab_count):
    tile_rows, tile_cols = eta.shape
    columns = magnitude.shape[-1]
    device_count = NXW // columns
    rows = NYW // device_count
    row_blocks, column_blocks = jnp.asarray(row_table), jnp.asarray(column_table)
    both = jnp.stack([potential, eta]).reshape(2, slab_count, rows, tile_cols)
    both = lax.all_to_all(both, "slab", split_axis=1, concat_axis=1, tiled=True)
    both = both.transpose(0, 2, 1, 3).reshape(2, rows, NXW)
    potential, eta = both[0], both[1]
    first_mult = magnitude * (1.0 / (NXW * NYW))
    second_mult = magnitude * first_mult
    third_mult = magnitude * second_mult

    def forward(field):
        arrived = exchange(rows_forward(field, row_blocks, device_count))
        return columns_forward(arrived.reshape(NYW, columns), column_blocks)

    def inverse(spectrum):
        field = columns_inverse(spectrum, column_blocks)
        return rows_inverse(exchange(field.reshape(device_count, rows, columns)), row_blocks)

    spectrum = forward(potential)
    slope_one = inverse(spectrum * first_mult)
    curve_one = inverse(spectrum * second_mult)
    cubic_one = inverse(spectrum * third_mult)
    spectrum = forward(-eta * slope_one)
    slope_two = inverse(spectrum * first_mult)
    curve_two = inverse(spectrum * second_mult)
    spectrum = forward(-eta * slope_two - 0.5 * eta * eta * curve_one)
    slope_three = inverse(spectrum * first_mult)
    vertical = (
        slope_one
        + slope_two
        + eta * curve_one
        + slope_three
        + eta * curve_two
        + 0.5 * eta * eta * cubic_one
    )
    vertical = vertical.reshape(rows, slab_count, tile_cols).transpose(1, 0, 2)
    vertical = lax.all_to_all(vertical, "slab", split_axis=0, concat_axis=0, tiled=True)
    vertical = vertical.reshape(tile_rows, tile_cols)

    return vertical


def ramp_weight(distance, reach_len):
    ratio = jnp.clip(1.0 - distance / reach_len, 0.0, 1.0)
    return ratio * ratio


def blend_weight(pos_x, pos_y, total_x, total_y, reach_x, reach_y):
    along_x = jnp.maximum(ramp_weight(pos_x, reach_x), ramp_weight(total_x - 1.0 - pos_x, reach_x))
    across = jnp.maximum(ramp_weight(pos_y, reach_y), ramp_weight(total_y - 1.0 - pos_y, reach_y))
    return jnp.maximum(along_x[:, None], across[None, :])[:, :, None]


def neighbours(shard, axis, dim):
    size, length = lax.axis_size(axis), shard.shape[dim]
    up = [(i, i + 1) for i in range(size - 1)]
    down = [(i + 1, i) for i in range(size - 1)]
    before = lax.ppermute(lax.slice_in_dim(shard, length - 1, length, axis=dim), axis, up)
    after = lax.ppermute(lax.slice_in_dim(shard, 0, 1, axis=dim), axis, down)
    minus = jnp.concatenate([before, lax.slice_in_dim(shard, 0, length - 1, axis=dim)], axis=dim)
    plus = jnp.concatenate([lax.slice_in_dim(shard, 1, length, axis=dim), after], axis=dim)
    return minus, plus


def predict(velocity):
    minus_x, plus_x = neighbours(velocity, "slab", 1)
    minus_y, plus_y = neighbours(velocity, "pencil", 2)
    padded = jnp.pad(velocity, ((0, 0), (0, 0), (0, 0), (1, 1)))
    minus_z, plus_z = padded[..., :-2], padded[..., 2:]
    laplace = plus_x + minus_x + (plus_y + minus_y) + (plus_z + minus_z) - 6.0 * velocity
    advect = (
        velocity[0] * (plus_x - minus_x)
        + velocity[1] * (plus_y - minus_y)
        + velocity[2] * (plus_z - minus_z)
    )
    return velocity + TIME_STEP * (VISCOSITY * laplace - 0.5 * advect)


def on_device(
    surface_eta, surface_potential, velocity, send_point, send_count, stencil, interp_weight
):
    slab_count = lax.axis_size("slab")
    pencil_count = lax.axis_size("pencil")
    device_count = slab_count * pencil_count
    slab_index = lax.axis_index("slab")
    pencil_index = lax.axis_index("pencil")
    tile_rows, tile_cols = surface_eta.shape
    rows = NYW // device_count
    columns = NXW // device_count
    if (
        columns % 128 == 0
        and rows % 16 == 0
        and INNER % rows == 0
        and velocity.shape[1] == velocity.shape[2]
        and STEPS == 2
    ):
        return whole_step(
            surface_potential,
            surface_eta,
            velocity,
            send_point[0, 0],
            send_count[0, 0],
            stencil,
            interp_weight,
            slab_count,
            pencil_count,
        )
    own = pencil_index * slab_count + slab_index
    row_table, row_order = tables(NXW)
    column_table, column_order = tables(NYW)
    wave_x = 2.0 * math.pi / NXW * jnp.asarray(row_order.reshape(-1)).astype(jnp.float32)
    wave_x = lax.dynamic_slice(wave_x, (own * columns,), (columns,))
    wave_y = 2.0 * math.pi / NYW * jnp.asarray(column_order).astype(jnp.float32)[:, :, None]
    magnitude = jnp.sqrt(wave_x * wave_x + wave_y * wave_y)
    vertical = surface_plain(
        surface_potential, surface_eta, magnitude, row_table, column_table, slab_count
    )

    points = send_point[0, 0]
    capacity = points.shape[1]
    counts = send_count[0, 0]
    flat_points = points.reshape(-1)
    live = (jnp.arange(capacity, dtype=jnp.int32)[None, :] < counts[:, None]).reshape(-1)
    row_pick = (
        (flat_points // tile_cols)[:, None] == jnp.arange(tile_rows, dtype=jnp.int32)[None, :]
    ).astype(jnp.float32)
    column_pick = (flat_points % tile_cols)[:, None] == jnp.arange(tile_cols, dtype=jnp.int32)[
        None, :
    ]
    column_pick = column_pick & live[:, None]

    def pick(tile):
        picked_rows = jnp.dot(row_pick, tile, precision=HIGH)
        return jnp.sum(jnp.where(column_pick, picked_rows, 0.0), axis=1)

    picked = jnp.stack([pick(surface_eta), pick(vertical)]).reshape(2, slab_count, capacity)
    arrived = lax.all_to_all(picked, "slab", split_axis=1, concat_axis=1, tiled=True).reshape(
        2, slab_count * capacity
    )
    block_x, block_y, depth_cells = velocity.shape[1:]
    shares = interp_weight / jnp.sum(interp_weight, axis=0)
    slots = jnp.arange(slab_count * capacity, dtype=jnp.int32)[:, None]
    mixing = 0.0
    for q in range(stencil.shape[0]):
        mixing = mixing + jnp.where(
            slots == stencil[q].reshape(1, -1), shares[q].reshape(1, -1), 0.0
        )
    surface_at = jnp.dot(arrived, mixing, precision=lax.Precision.HIGHEST)
    surface_at = surface_at.reshape(2, block_x, block_y)

    zone_slabs = max(1, slab_count // 16)
    pos_x = (slab_index * block_x + jnp.arange(block_x, dtype=jnp.int32)).astype(jnp.float32)
    pos_y = (pencil_index * block_y + jnp.arange(block_y, dtype=jnp.int32)).astype(jnp.float32)
    relax_weight = blend_weight(
        pos_x,
        pos_y,
        float(block_x * slab_count),
        float(block_y * pencil_count),
        float(zone_slabs * block_x),
        float(block_y),
    )
    levels = jnp.arange(depth_cells, dtype=jnp.float32)
    depth_decay = jnp.exp(-DEPTH_RATE * (depth_cells - 1.0 - levels) / depth_cells)
    target = jnp.stack(
        [
            surface_at[0][:, :, None] * depth_decay,
            jnp.zeros((block_x, block_y, depth_cells), jnp.float32),
            surface_at[1][:, :, None] * depth_decay,
        ]
    )
    for substep in range(STEPS):
        velocity = (1.0 - relax_weight) * predict(velocity) + relax_weight * target
    return (vertical, velocity)


def solution(mesh):
    in_specs = (
        P("pencil", "slab"),
        P("pencil", "slab"),
        P(None, "slab", "pencil", None),
        P("slab", "pencil", None, None),
        P("slab", "pencil", None),
        P(None, "slab", "pencil"),
        P(None, "slab", "pencil"),
    )
    out_specs = (P("pencil", "slab"), P(None, "slab", "pencil", None))
    return jax.shard_map(
        on_device, mesh=mesh, in_specs=in_specs, out_specs=out_specs, check_vma=False
    )
```

```python
import math

import jax
import jax.numpy as jnp
import numpy as np
from jax import lax
from jax.experimental import pallas as pl
from jax.experimental.pallas import tpu as pltpu
from jax.sharding import PartitionSpec as P

NXW = 4096
NYW = 2048
STEPS = 2
INNER = 256


TIME_STEP = 0.2
VISCOSITY = 0.6
DEPTH_RATE = 3.0

HIGH = lax.Precision.HIGH
BOTH = ("pencil", "slab")


def real_dft(parts):
    size = len(parts)
    if size == 2:
        return [(parts[0] + parts[1], None), (parts[0] - parts[1], None)]
    even = real_dft(parts[0::2])
    odd = real_dft(parts[1::2])
    half = size // 2
    result = [None] * (half + 1)
    for k in range(size // 4 + 1):
        (even_re, even_im), (odd_re, odd_im) = even[k], odd[k]
        if k == 0:
            result[0] = (even_re + odd_re, None)
            result[half] = (even_re - odd_re, None)
        elif 4 * k == size:
            result[k] = (even_re, -odd_re)
        else:
            c, s = math.cos(2.0 * math.pi * k / size), math.sin(2.0 * math.pi * k / size)
            turned_re = c * odd_re + s * odd_im
            turned_im = c * odd_im - s * odd_re
            result[k] = (even_re + turned_re, even_im + turned_im)
            result[half - k] = (even_re - turned_re, turned_im - even_im)
    return result


def outer_dft(parts):
    bins = real_dft(list(parts))
    out = [bins[0][0], bins[-1][0]]
    for re, im in bins[1:-1]:
        out += [re, im]
    return tuple(out)


def real_dft_transposed(bins):
    half = len(bins) - 1
    size = 2 * half
    if size == 2:
        return [bins[0][0] + bins[1][0], bins[0][0] - bins[1][0]]
    even, odd = [None] * (half // 2 + 1), [None] * (half // 2 + 1)
    for k in range(size // 4 + 1):
        re, im = bins[k]
        if k == 0:
            even[0] = (re + bins[half][0], None)
            odd[0] = (re - bins[half][0], None)
        elif 4 * k == size:
            even[k] = (re, None)
            odd[k] = (-im, None)
        else:
            other_re, other_im = bins[half - k]
            c, s = math.cos(2.0 * math.pi * k / size), math.sin(2.0 * math.pi * k / size)
            turned_re, turned_im = re - other_re, im + other_im
            even[k] = (re + other_re, im - other_im)
            odd[k] = (c * turned_re - s * turned_im, s * turned_re + c * turned_im)
    result = [None] * size
    result[0::2] = real_dft_transposed(even)
    result[1::2] = real_dft_transposed(odd)
    return result


def outer_dft_transposed(pieces):
    half = len(pieces) // 2
    bins = [(pieces[0], None)]
    bins += [(pieces[2 * k], pieces[2 * k + 1]) for k in range(1, half)]
    return real_dft_transposed(bins + [(pieces[1], None)])


def tables(length):
    outer = length // INNER
    within = np.arange(INNER)
    blocks = np.zeros((outer // 2, 2 * INNER, 2 * INNER), np.float64)
    order = np.zeros((outer // 2, 2 * INNER), np.int32)
    for b in range(outer // 2):
        for side in range(2):
            if b == 0:
                first = 0 if side == 0 else outer // 2
            else:
                first = b if side == 0 else outer - b
            freq = first + outer * within
            angle = 2.0 * math.pi / length * ((within[:, None] * freq[None, :]) % length)
            cos, sin = np.cos(angle), np.sin(angle)
            columns = slice(side * INNER, (side + 1) * INNER)
            order[b, columns] = freq
            if b == 0:
                blocks[b, columns, columns] = cos + sin
            else:
                sign = 1.0 if side == 0 else -1.0
                blocks[b, :INNER, columns] = cos + sin
                blocks[b, INNER:, columns] = sign * (sin - cos)
    return blocks.astype(np.float32), np.minimum(order, length - order)


def rows_forward(values, blocks, device_count):
    rows, length = values.shape
    pieces = outer_dft([values[:, i : i + INNER] for i in range(0, length, INNER)])
    stacked = jnp.stack(
        [jnp.concatenate(pieces[2 * b : 2 * b + 2], axis=1) for b in range(len(pieces) // 2)]
    )
    spectrum = jnp.einsum("brk,bkn->brn", stacked, blocks, precision=HIGH)
    columns = length // device_count
    spectrum = spectrum.reshape(spectrum.shape[0], rows, 2 * INNER // columns, columns)
    return spectrum.transpose(0, 2, 1, 3).reshape(device_count, rows, columns)


def rows_inverse(values, blocks):
    device_count, rows, columns = values.shape
    grouped = values.reshape(blocks.shape[0], 2 * INNER // columns, rows, columns)
    grouped = grouped.transpose(0, 2, 1, 3).reshape(blocks.shape[0], rows, 2 * INNER)
    stacked = jnp.einsum("brn,bkn->brk", grouped, blocks, precision=HIGH)
    pieces = []
    for b in range(blocks.shape[0]):
        pieces += [stacked[b, :, :INNER], stacked[b, :, INNER:]]
    return jnp.concatenate(outer_dft_transposed(pieces), axis=1)


def columns_forward(values, blocks):
    pieces = outer_dft([values[i : i + INNER] for i in range(0, values.shape[0], INNER)])
    stacked = jnp.concatenate(pieces, axis=0).reshape(
        blocks.shape[0], 2 * INNER, values.shape[1]
    )
    return jnp.einsum("bkn,bkc->bnc", blocks, stacked, precision=HIGH)


def columns_inverse(values, blocks):
    stacked = jnp.einsum("bkn,bnc->bkc", blocks, values, precision=HIGH)
    pieces = []
    for b in range(blocks.shape[0]):
        pieces += [stacked[b, :INNER], stacked[b, INNER:]]
    return jnp.concatenate(outer_dft_transposed(pieces), axis=0)


def exchange(values):
    return lax.all_to_all(values, BOTH, split_axis=0, concat_axis=0, tiled=True)


def split(values):
    high = values.astype(jnp.bfloat16)
    return high, (values - high.astype(jnp.float32)).astype(jnp.bfloat16)


def row_product(values, high_ref, low_ref, block, contract):
    rows = values.shape[0]
    high, low = split(values)
    dims = (((1,), (contract,)), ((), ()))
    main = lax.dot_general(
        jnp.concatenate([high, low], axis=0),
        high_ref[block],
        dims,
        preferred_element_type=jnp.float32,
    )
    rest = lax.dot_general(high, low_ref[block], dims, preferred_element_type=jnp.float32)
    return main[:rows] + (main[rows:] + rest)


def column_product(values, high_ref, low_ref, block):
    columns = values.shape[1]
    high, low = split(values)
    main = jnp.dot(
        high_ref[block],
        jnp.concatenate([high, low], axis=1),
        preferred_element_type=jnp.float32,
    )
    rest = jnp.dot(low_ref[block], high, preferred_element_type=jnp.float32)
    return main[:, :columns] + (main[:, columns:] + rest)


def surface_kernel(
    slab_count,
    pencil_count,
    potential_ref,
    eta_ref,
    velocity_ref,
    points_ref,
    counts_ref,
    mixing_ref,
    row_high_in,
    row_low_in,
    col_high_in,
    col_low_in,
    colt_high_in,
    colt_low_in,
    out_ref,
    velocity_out,
    row_high,
    row_low,
    col_high,
    col_low,
    colt_high,
    colt_low,
    potential,
    eta,
    back,
    total,
    curve,
    stage_rows,
    stage_cols,
    spectrum,
    magnitude,
    sent,
    held,
    tile_split,
    pick_cols,
    mix_high,
    mix_low,
    picks,
    arrived,
    flow,
    packed,
    halo,
    table_sem,
    send_sem,
    recv_sem,
    halo_send,
    halo_recv,
):
    slab = lax.axis_index("slab")
    pencil = lax.axis_index("pencil")
    device_count = slab_count * pencil_count
    own = pencil * slab_count + slab
    own_col = slab * pencil_count + pencil
    rows = sent.shape[2]
    columns = sent.shape[3]
    per_block = 2 * INNER // columns
    row_blocks = row_high.shape[0]
    col_blocks = col_high.shape[0]
    chunk = potential.shape[2]
    per_part = INNER // rows
    row_parts = 2 * row_blocks
    col_parts = 2 * col_blocks
    step = 8

    pairs = (
        (row_high_in, row_high),
        (row_low_in, row_low),
        (colt_high_in, colt_high),
        (colt_low_in, colt_low),
        (col_high_in, col_high),
        (col_low_in, col_low),
    )
    tables_in = [
        pltpu.make_async_copy(source, target, table_sem.at[i])
        for i, (source, target) in enumerate(pairs)
    ]
    for copy in tables_in:
        copy.start()

    def partner(i):
        return lax.rem(pencil + lax.rem(i, pencil_count), pencil_count), lax.rem(
            slab + i // pencil_count, slab_count
        )

    halo[...] = jnp.zeros(halo.shape, jnp.float32)
    barrier = pltpu.get_barrier_semaphore()

    @pl.loop(1, device_count)
    def _(i):
        to_pencil, to_slab = partner(i)
        pl.semaphore_signal(
            barrier,
            inc=1,
            device_id={"slab": to_slab, "pencil": to_pencil},
            device_id_type=pl.DeviceIdType.MESH,
        )

    pl.semaphore_wait(barrier, device_count - 1)

    def remote(source, target, index, to_slab, to_pencil):
        return pltpu.make_async_remote_copy(
            src_ref=source,
            dst_ref=target,
            send_sem=send_sem.at[index],
            recv_sem=recv_sem.at[index],
            device_id={"slab": to_slab, "pencil": to_pencil},
            device_id_type=pl.DeviceIdType.MESH,
        )

    def start_to_columns(n, to):
        @pl.when(to != own_col)
        def _():
            remote(
                sent.at[n, to], held.at[n, own], n, to // pencil_count, lax.rem(to, pencil_count)
            ).start()

    def start_to_rows(n, to):
        @pl.when(to != own)
        def _():
            remote(
                sent.at[n, to], held.at[n, own_col], n, lax.rem(to, slab_count), to // slab_count
            ).start()

    def send(n, first, last):
        @pl.loop(first, last)
        def _(i):
            to_pencil, to_slab = partner(i)
            to = to_pencil * slab_count + to_slab
            remote(sent.at[n, to], held.at[n, own_col], n, to_slab, to_pencil).start()

    def all_of(n):
        others = pl.ds(0, device_count - 1)
        return remote(sent.at[n, others], held.at[n, others], n, slab, pencil)

    def send_slab(source_of, target, n):
        for i in range(1, slab_count):
            to = lax.rem(slab + i, slab_count)
            remote(source_of(to), target.at[slab], n, to, pencil).start()

    def all_of_slab(target, n):
        others = target.at[pl.ds(0, slab_count - 1)]
        return remote(others, others, n, slab, pencil)

    fields = sent.shape[0]
    half_rows = rows // 2
    halves = (pl.ds(0, half_rows), pl.ds(half_rows, half_rows))
    potential_sems = (fields, fields + 4)
    first_sems = (0, fields + 5)
    last_sems = (8, fields + 6)
    back_sems = (fields + 2, fields + 7)

    def tile_rows(ref, half=None):
        if half is None:
            return lambda to: ref.at[pl.ds(pl.multiple_of(to * rows, rows), rows)]
        return lambda to: ref.at[
            pl.ds(pl.multiple_of(to * rows + half * half_rows, half_rows), half_rows)
        ]

    def send_slab_half(source_of, target, half, sems):
        for i in range(1, slab_count):
            to = lax.rem(slab + i, slab_count)
            remote(
                source_of(to), target.at[slab, halves[half]], sems[half], to, pencil
            ).start()

    def all_of_slab_half(target, half, sems):
        others = target.at[pl.ds(0, slab_count - 1), halves[half]]
        return remote(others, others, sems[half], slab, pencil)

    def all_of_half(n, half, sems):
        others = pl.ds(0, device_count - 1)
        return remote(
            sent.at[n, others, halves[half]],
            held.at[n, others, halves[half]],
            sems[half],
            slab,
            pencil,
        )

    own_rows = pl.ds(pl.multiple_of(slab * rows, rows), rows)
    send_slab_half(tile_rows(potential_ref, 0), potential, 0, potential_sems)
    potential[slab] = potential_ref[own_rows]
    eta[slab] = eta_ref[own_rows]

    def part_of(ref, part, at):
        start = part * INNER % chunk
        return ref.at[part * INNER // chunk, at, pl.ds(start, INNER)]

    def piece_of(piece, at):
        return stage_rows.at[piece // 2, at, pl.ds(piece % 2 * INNER, INNER)]

    def over_rows(body, half=None):
        start = 0 if half is None else half * half_rows
        stop = rows if half is None else start + half_rows

        @pl.loop(start // step, stop // step)
        def _(i):
            body(pl.ds(pl.multiple_of(i * step, step), step))

    def begin_rows(parts, at):
        for piece, value in enumerate(outer_dft(parts)):
            piece_of(piece, at)[...] = value

    def finish_rows(n):
        @pl.loop(0, row_blocks)
        def _(i):
            b = lax.rem(i + own_col // per_block, row_blocks)
            result = row_product(stage_rows[b], row_high, row_low, b, 0)
            for i in range(per_block):
                sent[n, b * per_block + i] = result[:, i * columns : (i + 1) * columns]
                start_to_columns(n, b * per_block + i)

        held[n, own] = sent[n, own_col]

    def finish_rows_half(n, half, sems):
        part = halves[half]

        @pl.loop(0, row_blocks)
        def _(i):
            b = lax.rem(i + own_col // per_block, row_blocks)
            result = row_product(stage_rows[b, part], row_high, row_low, b, 0)
            for j in range(per_block):
                to = b * per_block + j
                sent[n, to, part] = result[:, j * columns : (j + 1) * columns]

                @pl.when(to != own_col)
                def _(to=to):
                    remote(
                        sent.at[n, to, part],
                        held.at[n, own, part],
                        sems[half],
                        to // pencil_count,
                        lax.rem(to, pencil_count),
                    ).start()

        held[n, own, part] = sent[n, own_col, part]

    def inverse_rows_half(n, use, half, sems):
        part = halves[half]
        all_of_half(n, half, sems).wait_recv()

        @pl.loop(0, row_blocks)
        def _(b):
            values = jnp.concatenate(
                [held[n, b * per_block + i, part] for i in range(per_block)], axis=1
            )
            stage_rows[b, part] = row_product(values, row_high, row_low, b, 1)

        def body(at):
            use(at, outer_dft_transposed([piece_of(p, at)[...] for p in range(row_parts)]))

        over_rows(body, half)

    def send_half_to_rows(n, half, sems):
        part = halves[half]

        @pl.loop(1, device_count)
        def _(i):
            to_pencil, to_slab = partner(i)
            to = to_pencil * slab_count + to_slab
            remote(
                sent.at[n, to, part], held.at[n, own_col, part], sems[half], to_slab, to_pencil
            ).start()

    def inverse_rows(n, use):
        if n in (2, 3, 6, 8):
            all_of(n).wait_recv()

        @pl.loop(0, row_blocks)
        def _(b):
            values = jnp.concatenate(
                [held[n, b * per_block + i] for i in range(per_block)], axis=1
            )
            stage_rows[b] = row_product(values, row_high, row_low, b, 1)

        def body(at):
            use(at, outer_dft_transposed([piece_of(p, at)[...] for p in range(row_parts)]))

        over_rows(body)

    def over_columns(body):
        @pl.loop(0, 2 * per_part)
        def _(i):
            body(i // 2, pl.multiple_of(lax.rem(i, 2) * (rows // 2), rows // 2))

    def forward_columns(n):
        def body(q, start):
            parts = [held[n, p * per_part + q, pl.ds(start, rows // 2)] for p in range(col_parts)]
            for piece, value in enumerate(outer_dft(parts)):
                at = pl.multiple_of(piece % 2 * INNER + q * rows + start, rows // 2)
                stage_cols[piece // 2, pl.ds(at, rows // 2)] = value

        over_columns(body)

        @pl.loop(0, col_blocks)
        def _(b):
            spectrum[b] = column_product(stage_cols[b], colt_high, colt_low, b)

    def inverse_columns(n, now):
        @pl.loop(0, col_blocks)
        def _(b):
            values = spectrum[b] * magnitude[b]
            spectrum[b] = values
            stage_cols[b] = column_product(values, col_high, col_low, b)

        @pl.loop(0, per_part)
        def _(i):
            q = lax.rem(i + own, per_part)
            for half in (0, 1):
                offset = half * (rows // 2)
                pieces = []
                for piece in range(col_parts):
                    at = pl.multiple_of(piece % 2 * INNER + q * rows + offset, rows // 2)
                    pieces.append(stage_cols[piece // 2, pl.ds(at, rows // 2)])
                for p, value in enumerate(outer_dft_transposed(pieces)):
                    sent[n, p * per_part + q, pl.ds(offset, rows // 2)] = value * (
                        1.0 / (NXW * NYW)
                    )
            if now:
                turn = (pencil + 1) * (col_parts // pencil_count)
                for p in range(col_parts):
                    start_to_rows(n, lax.rem(p + turn, col_parts) * per_part + q)

        held[n, own_col] = sent[n, own]

    capacity = points_ref.shape[1]
    block_x, block_y, depth_cells = velocity_ref.shape[1:]
    tile_rows_count, tile_cols = eta_ref.shape
    cells = (block_x, block_y, depth_cells)

    def position(axis):
        return lax.broadcasted_iota(jnp.int32, cells, axis)

    links = (
        (slab < slab_count - 1, slab + 1, pencil, slab > 0),
        (slab > 0, slab - 1, pencil, slab < slab_count - 1),
        (pencil < pencil_count - 1, slab, pencil + 1, pencil > 0),
        (pencil > 0, slab, pencil - 1, pencil < pencil_count - 1),
    )

    def halo_copy(k, side, to_slab, to_pencil):
        return pltpu.make_async_remote_copy(
            src_ref=packed.at[k, side],
            dst_ref=halo.at[k, side],
            send_sem=halo_send.at[4 * k + side],
            recv_sem=halo_recv.at[4 * k + side],
            device_id={"slab": to_slab, "pencil": to_pencil},
            device_id_type=pl.DeviceIdType.MESH,
        )

    def send_halo(k, velocity):
        for c in range(3):
            packed[k, 0, c] = velocity[c][block_x - 1]
            packed[k, 1, c] = velocity[c][0]
            packed[k, 2, c] = velocity[c][:, block_y - 1]
            packed[k, 3, c] = velocity[c][:, 0]
        for side, (sends, to_slab, to_pencil, _) in enumerate(links):

            @pl.when(sends)
            def _(side=side, to_slab=to_slab, to_pencil=to_pencil):
                halo_copy(k, side, to_slab, to_pencil).start()

    def wait_halo(k):
        for side, (_, _, _, receives) in enumerate(links):

            @pl.when(receives)
            def _(side=side):
                halo_copy(k, side, slab, pencil).wait_recv()

    def end_halo(k):
        for side, (sends, _, _, _) in enumerate(links):

            @pl.when(sends)
            def _(side=side):
                halo_copy(k, side, slab, pencil).wait_send()

    def predicted(k, velocity):
        result = []
        for c in range(3):
            here = velocity[c]
            minus_x = jnp.concatenate([halo[k, 0, c][None], here[:-1]], axis=0)
            plus_x = jnp.concatenate([here[1:], halo[k, 1, c][None]], axis=0)
            minus_y = jnp.where(
                position(1) == 0, halo[k, 2, c][:, None], pltpu.roll(here, 1, 1)
            )
            plus_y = jnp.where(
                position(1) == block_y - 1,
                halo[k, 3, c][:, None],
                pltpu.roll(here, block_y - 1, 1),
            )
            minus_z = jnp.where(position(2) == 0, 0.0, pltpu.roll(here, 1, 2))
            plus_z = jnp.where(
                position(2) == depth_cells - 1, 0.0, pltpu.roll(here, depth_cells - 1, 2)
            )
            laplace = (
                plus_x + minus_x + (plus_y + minus_y) + (plus_z + minus_z) - 6.0 * here
            )
            advect = (
                velocity[0] * (plus_x - minus_x)
                + velocity[1] * (plus_y - minus_y)
                + velocity[2] * (plus_z - minus_z)
            )
            result.append(here + TIME_STEP * (VISCOSITY * laplace - 0.5 * advect))
        return result

    def split_tile(ref):
        @pl.loop(0, slab_count)
        def _(i):
            at = pl.multiple_of(i * rows, rows)
            high, low = split(ref[pl.ds(at, rows)])
            tile_split[pl.ds(at, rows)] = high
            tile_split[pl.ds(pl.multiple_of(tile_rows_count + at, rows), rows)] = low

    def pick(d):
        both = jnp.dot(tile_split[...], pick_cols[d], preferred_element_type=jnp.float32)
        row = lax.broadcasted_iota(jnp.int32, (tile_rows_count, capacity), 0)
        slot = lax.broadcasted_iota(jnp.int32, (1, capacity), 1)
        counts = counts_ref[...]
        toward = lax.broadcasted_iota(jnp.int32, counts.shape, 1) == d
        live = slot < jnp.sum(jnp.where(toward, counts, 0), axis=1, keepdims=True)
        wanted = jnp.where(live, points_ref[pl.ds(d, 1)] // tile_cols, -1)
        found = both[:tile_rows_count] + both[tile_rows_count:]
        return jnp.sum(jnp.where(row == wanted, found, 0.0), axis=0, keepdims=True)

    list_row = lax.broadcasted_iota(jnp.int32, (8, capacity), 0)

    def prepare_flow():
        split_tile(eta_ref)
        mixing_in = mixing_ref[...]
        points_each = mixing_in.shape[0] // 2
        weights = [mixing_in[points_each + q][None] for q in range(points_each)]
        shares = [weight / sum(weights[1:], weights[0]) for weight in weights]
        slots = [mixing_in[q][None].astype(jnp.int32) for q in range(points_each)]

        @pl.loop(0, slab_count)
        def _(d):
            column = lax.broadcasted_iota(jnp.int32, (tile_cols, capacity), 0)
            chosen = jnp.where(column == points_ref[pl.ds(d, 1)] % tile_cols, 1.0, 0.0)
            pick_cols[d] = chosen.astype(jnp.bfloat16)
            slot = lax.broadcasted_iota(jnp.int32, (capacity, block_x * block_y), 0) + d * capacity
            mixing = jnp.zeros(slot.shape, jnp.float32)
            for q in range(points_each):
                mixing = mixing + jnp.where(slot == slots[q], shares[q], 0.0)
            mix_high[d], mix_low[d] = split(mixing)

        @pl.loop(0, slab_count)
        def _(d):
            picks[d] = jnp.where(list_row == 0, pick(d), 0.0)

        wait_halo(0)
        for c, value in enumerate(predicted(0, [velocity_ref[c] for c in range(3)])):
            flow[c] = value

    def finish_flow():
        split_tile(out_ref)

        @pl.loop(1, slab_count + 1)
        def _(i):
            d = lax.rem(slab + i, slab_count)
            picks[d] = jnp.where(list_row == 1, pick(d), picks[d])

            @pl.when(i < slab_count)
            def _():
                remote(picks.at[d], arrived.at[slab], fields + 3, d, pencil).start()

        arrived[slab] = picks[slab]
        all_of_slab(arrived, fields + 3).wait_recv()
        surface = jnp.zeros((8, block_x * block_y), jnp.float32)
        for r in range(slab_count):
            high, low = split(arrived[r])
            surface += jnp.dot(high, mix_high[r], preferred_element_type=jnp.float32) + (
                jnp.dot(low, mix_high[r], preferred_element_type=jnp.float32)
                + jnp.dot(high, mix_low[r], preferred_element_type=jnp.float32)
            )
        turned = surface.T
        level = position(2).astype(jnp.float32)
        decay = jnp.exp(-DEPTH_RATE * (depth_cells - 1.0 - level) / depth_cells)

        def target(c):
            spread = jnp.broadcast_to(turned[:, c : c + 1], (block_x * block_y, depth_cells))
            return spread.reshape(cells) * decay

        targets = [target(0), None, target(1)]
        pos_x = (slab * block_x + position(0)).astype(jnp.float32)
        pos_y = (pencil * block_y + position(1)).astype(jnp.float32)
        reach_x = float(max(1, slab_count // 16) * block_x)
        total_x, total_y = float(block_x * slab_count), float(block_y * pencil_count)
        relax = jnp.maximum(
            jnp.maximum(ramp_weight(pos_x, reach_x), ramp_weight(total_x - 1.0 - pos_x, reach_x)),
            jnp.maximum(
                ramp_weight(pos_y, float(block_y)),
                ramp_weight(total_y - 1.0 - pos_y, float(block_y)),
            ),
        )

        def blend(values):
            blended = [(1.0 - relax) * value for value in values]
            return [
                value if aim is None else value + relax * aim
                for value, aim in zip(blended, targets)
            ]

        velocity = blend([flow[c] for c in range(3)])
        send_halo(1, velocity)
        wait_halo(1)
        for c, value in enumerate(blend(predicted(1, velocity))):
            velocity_out[c] = value
        end_halo(0)
        end_halo(1)
        all_of_slab(arrived, fields + 3).wait_send()

    send_halo(0, [velocity_ref[c] for c in range(3)])

    outer_x, outer_y = row_parts, col_parts
    lane = own_col * columns + lax.broadcasted_iota(jnp.int32, (2 * INNER, columns), 1)

    def wave(index, block, outer, length):
        first = jnp.where(
            index < INNER,
            jnp.where(block == 0, 0, block),
            jnp.where(block == 0, outer // 2, outer - block),
        )
        freq = first + outer * (index % INNER)
        folded = jnp.minimum(freq, length - freq).astype(jnp.float32)
        return 2.0 * math.pi / length * folded

    wave_x = wave(lane % (2 * INNER), lane // (2 * INNER), outer_x, NXW)
    place = lax.broadcasted_iota(jnp.int32, (2 * INNER, columns), 0)
    for b in range(col_blocks):
        wave_y = wave(place, jnp.full(place.shape, b, jnp.int32), outer_y, NYW)
        magnitude[b] = jnp.sqrt(wave_x * wave_x + wave_y * wave_y)

    def begin_potential(half):
        over_rows(
            lambda at: begin_rows([part_of(potential, p, at)[...] for p in range(row_parts)], at),
            half,
        )

    all_of_slab_half(potential, 0, potential_sems).wait_recv()
    send_slab_half(tile_rows(potential_ref, 1), potential, 1, potential_sems)
    begin_potential(0)
    tables_in[0].wait()
    tables_in[1].wait()
    finish_rows_half(0, 0, first_sems)
    all_of_slab_half(potential, 1, potential_sems).wait_recv()
    begin_potential(1)
    finish_rows_half(0, 1, first_sems)
    for copy in tables_in[2:]:
        copy.wait()

    prepare_flow()
    all_of_half(0, 0, first_sems).wait_recv()
    all_of_half(0, 1, first_sems).wait_recv()
    send_slab(tile_rows(eta_ref), eta, fields + 1)
    forward_columns(0)
    inverse_columns(1, True)
    inverse_columns(2, False)
    inverse_columns(3, False)
    all_of_slab(eta, fields + 1).wait_recv()

    def use_slope_one(at, parts):
        for p, value in enumerate(parts):
            part_of(total, p, at)[...] = value
        begin_rows([-part_of(eta, p, at)[...] * value for p, value in enumerate(parts)], at)

    def use_curve_one(at, parts):
        for p, value in enumerate(parts):
            height = part_of(eta, p, at)[...]
            term = height * value
            part_of(total, p, at)[...] += term
            part_of(curve, p, at)[...] = 0.5 * height * term

    def use_cubic_one(at, parts):
        for p, value in enumerate(parts):
            height = part_of(eta, p, at)[...]
            part_of(total, p, at)[...] += 0.5 * height * height * value

    def use_slope_two(at, parts):
        following = []
        for p, value in enumerate(parts):
            part_of(total, p, at)[...] += value
            following.append(-part_of(eta, p, at)[...] * value - part_of(curve, p, at)[...])
        begin_rows(following, at)

    def use_curve_two(at, parts):
        for p, value in enumerate(parts):
            part_of(total, p, at)[...] += part_of(eta, p, at)[...] * value

    def use_slope_three(at, parts):
        for p, value in enumerate(parts):
            part_of(total, p, at)[...] += value

    middle = device_count // 2
    all_of(1).wait_send()
    send(2, 1, device_count)
    all_of(1).wait_recv()
    inverse_rows(1, use_slope_one)
    finish_rows(4)
    inverse_rows(2, use_curve_one)
    all_of(4).wait_recv()
    send(3, 1, middle)
    forward_columns(4)
    inverse_columns(5, True)
    inverse_columns(6, False)
    all_of(5).wait_send()
    send(6, 1, device_count)
    all_of(5).wait_recv()
    inverse_rows(5, use_slope_two)
    finish_rows(7)
    inverse_rows(6, use_curve_two)
    all_of(7).wait_recv()
    send(3, middle, device_count)
    forward_columns(7)
    inverse_columns(8, False)
    send_half_to_rows(8, 0, last_sems)
    all_of_half(8, 0, last_sems).wait_send()
    send_half_to_rows(8, 1, last_sems)
    inverse_rows(3, use_cubic_one)
    for half in (0, 1):
        inverse_rows_half(8, use_slope_three, half, last_sems)
        send_slab_half(lambda to, half=half: total.at[to, halves[half]], back, half, back_sems)
    out_ref[own_rows] = total[slab]
    for half in (0, 1):
        all_of_slab_half(back, half, back_sems).wait_recv()
        for i in range(1, slab_count):
            source = lax.rem(slab + i, slab_count)
            at = pl.multiple_of(source * rows + half * half_rows, half_rows)
            out_ref[pl.ds(at, half_rows)] = back[source, halves[half]]
    finish_flow()
    for n in (2, 3, 4, 6, 7):
        all_of(n).wait_send()
    all_of_slab(eta, fields + 1).wait_send()
    all_of_half(8, 1, last_sems).wait_send()
    for half in (0, 1):
        all_of_half(0, half, first_sems).wait_send()
        all_of_slab_half(potential, half, potential_sems).wait_send()
        all_of_slab_half(back, half, back_sems).wait_send()


def two_terms(table):
    high = table.astype(jnp.bfloat16)
    low = (table - high.astype(np.float32)).astype(jnp.bfloat16)
    return jnp.asarray(high), jnp.asarray(low)


def whole_step(
    potential, eta, velocity, points, counts, stencil, interp_weight, slab_count, pencil_count
):
    tile_rows, tile_cols = eta.shape
    device_count = slab_count * pencil_count
    rows, columns = NYW // device_count, NXW // device_count
    row_table, _ = tables(NXW)
    col_table, _ = tables(NYW)
    constants = [
        *two_terms(row_table),
        *two_terms(col_table),
        *two_terms(np.ascontiguousarray(col_table.transpose(0, 2, 1))),
    ]
    capacity = points.shape[1]
    block_x, block_y, _ = velocity.shape[1:]
    mixing = jnp.concatenate([stencil.astype(jnp.float32), interp_weight])
    mixing = mixing.reshape(-1, block_x * block_y)
    spectrum = (col_table.shape[0], 2 * INNER, columns)
    list_shape = (slab_count, 8, capacity)
    halo_shape = (STEPS, 4, 3, block_x, velocity.shape[3])
    fields = 9
    strip = pltpu.VMEM((slab_count, rows, tile_cols), jnp.float32)
    vmem = pl.BlockSpec(memory_space=pltpu.VMEM)
    return pl.pallas_call(
        lambda *refs: surface_kernel(slab_count, pencil_count, *refs),
        out_shape=(
            jax.ShapeDtypeStruct((tile_rows, tile_cols), jnp.float32),
            jax.ShapeDtypeStruct(velocity.shape, jnp.float32),
        ),
        in_specs=[vmem] * 6 + [pl.BlockSpec(memory_space=pl.ANY)] * 6,
        out_specs=(vmem, vmem),
        scratch_shapes=[
            *(pltpu.VMEM(table.shape, jnp.bfloat16) for table in constants),
            *([strip] * 5),
            pltpu.VMEM(row_table.shape[:1] + (rows, 2 * INNER), jnp.float32),
            pltpu.VMEM(spectrum, jnp.float32),
            pltpu.VMEM(spectrum, jnp.float32),
            pltpu.VMEM(spectrum, jnp.float32),
            pltpu.VMEM((fields, device_count, rows, columns), jnp.float32),
            pltpu.VMEM((fields, device_count, rows, columns), jnp.float32),
            pltpu.VMEM((2 * tile_rows, tile_cols), jnp.bfloat16),
            pltpu.VMEM((slab_count, tile_cols, capacity), jnp.bfloat16),
            pltpu.VMEM((slab_count, capacity, block_x * block_y), jnp.bfloat16),
            pltpu.VMEM((slab_count, capacity, block_x * block_y), jnp.bfloat16),
            pltpu.VMEM(list_shape, jnp.float32),
            pltpu.VMEM(list_shape, jnp.float32),
            pltpu.VMEM(velocity.shape, jnp.float32),
            pltpu.VMEM(halo_shape, jnp.float32),
            pltpu.VMEM(halo_shape, jnp.float32),
            pltpu.SemaphoreType.DMA((6,)),
            pltpu.SemaphoreType.DMA((fields + 8,)),
            pltpu.SemaphoreType.DMA((fields + 8,)),
            pltpu.SemaphoreType.DMA((4 * STEPS,)),
            pltpu.SemaphoreType.DMA((4 * STEPS,)),
        ],
        compiler_params=pltpu.CompilerParams(
            collective_id=0, has_side_effects=True, vmem_limit_bytes=60 * 1024 * 1024
        ),
    )(
        potential,
        eta,
        velocity,
        points,
        counts[None],
        mixing,
        *constants,
    )


def surface_plain(potential, eta, magnitude, row_table, column_table, slab_count):
    tile_rows, tile_cols = eta.shape
    columns = magnitude.shape[-1]
    device_count = NXW // columns
    rows = NYW // device_count
    row_blocks, column_blocks = jnp.asarray(row_table), jnp.asarray(column_table)
    both = jnp.stack([potential, eta]).reshape(2, slab_count, rows, tile_cols)
    both = lax.all_to_all(both, "slab", split_axis=1, concat_axis=1, tiled=True)
    both = both.transpose(0, 2, 1, 3).reshape(2, rows, NXW)
    potential, eta = both[0], both[1]
    first_mult = magnitude * (1.0 / (NXW * NYW))
    second_mult = magnitude * first_mult
    third_mult = magnitude * second_mult

    def forward(field):
        arrived = exchange(rows_forward(field, row_blocks, device_count))
        return columns_forward(arrived.reshape(NYW, columns), column_blocks)

    def inverse(spectrum):
        field = columns_inverse(spectrum, column_blocks)
        return rows_inverse(exchange(field.reshape(device_count, rows, columns)), row_blocks)

    spectrum = forward(potential)
    slope_one = inverse(spectrum * first_mult)
    curve_one = inverse(spectrum * second_mult)
    cubic_one = inverse(spectrum * third_mult)
    spectrum = forward(-eta * slope_one)
    slope_two = inverse(spectrum * first_mult)
    curve_two = inverse(spectrum * second_mult)
    spectrum = forward(-eta * slope_two - 0.5 * eta * eta * curve_one)
    slope_three = inverse(spectrum * first_mult)
    vertical = (
        slope_one
        + slope_two
        + eta * curve_one
        + slope_three
        + eta * curve_two
        + 0.5 * eta * eta * cubic_one
    )
    vertical = vertical.reshape(rows, slab_count, tile_cols).transpose(1, 0, 2)
    vertical = lax.all_to_all(vertical, "slab", split_axis=0, concat_axis=0, tiled=True)
    vertical = vertical.reshape(tile_rows, tile_cols)

    return vertical


def ramp_weight(distance, reach_len):
    ratio = jnp.clip(1.0 - distance / reach_len, 0.0, 1.0)
    return ratio * ratio


def blend_weight(pos_x, pos_y, total_x, total_y, reach_x, reach_y):
    along_x = jnp.maximum(ramp_weight(pos_x, reach_x), ramp_weight(total_x - 1.0 - pos_x, reach_x))
    across = jnp.maximum(ramp_weight(pos_y, reach_y), ramp_weight(total_y - 1.0 - pos_y, reach_y))
    return jnp.maximum(along_x[:, None], across[None, :])[:, :, None]


def neighbours(shard, axis, dim):
    size, length = lax.axis_size(axis), shard.shape[dim]
    up = [(i, i + 1) for i in range(size - 1)]
    down = [(i + 1, i) for i in range(size - 1)]
    before = lax.ppermute(lax.slice_in_dim(shard, length - 1, length, axis=dim), axis, up)
    after = lax.ppermute(lax.slice_in_dim(shard, 0, 1, axis=dim), axis, down)
    minus = jnp.concatenate([before, lax.slice_in_dim(shard, 0, length - 1, axis=dim)], axis=dim)
    plus = jnp.concatenate([lax.slice_in_dim(shard, 1, length, axis=dim), after], axis=dim)
    return minus, plus


def predict(velocity):
    minus_x, plus_x = neighbours(velocity, "slab", 1)
    minus_y, plus_y = neighbours(velocity, "pencil", 2)
    padded = jnp.pad(velocity, ((0, 0), (0, 0), (0, 0), (1, 1)))
    minus_z, plus_z = padded[..., :-2], padded[..., 2:]
    laplace = plus_x + minus_x + (plus_y + minus_y) + (plus_z + minus_z) - 6.0 * velocity
    advect = (
        velocity[0] * (plus_x - minus_x)
        + velocity[1] * (plus_y - minus_y)
        + velocity[2] * (plus_z - minus_z)
    )
    return velocity + TIME_STEP * (VISCOSITY * laplace - 0.5 * advect)


def on_device(
    surface_eta, surface_potential, velocity, send_point, send_count, stencil, interp_weight
):
    slab_count = lax.axis_size("slab")
    pencil_count = lax.axis_size("pencil")
    device_count = slab_count * pencil_count
    slab_index = lax.axis_index("slab")
    pencil_index = lax.axis_index("pencil")
    tile_rows, tile_cols = surface_eta.shape
    rows = NYW // device_count
    columns = NXW // device_count
    if (
        columns % 128 == 0
        and rows % 16 == 0
        and INNER % rows == 0
        and velocity.shape[1] == velocity.shape[2]
        and STEPS == 2
    ):
        return whole_step(
            surface_potential,
            surface_eta,
            velocity,
            send_point[0, 0],
            send_count[0, 0],
            stencil,
            interp_weight,
            slab_count,
            pencil_count,
        )
    own = pencil_index * slab_count + slab_index
    row_table, row_order = tables(NXW)
    column_table, column_order = tables(NYW)
    wave_x = 2.0 * math.pi / NXW * jnp.asarray(row_order.reshape(-1)).astype(jnp.float32)
    wave_x = lax.dynamic_slice(wave_x, (own * columns,), (columns,))
    wave_y = 2.0 * math.pi / NYW * jnp.asarray(column_order).astype(jnp.float32)[:, :, None]
    magnitude = jnp.sqrt(wave_x * wave_x + wave_y * wave_y)
    vertical = surface_plain(
        surface_potential, surface_eta, magnitude, row_table, column_table, slab_count
    )

    points = send_point[0, 0]
    capacity = points.shape[1]
    counts = send_count[0, 0]
    flat_points = points.reshape(-1)
    live = (jnp.arange(capacity, dtype=jnp.int32)[None, :] < counts[:, None]).reshape(-1)
    row_pick = (
        (flat_points // tile_cols)[:, None] == jnp.arange(tile_rows, dtype=jnp.int32)[None, :]
    ).astype(jnp.float32)
    column_pick = (flat_points % tile_cols)[:, None] == jnp.arange(tile_cols, dtype=jnp.int32)[
        None, :
    ]
    column_pick = column_pick & live[:, None]

    def pick(tile):
        picked_rows = jnp.dot(row_pick, tile, precision=HIGH)
        return jnp.sum(jnp.where(column_pick, picked_rows, 0.0), axis=1)

    picked = jnp.stack([pick(surface_eta), pick(vertical)]).reshape(2, slab_count, capacity)
    arrived = lax.all_to_all(picked, "slab", split_axis=1, concat_axis=1, tiled=True).reshape(
        2, slab_count * capacity
    )
    block_x, block_y, depth_cells = velocity.shape[1:]
    shares = interp_weight / jnp.sum(interp_weight, axis=0)
    slots = jnp.arange(slab_count * capacity, dtype=jnp.int32)[:, None]
    mixing = 0.0
    for q in range(stencil.shape[0]):
        mixing = mixing + jnp.where(
            slots == stencil[q].reshape(1, -1), shares[q].reshape(1, -1), 0.0
        )
    surface_at = jnp.dot(arrived, mixing, precision=lax.Precision.HIGHEST)
    surface_at = surface_at.reshape(2, block_x, block_y)

    zone_slabs = max(1, slab_count // 16)
    pos_x = (slab_index * block_x + jnp.arange(block_x, dtype=jnp.int32)).astype(jnp.float32)
    pos_y = (pencil_index * block_y + jnp.arange(block_y, dtype=jnp.int32)).astype(jnp.float32)
    relax_weight = blend_weight(
        pos_x,
        pos_y,
        float(block_x * slab_count),
        float(block_y * pencil_count),
        float(zone_slabs * block_x),
        float(block_y),
    )
    levels = jnp.arange(depth_cells, dtype=jnp.float32)
    depth_decay = jnp.exp(-DEPTH_RATE * (depth_cells - 1.0 - levels) / depth_cells)
    target = jnp.stack(
        [
            surface_at[0][:, :, None] * depth_decay,
            jnp.zeros((block_x, block_y, depth_cells), jnp.float32),
            surface_at[1][:, :, None] * depth_decay,
        ]
    )
    for substep in range(STEPS):
        velocity = (1.0 - relax_weight) * predict(velocity) + relax_weight * target
    return (vertical, velocity)


def solution(mesh):
    in_specs = (
        P("pencil", "slab"),
        P("pencil", "slab"),
        P(None, "slab", "pencil", None),
        P("slab", "pencil", None, None),
        P("slab", "pencil", None),
        P(None, "slab", "pencil"),
        P(None, "slab", "pencil"),
    )
    out_specs = (P("pencil", "slab"), P(None, "slab", "pencil", None))
    return jax.shard_map(
        on_device, mesh=mesh, in_specs=in_specs, out_specs=out_specs, check_vma=False
    )
```
